256 devices in a mesh: row: 8 (over x, y_lo), col: 32 (over z, y_hi, core).
Axes of the slice: x: 4, y: 4 (y_hi: 2, y_lo: 2; y = y_hi * 2 + y_lo), z: 8, core: 2. Of those that a mesh axis runs over, the one named last changes fastest.
Arguments:
- query_map: bfloat16 [128, 512, 1024], P('row', 'col'), may hold values from -12 to 12
- key_map: bfloat16 [128, 512, 1024], P('row', 'col'), may hold values from -12 to 12
- value_map: bfloat16 [128, 512, 1024], P('row', 'col'), may hold values from -6 to 6
- out_grad: bfloat16 [128, 512, 2048], P('row', 'col'), may hold values from -6 to 6
- keep_mask: int32 [128, 512, 2048], P('row', 'col'), may hold values 0 or 1
- log_scale: float32 [32], replicated, may hold values from 1 to 4.6
- bias_table: float32 [32, 31, 31], replicated, may hold values from 0 to 16
- proj_weight: bfloat16 [1024, 2048], replicated, may hold values from -0.1875 to 0.1875
Outputs:
- query_grad: bfloat16 [128, 512, 1024], P('row', 'col')
- key_grad: bfloat16 [128, 512, 1024], P('row', 'col')
- value_grad: bfloat16 [128, 512, 1024], P('row', 'col')
- weight_grad: float32 [1024, 2048], P(('row', 'col'))
- table_grad: float32 [32, 31, 31], replicated
- scale_grad: float32 [32], replicated
The draws below stay inside these ranges and needn't reach their ends.
All inputs are finite; a program needn't handle non-finite values. No bound on the sum of `keep_mask` on one device may be relied on, other than what follows from the above.
Results may differ from the reference program's by a relative error of at most 0.013.
The reference program's roundings to bfloat16 on the way count: a program that leaves them out, or rounds other values in their place, can miss the bound.
Values may be sent and summed in bfloat16 or wider, within the bound.
No kernel may reach another device: no remote copies, remote signals or barrier semaphores. Data moves between devices by JAX's collectives and lax.ppermute only.
A program may use at most 192 MiB of HBM per device.

```python
import jax
import jax.numpy as jnp
from jax import lax

D = 2048
HEADS = 32
HEAD_DIM = 32
WIN = 16
HALF = 8
INNER = 1024
NR = 128
NC = 512


def head_scales(key, lowest, highest):
    spread = jax.random.uniform(key, (NR, NC, HEADS, 1), jnp.float32, jnp.log(lowest), jnp.log(highest))
    return jnp.exp(spread)


def draw_query_map(key, part):
    key = jax.random.fold_in(key, 11)
    random_key, scale_key = jax.random.split(key, 2)
    random_part = jnp.clip(jax.random.normal(random_key, (NR, NC, HEADS, HEAD_DIM), jnp.float32), -6.0, 6.0)
    result = random_part * head_scales(scale_key, 0.05, 2.0)
    return result.reshape(NR, NC, INNER).astype(jnp.bfloat16)


def draw_key_map(key, part):
    key = jax.random.fold_in(key, 17)
    random_key, scale_key = jax.random.split(key, 2)
    random_part = jnp.clip(jax.random.normal(random_key, (NR, NC, HEADS, HEAD_DIM), jnp.float32), -6.0, 6.0)
    result = random_part * head_scales(scale_key, 0.05, 2.0)
    return result.reshape(NR, NC, INNER).astype(jnp.bfloat16)


def draw_log_scale(key, part):
    key = jax.random.fold_in(key, 29)
    drawn_key = jax.random.fold_in(key, 0)
    drawn = jax.random.uniform(drawn_key, (HEADS,), jnp.float32, 1.0, 4.6)
    return drawn


def draw_bias_table(key, part):
    key = jax.random.fold_in(key, 23)
    table_side = 2 * WIN - 1
    entries = jnp.clip(jax.random.normal(key, (HEADS, table_side, table_side), jnp.float32), -4.0, 4.0)
    return 16.0 * jax.nn.sigmoid(1.5 * entries)


def plant(values, stream_key, least, high):
    longest = values.shape.index(max(values.shape))
    spots = []
    for shift in (0, 1):
        where = [jax.random.randint(jax.random.fold_in(stream_key, axis), (), 0, length) for axis, length in enumerate(values.shape)]
        where[longest] = (where[longest] + shift) % values.shape[longest]
        spots.append(tuple(where))
    return values.at[spots[0]].set(least).at[spots[1]].set(high)


def block_scale(stream_key, extent, shards, least, top_value):
    gain = 1.0
    for dim, blocks in shards:
        heights = jax.random.uniform(jax.random.fold_in(jax.random.fold_in(stream_key, 6), dim), (blocks,), jnp.float32, least / len(shards), top_value / len(shards))
        gain = gain * jnp.repeat(jnp.exp(heights), extent[dim] // blocks).reshape((-1,) + (1,) * (len(extent) - 1 - dim))
    return gain


def centred(rng, extent, scale, most, cuts=(), held_as=jnp.bfloat16):
    values = jax.random.normal(rng, extent, jnp.float32) * scale
    if len(cuts) > 0:
        values = block_scale(rng, extent, cuts, -0.22, 0.18) * values
    return jnp.clip(values, min=-most, max=most).astype(held_as)


def setup_inputs(seed: int = 0) -> dict:
    key_of = jax.random.split(jax.random.key(seed), 9)
    query_map = draw_query_map(jax.random.fold_in(key_of[8], 71), 0)
    key_map = draw_key_map(jax.random.fold_in(key_of[8], 71), 0)
    value_map = centred(key_of[2], (NR, NC, INNER), 1.0, 6.0, ((0, 8), (1, 32)))
    out_grad = centred(key_of[3], (NR, NC, D), 1.0, 6.0, ((0, 8), (1, 32)))
    keep_mask = plant((jax.random.randint(key_of[4], (NR, NC, D), 0, 10) < 9).astype(jnp.int32), jax.random.fold_in(key_of[4], 1), 0, 1)
    log_scale = draw_log_scale(jax.random.fold_in(key_of[8], 71), 0)
    bias_table = draw_bias_table(jax.random.fold_in(key_of[8], 71), 0)
    proj_weight = centred(key_of[7], (INNER, D), INNER ** -0.5, 0.1875)
    return {"query_map": query_map, "key_map": key_map, "value_map": value_map, "out_grad": out_grad, "keep_mask": keep_mask, "log_scale": log_scale, "bias_table": bias_table, "proj_weight": proj_weight}


KEEP_RATE = 0.9

def to_windows(tensor, win_size):
    row_count, col_count, features = tensor.shape
    blocks = tensor.reshape(row_count // win_size, win_size, col_count // win_size, win_size, features)
    return blocks.transpose(0, 2, 1, 3, 4).reshape(-1, win_size * win_size, features)

def from_windows(blocks, row_count, col_count, win_size):
    features = blocks.shape[-1]
    grid = blocks.reshape(row_count // win_size, col_count // win_size, win_size, win_size, features)
    return grid.transpose(0, 2, 1, 3, 4).reshape(row_count, col_count, features)

def normalize_rows(tensor):
    length = jnp.sqrt(lax.optimization_barrier(jnp.sum(tensor * tensor, axis=-1, keepdims=True)))
    return (tensor / jnp.maximum(length, 1.0), length)

def normalize_back(unit_vec, length, grad_unit):
    projection = lax.optimization_barrier(jnp.sum(unit_vec * grad_unit, axis=-1, keepdims=True))
    return jnp.where(length > 1.0, (grad_unit - unit_vec * projection) / jnp.maximum(length, 1.0), grad_unit)

def attend(query_rows, key_rows, value_rows, logit_scale, bias_full):
    tokens = query_rows.shape[0]
    q_unit, q_len = normalize_rows(query_rows.astype(jnp.float32).reshape(tokens, HEADS, HEAD_DIM))
    k_unit, k_len = normalize_rows(key_rows.astype(jnp.float32).reshape(tokens, HEADS, HEAD_DIM))
    q_round = q_unit.astype(jnp.bfloat16)
    k_round = k_unit.astype(jnp.bfloat16)
    cosine = jnp.einsum('ihe,jhe->hij', q_round.astype(jnp.float32), k_round.astype(jnp.float32))
    scores = logit_scale[:, None, None] * cosine + bias_full
    row_peak = lax.optimization_barrier(jnp.max(scores, axis=-1, keepdims=True))
    weights = jnp.exp(scores - row_peak)
    attn_probs = weights / lax.optimization_barrier(jnp.sum(weights, axis=-1, keepdims=True))
    prob_round = attn_probs.astype(jnp.bfloat16)
    value_heads = value_rows.astype(jnp.float32).reshape(tokens, HEADS, HEAD_DIM)
    mixture = jnp.einsum('hij,jhe->ihe', prob_round.astype(jnp.float32), value_heads)
    attended = mixture.reshape(tokens, INNER).astype(jnp.bfloat16)
    return (attended, (q_unit, q_len, k_unit, k_len, q_round, k_round, cosine, attn_probs, prob_round))

def attend_back(kept_state, value_rows, grad_rows, logit_scale):
    q_unit, q_len, k_unit, k_len, q_round, k_round, cosine, attn_probs, prob_round = kept_state
    tokens = grad_rows.shape[0]
    grad_mix = grad_rows.astype(jnp.float32).reshape(tokens, HEADS, HEAD_DIM)
    value_heads = value_rows.astype(jnp.float32).reshape(tokens, HEADS, HEAD_DIM)
    grad_probs = jnp.einsum('ihe,jhe->hij', grad_mix, value_heads)
    grad_value = jnp.einsum('hij,ihe->jhe', prob_round.astype(jnp.float32), grad_mix)
    row_inner = lax.optimization_barrier(jnp.sum(attn_probs * grad_probs, axis=-1, keepdims=True))
    grad_scores = attn_probs * (grad_probs - row_inner)
    grad_log = lax.optimization_barrier(jnp.sum(grad_scores * cosine, axis=(1, 2))) * logit_scale
    grad_cos = (grad_scores * logit_scale[:, None, None]).astype(jnp.bfloat16)
    grad_qunit = jnp.einsum('hij,jhe->ihe', grad_cos.astype(jnp.float32), k_round.astype(jnp.float32))
    grad_kunit = jnp.einsum('hij,ihe->jhe', grad_cos.astype(jnp.float32), q_round.astype(jnp.float32))
    grad_query = normalize_back(q_unit, q_len, grad_qunit).reshape(tokens, INNER).astype(jnp.bfloat16)
    grad_key = normalize_back(k_unit, k_len, grad_kunit).reshape(tokens, INNER).astype(jnp.bfloat16)
    grad_val = grad_value.reshape(tokens, INNER).astype(jnp.bfloat16)
    return (grad_query, grad_key, grad_val, grad_scores, grad_log)

def reference(query_map, key_map, value_map, out_grad, keep_mask, log_scale, bias_table, proj_weight):
    row_count = query_map.shape[0]
    col_count = query_map.shape[1]

    def shifted(tensor):
        return to_windows(jnp.roll(tensor, (-HALF, -HALF), axis=(0, 1)), WIN)

    def unshift(blocks):
        return jnp.roll(from_windows(blocks, row_count, col_count, WIN), (HALF, HALF), axis=(0, 1))
    dropped = (out_grad.astype(jnp.float32) * keep_mask.astype(jnp.float32) * (1.0 / KEEP_RATE)).astype(jnp.bfloat16)
    query_win = shifted(query_map)
    key_win = shifted(key_map)
    value_win = shifted(value_map)
    dropped_win = shifted(dropped)
    window_count = query_win.shape[0]
    grad_attn = jnp.dot(dropped_win.reshape(-1, D), proj_weight.T, preferred_element_type=jnp.float32)
    grad_attn = grad_attn.astype(jnp.bfloat16).reshape(window_count, WIN * WIN, INNER)
    places = jnp.arange(WIN * WIN)
    rel_rows = (places[:, None] // WIN - places[None, :] // WIN + WIN - 1).astype(jnp.int32)
    rel_cols = (places[:, None] % WIN - places[None, :] % WIN + WIN - 1).astype(jnp.int32)
    bias_full = bias_table[:, rel_rows, rel_cols]
    logit_scale = jnp.exp(log_scale)

    def one_window(running, pieces):
        query_rows, key_rows, value_rows, grad_rows = pieces
        attended, kept_state = attend(query_rows, key_rows, value_rows, logit_scale, bias_full)
        grad_query, grad_key, grad_val, grad_scores, grad_log = attend_back(kept_state, value_rows, grad_rows, logit_scale)
        return ((running[0] + grad_scores, running[1] + grad_log), (attended, grad_query, grad_key, grad_val))
    start_state = (jnp.zeros((HEADS, WIN * WIN, WIN * WIN), jnp.float32), jnp.zeros((HEADS,), jnp.float32))
    (score_sum, log_sum), (attended, grad_query, grad_key, grad_val) = lax.scan(one_window, start_state, (query_win, key_win, value_win, grad_attn))
    weight_grad = lax.dot_general(attended.reshape(-1, INNER), dropped_win.reshape(-1, D), (((0,), (0,)), ((), ())), preferred_element_type=jnp.float32) / window_count
    table_grad = jnp.zeros(bias_table.shape, jnp.float32).at[:, rel_rows, rel_cols].add(score_sum) / window_count
    scale_grad = log_sum / window_count
    return (unshift(grad_query), unshift(grad_key), unshift(grad_val), weight_grad, table_grad, scale_grad)
```

```python
import functools

import jax
import jax.numpy as jnp
import numpy as np
from jax import lax
from jax.experimental import pallas as pl
from jax.experimental.pallas import tpu as pltpu
from jax.sharding import PartitionSpec as P

D = 2048
HEADS = 32
HEAD_DIM = 32
INNER = 1024
WINDOWS = 256
KEEP_RATE = 0.9
SIDE = 31
LOG2E = 1.4426950408889634

NX, NYL, NZ, NYH, NCORE = 4, 2, 8, 2, 2

F32 = jnp.float32
BF16 = jnp.bfloat16
TILE = 128
PER_TILE = TILE // HEAD_DIM
QUAD = 64
TOKENS = 256

VMEM_BYTES = 48 * 1024 * 1024


def params():
    return pltpu.CompilerParams(vmem_limit_bytes=VMEM_BYTES)


def cost(flops, nbytes):
    return pl.CostEstimate(flops=int(flops), bytes_accessed=int(nbytes), transcendentals=0)


def move(value, target):
    sizes = (NX, NYL, NZ, NYH, NCORE)
    pairs = []
    for src in range(NX * NYL * NZ * NYH * NCORE):
        place = np.unravel_index(src, sizes)
        goal = [int(g) % s for g, s in zip(target(*[int(p) for p in place]), sizes)]
        pairs.append((src, int(np.ravel_multi_index(goal, sizes))))
    return lax.ppermute(value, ("row", "col"), pairs)


def move_map(value, d_row, d_col):
    rows, cols = NX * NYL, NZ * NYH * NCORE
    pairs = [
        (r * cols + c, ((r + d_row) % rows) * cols + (c + d_col) % cols)
        for r in range(rows)
        for c in range(cols)
    ]
    return lax.ppermute(value, ("row", "col"), pairs)


def along_x(step):
    return lambda x, yl, z, yh, c: (x + step, yl, z, yh, c)


def along_y(step):
    def goal(x, yl, z, yh, c):
        y = (2 * yh + yl + step) % 4
        return (x, y % 2, z, y // 2, c)

    return goal


def along_z(step):
    return lambda x, yl, z, yh, c: (x, yl, z + step, yh, c)


def other_core(x, yl, z, yh, c):
    return (x, yl, z, yh, 1 - c)


def coordinates():
    row = lax.axis_index("row")
    col = lax.axis_index("col")
    x, y_lo = row // 2, row % 2
    z, y_hi, core = col // 4, (col // 2) % 2, col % 2
    return x, 2 * y_hi + y_lo, z, core


def quarters_of(block):
    n = block.shape[-1]
    cut = lambda a, b: block[a : a + 8, b : b + 8, :].reshape(QUAD, n).astype(BF16)
    return cut(0, 0), cut(0, 8), cut(8, 0), cut(8, 8)


def split_kernel(q_ref, k_ref, v_ref, tl_ref, tr_ref, bl_ref, br_ref):
    for which, ref in enumerate((q_ref, k_ref, v_ref)):
        for out, part in zip((tl_ref, tr_ref, bl_ref, br_ref), quarters_of(ref[...].astype(F32))):
            out[which] = part


def split_maps(query_map, key_map, value_map):
    spec = pl.BlockSpec((16, 16, 256), lambda t: (0, 0, t))
    out = pl.BlockSpec((3, QUAD, 256), lambda t: (0, 0, t))
    return pl.pallas_call(
        split_kernel,
        grid=(INNER // 256,),
        in_specs=[spec] * 3,
        out_specs=[out] * 4,
        out_shape=[jax.ShapeDtypeStruct((3, QUAD, INNER), BF16)] * 4,
        compiler_params=params(),
        name="split_maps",
    )(query_map, key_map, value_map)


def drop_kernel(grad_ref, keep_ref, tl_ref, tr_ref, bl_ref, br_ref):
    dropped = grad_ref[...].astype(F32) * keep_ref[...].astype(F32) * (1.0 / KEEP_RATE)
    for out, part in zip((tl_ref, tr_ref, bl_ref, br_ref), quarters_of(dropped)):
        out[...] = part


def split_dropped(out_grad, keep_mask):
    spec = pl.BlockSpec((16, 16, 512), lambda t: (0, 0, t))
    out = pl.BlockSpec((QUAD, 512), lambda t: (0, t))
    return pl.pallas_call(
        drop_kernel,
        grid=(D // 512,),
        in_specs=[spec] * 2,
        out_specs=[out] * 4,
        out_shape=[jax.ShapeDtypeStruct((QUAD, D), BF16)] * 4,
        compiler_params=params(),
        name="split_dropped",
    )(out_grad, keep_mask)


def join_kernel(tl_ref, tr_ref, bl_ref, br_ref, *outs):
    for which, out in enumerate(outs):
        part = lambda ref: ref[which].astype(F32).reshape(8, 8, ref.shape[-1])
        out[:8] = jnp.concatenate([part(tl_ref), part(tr_ref)], axis=1).astype(BF16)
        out[8:] = jnp.concatenate([part(bl_ref), part(br_ref)], axis=1).astype(BF16)


def join_maps(tl, tr, bl, br):
    spec = pl.BlockSpec((3, QUAD, 256), lambda t: (0, 0, t))
    out = pl.BlockSpec((16, 16, 256), lambda t: (0, 0, t))
    return pl.pallas_call(
        join_kernel,
        grid=(INNER // 256,),
        in_specs=[spec] * 4,
        out_specs=[out] * 3,
        out_shape=[jax.ShapeDtypeStruct((16, 16, INNER), BF16)] * 3,
        compiler_params=params(),
        name="join_maps",
    )(tl, tr, bl, br)


def bias_strips(bias_table):
    pick = np.zeros((SIDE, 3, 8, 8), np.float32)
    for d in range(3):
        for xj in range(8):
            for xi in range(8):
                pick[8 * (d - 1) + 15 + xi - xj, d, xj, xi] = 1.0
    strips = jnp.einsum(
        "hkm,mdji->hdjki", bias_table * LOG2E, jnp.asarray(pick), precision=lax.Precision.HIGHEST
    )
    strips = strips.reshape(HEADS, 3, 8, SIDE * 8)
    return jnp.pad(strips, ((0, 0), (0, 0), (0, 0), (0, 8)))


def bias_kernel(strip_ref, out_ref):
    strips = strip_ref[...].reshape(PER_TILE * 3 * 8, 256)
    for yj in range(16):
        start = 8 * (15 - yj)
        moved = strips if start == 0 else pltpu.roll(strips, 256 - start, 1)
        out_ref[:, :, 8 * yj : 8 * yj + 8, :] = moved[:, :128].reshape(PER_TILE, 3, 8, 128)


def bias_blocks(strips):
    return pl.pallas_call(
        bias_kernel,
        grid=(HEADS // PER_TILE,),
        in_specs=[pl.BlockSpec((PER_TILE, 3, 8, 256), lambda t: (t, 0, 0, 0))],
        out_specs=pl.BlockSpec((PER_TILE, 3, 128, 128), lambda t: (t, 0, 0, 0)),
        out_shape=jax.ShapeDtypeStruct((HEADS, 3, 128, 128), F32),
        compiler_params=params(),
        cost_estimate=cost(1e7, 8e6),
        name="bias_blocks",
    )(strips)


def iota(shape, dim):
    return lax.broadcasted_iota(jnp.int32, shape, dim)


def per_head_sum(value):
    high = value.astype(BF16)
    low = (value - high.astype(F32)).astype(BF16)
    shape = (2 * TILE, TILE)
    same = (iota(shape, 0) % TILE) // HEAD_DIM == iota(shape, 1) // HEAD_DIM
    ones = jnp.where(same, 1.0, 0.0).astype(BF16)
    both = jnp.concatenate([high, low], axis=1)
    return jnp.dot(both, ones, preferred_element_type=F32)


def normalize(rows):
    value = rows.astype(F32)
    length = jnp.sqrt(per_head_sum(value * value))
    inverse = 1.0 / jnp.maximum(length, 1.0)
    return value * inverse, length, inverse


def normalize_back(unit, length, inverse, grad):
    projection = per_head_sum(unit * grad)
    return jnp.where(length > 1.0, (grad - unit * projection) * inverse, grad)


def of_head(rows, head):
    keep = iota(rows.shape, 1) // HEAD_DIM == head
    return jnp.where(keep, rows, jnp.zeros_like(rows))


def rows_of(refs, which):
    return jnp.concatenate([ref[which] for ref in refs], axis=0)


def product_t(left, right):
    return lax.dot_general(left, right, (((1,), (1,)), ((), ())), preferred_element_type=F32)


def forward_kernel(scale_ref, tl_ref, bl_ref, tr_ref, br_ref, bias_ref, attn_ref, probs_ref):
    tile = pl.program_id(0)
    quads = (tl_ref, bl_ref, tr_ref, br_ref)
    q_round = normalize(rows_of(quads, 0))[0].astype(BF16)
    k_round = normalize(rows_of(quads, 1))[0].astype(BF16)
    value_t = rows_of(quads, 2).T
    mixed = []
    for head in range(PER_TILE):
        cosine = product_t(of_head(k_round, head), q_round)
        scale = scale_ref[tile * PER_TILE + head]
        halves = []
        for half in range(2):
            lanes = slice(128 * half, 128 * half + 128)
            bias = jnp.concatenate([bias_ref[head, 1 + half], bias_ref[head, half]], axis=0)
            scores = cosine[:, lanes] * scale + bias
            weights = jnp.exp2(scores - jnp.max(scores, axis=0, keepdims=True))
            probs = weights * (1.0 / jnp.sum(weights, axis=0, keepdims=True))
            probs_ref[head, :, lanes] = probs
            halves.append(probs.astype(BF16))
        rounded = jnp.concatenate(halves, axis=1)
        mixed.append(
            jnp.dot(
                value_t[HEAD_DIM * head : HEAD_DIM * head + HEAD_DIM],
                rounded,
                preferred_element_type=F32,
            )
        )
    mixture = jnp.concatenate(mixed, axis=0).astype(BF16)
    goal, source = iota((TILE, TILE), 0), iota((TILE, TILE), 1)
    wanted = (
        ((goal // 4) % NZ) * 16 + ((goal // 32) % NYH) * 8 + (goal // 64) * 4 + goal % 4
    )
    sort = jnp.where(source == wanted, 1.0, 0.0).astype(BF16)
    ordered = jnp.dot(sort, mixture, preferred_element_type=F32).astype(BF16)
    attn_ref[0, 0] = ordered[:64]
    attn_ref[1, 0] = ordered[64:]


def quad_spec():
    return pl.BlockSpec((3, QUAD, TILE), lambda t: (0, 0, t))


def forward(scales, quads, bias):
    return pl.pallas_call(
        forward_kernel,
        grid=(INNER // TILE,),
        in_specs=[pl.BlockSpec(memory_space=pltpu.SMEM)]
        + [quad_spec()] * 4
        + [pl.BlockSpec((PER_TILE, 3, 128, 128), lambda t: (t, 0, 0, 0))],
        out_specs=[
            pl.BlockSpec((2, 1, 64, TOKENS), lambda t: (0, t, 0, 0)),
            pl.BlockSpec((PER_TILE, TOKENS, TOKENS), lambda t: (t, 0, 0)),
        ],
        out_shape=[
            jax.ShapeDtypeStruct((2, 8, 64, TOKENS), BF16),
            jax.ShapeDtypeStruct((HEADS, TOKENS, TOKENS), F32),
        ],
        compiler_params=params(),
        cost_estimate=cost(8e9, 16e6),
        name="forward",
    )(scales, *quads, bias)


def diagonal_sums(blocks):
    lane = iota((8, 128), 1)
    strips = []
    for block in blocks:
        total = jnp.zeros((8, 128), F32)
        first = jnp.zeros((8, 128), F32)
        for yj in range(16):
            start = 8 * (15 - yj)
            piece = block[8 * yj : 8 * yj + 8]
            if start:
                piece = pltpu.roll(piece, start, 1)
                first = first + jnp.where(lane >= start, piece, 0.0)
            else:
                first = first + piece
            total = total + piece
        strips.append(jnp.concatenate([first, total - first], axis=1))
    return strips


def offset_sums(strips):
    shape = strips[0].shape
    xj, lane = iota(shape, 0) % 8, iota(shape, 1)
    even = ((lane + xj) // 8) % 2 == 0
    sums = []
    for strip in strips:
        for bit in range(3):
            moved = pltpu.roll(strip, 256 - (1 << bit), 1)
            strip = jnp.where((xj // (1 << bit)) % 2 == 1, moved, strip)
        part = jnp.where(even, strip, 0.0)
        total = lambda v: jnp.sum(v.reshape(PER_TILE, 8, 256), axis=1)
        sums.append((pltpu.roll(total(part), 7, 1), pltpu.roll(total(strip - part), 255, 1)))
    inner = iota((PER_TILE, 256), 1) % 16
    result = []
    for parity in range(2):
        left, middle, right = (pair[parity] for pair in sums)
        result.append(left + jnp.where(inner >= 8, pltpu.roll(middle, 8, 1), 0.0))
        result.append(right + jnp.where(inner < 8, pltpu.roll(middle, 248, 1), 0.0))
    return result


def backward_kernel(
    scale_ref,
    tl_ref,
    bl_ref,
    tr_ref,
    br_ref,
    dtl_ref,
    dbl_ref,
    dtr_ref,
    dbr_ref,
    weight_ref,
    probs_ref,
    gtl_ref,
    gbl_ref,
    gtr_ref,
    gbr_ref,
    table_ref,
    drop_ref,
):
    tile = pl.program_id(0)
    quads = (tl_ref, bl_ref, tr_ref, br_ref)

    @pl.when(tile == 0)
    def _():
        for part, ref in enumerate((dtl_ref, dbl_ref, dtr_ref, dbr_ref)):
            drop_ref[QUAD * part : QUAD * part + QUAD] = ref[...]

    grad = product_t(drop_ref[...], weight_ref[...]).astype(BF16)
    q_unit, q_len, q_inv = normalize(rows_of(quads, 0))
    k_unit, k_len, k_inv = normalize(rows_of(quads, 1))
    q_round, k_round = q_unit.astype(BF16), k_unit.astype(BF16)
    value = rows_of(quads, 2)
    key_t = k_round.T
    grad_v = jnp.zeros((TOKENS, TILE), F32)
    grad_k = jnp.zeros((TOKENS, TILE), F32)
    grad_q_t, log_sums = [], []
    strips = [[], [], []]
    for head in range(PER_TILE):
        scale = scale_ref[tile * PER_TILE + head]
        grad_probs = product_t(of_head(value, head), grad)
        cosine = product_t(of_head(k_round, head), q_round)
        log_sum = jnp.zeros((1, 128), F32)
        halves, rounded, cos_grads = [], [], []
        for half in range(2):
            lanes = slice(128 * half, 128 * half + 128)
            probs = probs_ref[head, :, lanes]
            part = grad_probs[:, lanes]
            inner = jnp.sum(probs * part, axis=0, keepdims=True)
            score_grad = probs * (part - inner)
            halves.append(score_grad)
            log_sum = log_sum + jnp.sum(score_grad * cosine[:, lanes], axis=0, keepdims=True)
            rounded.append(probs.astype(BF16))
            cos_grads.append((score_grad * scale).astype(BF16))
        blocks = (halves[0][128:], halves[0][:128] + halves[1][128:], halves[1][:128])
        for strip, found in zip(strips, diagonal_sums(blocks)):
            strip.append(found)
        prob_round = jnp.concatenate(rounded, axis=1)
        grad_cos = jnp.concatenate(cos_grads, axis=1)
        grad_v = grad_v + jnp.dot(prob_round, of_head(grad, head), preferred_element_type=F32)
        grad_k = grad_k + jnp.dot(grad_cos, of_head(q_round, head), preferred_element_type=F32)
        rows = slice(HEAD_DIM * head, HEAD_DIM * head + HEAD_DIM)
        grad_q_t.append(jnp.dot(key_t[rows], grad_cos, preferred_element_type=F32))
        log_sums.append(scale * jnp.sum(log_sum, axis=1, keepdims=True))
    grad_q = jnp.concatenate(grad_q_t, axis=0).T
    results = (
        normalize_back(q_unit, q_len, q_inv, grad_q).astype(BF16),
        normalize_back(k_unit, k_len, k_inv, grad_k).astype(BF16),
        grad_v.astype(BF16),
    )
    for part, ref in enumerate((gtl_ref, gbl_ref, gtr_ref, gbr_ref)):
        for which, result in enumerate(results):
            ref[which] = result[QUAD * part : QUAD * part + QUAD]
    found = offset_sums([jnp.concatenate(strip, axis=0) for strip in strips])
    last = iota((PER_TILE, 256), 1) == 255
    for which, rows in enumerate(found):
        if which == 2:
            rows = jnp.where(last, jnp.concatenate(log_sums, axis=0), rows)
        table_ref[0, which] = rows


def backward(scales, quads, dropped, proj_weight, probs):
    full = pl.BlockSpec((QUAD, D), lambda t: (0, 0))
    return pl.pallas_call(
        backward_kernel,
        grid=(INNER // TILE,),
        in_specs=[pl.BlockSpec(memory_space=pltpu.SMEM)]
        + [quad_spec()] * 4
        + [full] * 4
        + [
            pl.BlockSpec((TILE, D), lambda t: (t, 0)),
            pl.BlockSpec((PER_TILE, TOKENS, TOKENS), lambda t: (t, 0, 0)),
        ],
        out_specs=[quad_spec()] * 4 + [pl.BlockSpec((1, 4, PER_TILE, 256), lambda t: (t, 0, 0, 0))],
        out_shape=[jax.ShapeDtypeStruct((3, QUAD, INNER), BF16)] * 4
        + [jax.ShapeDtypeStruct((INNER // TILE, 4, PER_TILE, 256), F32)],
        scratch_shapes=[pltpu.VMEM((TOKENS, D), BF16)],
        compiler_params=params(),
        cost_estimate=cost(16e9, 20e6),
        name="backward",
    )(scales, *quads, *dropped, proj_weight, probs)


def outer_kernel(place_ref, own_ref, other_ref, *refs):
    drops, outs, (left_ref, drop_ref) = refs[:8], refs[8:12], refs[12:]
    for part in range(8):
        drop_ref[QUAD * part : QUAD * part + QUAD] = drops[part][...]
    left_ref[:, :TOKENS] = own_ref[...]
    left_ref[:, TOKENS:] = other_ref[...]
    for step, out in enumerate(outs):
        start = pl.multiple_of(((place_ref[0] + step) % NX) * 128, 128)
        left = left_ref[pl.ds(start, 128), :]
        for col in range(0, D, 512):
            part = jnp.dot(left, drop_ref[:, col : col + 512], preferred_element_type=F32)
            out[:, col : col + 512] = part.astype(out.dtype)


def outer_terms(place, own, other, dropped, dropped_other):
    whole = pl.BlockSpec(memory_space=pltpu.VMEM)
    return pl.pallas_call(
        outer_kernel,
        in_specs=[pl.BlockSpec(memory_space=pltpu.SMEM)] + [whole] * 10,
        out_specs=[whole] * 4,
        out_shape=[jax.ShapeDtypeStruct((128, D), F32 if s == 0 else BF16) for s in range(NX)],
        scratch_shapes=[pltpu.VMEM((512, 2 * TOKENS), BF16), pltpu.VMEM((2 * TOKENS, D), BF16)],
        compiler_params=params(),
        cost_estimate=cost(1.1e9, 6e6),
        name="outer_terms",
    )(place, own, other, *dropped, *dropped_other)


def sum_y_kernel(place_ref, *refs):
    terms, outs = refs[:4], refs[4:8]
    for step, out in enumerate(outs):
        y = (place_ref[1] + step) % 4
        start = pl.multiple_of(((y % 2) * 2 + y // 2) * 32, 32)
        rows = pl.ds(start, 32)
        total = terms[0][rows, :]
        for term in terms[1:]:
            total = total + term[rows, :].astype(F32)
        out[...] = total.astype(out.dtype)


def sum_for_y(place, terms):
    whole = pl.BlockSpec(memory_space=pltpu.VMEM)
    return pl.pallas_call(
        sum_y_kernel,
        in_specs=[pl.BlockSpec(memory_space=pltpu.SMEM)] + [whole] * 4,
        out_specs=[whole] * 4,
        out_shape=[jax.ShapeDtypeStruct((32, D), F32 if s == 0 else BF16) for s in range(4)],
        compiler_params=params(),
        name="sum_for_y",
    )(place, *terms)


def sum_z_kernel(place_ref, *refs):
    terms, outs, total_ref = refs[:4], refs[4:12], refs[12]
    total = terms[0][...]
    for term in terms[1:]:
        total = total + term[...].astype(F32)
    for z in range(NZ):
        total_ref[z] = total[4 * z : 4 * z + 4]
    for step, out in enumerate(outs):
        out[...] = total_ref[(place_ref[2] + step) % NZ].astype(out.dtype)


def sum_for_z(place, terms):
    whole = pl.BlockSpec(memory_space=pltpu.VMEM)
    return pl.pallas_call(
        sum_z_kernel,
        in_specs=[pl.BlockSpec(memory_space=pltpu.SMEM)] + [whole] * 4,
        out_specs=[whole] * NZ,
        out_shape=[jax.ShapeDtypeStruct((4, D), F32 if s == 0 else BF16) for s in range(NZ)],
        scratch_shapes=[pltpu.VMEM((NZ, 4, D), F32)],
        compiler_params=params(),
        name="sum_for_z",
    )(place, *terms)


def weight_total(attn_t, dropped):
    x, y, z, core = coordinates()
    place = jnp.stack([x, y, z]).astype(jnp.int32)
    dropped_other = [move(part, other_core) for part in dropped]
    own = lax.dynamic_index_in_dim(attn_t, core, 0, keepdims=False).reshape(512, TOKENS)
    sent = lax.dynamic_index_in_dim(attn_t, 1 - core, 0, keepdims=False).reshape(512, TOKENS)
    other = move(sent, other_core)
    terms = outer_terms(place, own, other, dropped, dropped_other)
    terms = [terms[0]] + [move(terms[s], along_x(s)) for s in range(1, NX)]
    terms = sum_for_y(place, terms)
    terms = [terms[0]] + [move(terms[s], along_y(s)) for s in range(1, 4)]
    terms = sum_for_z(place, terms)
    terms = [terms[0]] + [move(terms[s], along_z(s)) for s in range(1, NZ)]
    return sum(term.astype(F32) for term in terms)


def sum_over(value, steps):
    terms = [value] + [move(value, step) for step in steps]
    terms = [term.astype(F32) for term in terms]
    while len(terms) > 1:
        half = len(terms) // 2
        terms = [terms[s] + terms[s + half] for s in range(half)]
    return terms[0].astype(BF16)


def z_pair(x, yl, z, yh, c):
    return (x, yl, z ^ 1, yh, c)


def table_total(part):
    value = part.astype(BF16)
    value = sum_over(value, [other_core])
    value = sum_over(value, [along_x(s) for s in range(1, 4)])
    value = sum_over(value, [along_y(s) for s in range(1, 4)])
    value = sum_over(value, [z_pair])
    return sum_over(value, [along_z(s) for s in (2, 4, 6)]).astype(F32)


def unpack_table(total, logit_scale):
    table = total.reshape(8, 2, 2, PER_TILE, 16, 16)
    log_sum = table[:, 1, 0, :, 15, 15].reshape(HEADS)
    table = table.transpose(0, 3, 4, 1, 2, 5).reshape(HEADS, 32, 32)[:, :SIDE, :SIDE]
    return table, log_sum


def per_device(
    query_map, key_map, value_map, out_grad, keep_mask, log_scale, bias_table, proj_weight
):
    logit_scale = jnp.exp(log_scale)
    tl, tr, bl, br = split_maps(query_map, key_map, value_map)
    quads = (br, move_map(tr, -1, 0), move_map(bl, 0, -1), move_map(tl, -1, -1))
    tl, tr, bl, br = split_dropped(out_grad, keep_mask)
    dropped = (br, move_map(tr, -1, 0), move_map(bl, 0, -1), move_map(tl, -1, -1))
    bias = bias_blocks(bias_strips(bias_table))
    attn_t, probs = forward(logit_scale * LOG2E, quads, bias)
    weight_grad = weight_total(attn_t, dropped)
    g_tl, g_bl, g_tr, g_br, table_part = backward(logit_scale, quads, dropped, proj_weight, probs)
    grads = join_maps(
        move_map(g_br, 1, 1), move_map(g_bl, 1, 0), move_map(g_tr, 0, 1), g_tl
    )
    table_grad, log_grad = unpack_table(table_total(table_part), logit_scale)
    return (
        *grads,
        weight_grad / WINDOWS,
        table_grad / WINDOWS,
        log_grad / WINDOWS,
    )


def solution(mesh):
    return jax.shard_map(
        per_device,
        mesh=mesh,
        in_specs=(
            P("row", "col", None),
            P("row", "col", None),
            P("row", "col", None),
            P("row", "col", None),
            P("row", "col", None),
            P(),
            P(),
            P(),
        ),
        out_specs=(
            P("row", "col", None),
            P("row", "col", None),
            P("row", "col", None),
            P(("row", "col"), None),
            P(),
            P(),
        ),
        check_vma=False,
    )
```

```python
import functools

import jax
import jax.numpy as jnp
import numpy as np
from jax import lax
from jax.experimental import pallas as pl
from jax.experimental.pallas import tpu as pltpu
from jax.sharding import PartitionSpec as P

D = 2048
HEADS = 32
HEAD_DIM = 32
INNER = 1024
WINDOWS = 256
KEEP_RATE = 0.9
SIDE = 31
LOG2E = 1.4426950408889634

NX, NYL, NZ, NYH, NCORE = 4, 2, 8, 2, 2

F32 = jnp.float32
BF16 = jnp.bfloat16
TILE = 128
PER_TILE = TILE // HEAD_DIM
GROUP = 2
QUAD = 64
TOKENS = 256

VMEM_BYTES = 48 * 1024 * 1024


def params():
    return pltpu.CompilerParams(vmem_limit_bytes=VMEM_BYTES)


def cost(flops, nbytes):
    return pl.CostEstimate(flops=int(flops), bytes_accessed=int(nbytes), transcendentals=0)


def move(value, target):
    sizes = (NX, NYL, NZ, NYH, NCORE)
    pairs = []
    for src in range(NX * NYL * NZ * NYH * NCORE):
        place = np.unravel_index(src, sizes)
        goal = [int(g) % s for g, s in zip(target(*[int(p) for p in place]), sizes)]
        pairs.append((src, int(np.ravel_multi_index(goal, sizes))))
    return lax.ppermute(value, ("row", "col"), pairs)


def move_map(value, d_row, d_col):
    rows, cols = NX * NYL, NZ * NYH * NCORE
    pairs = [
        (r * cols + c, ((r + d_row) % rows) * cols + (c + d_col) % cols)
        for r in range(rows)
        for c in range(cols)
    ]
    return lax.ppermute(value, ("row", "col"), pairs)


def along_x(step):
    return lambda x, yl, z, yh, c: (x + step, yl, z, yh, c)


def along_y(step):
    def goal(x, yl, z, yh, c):
        y = (2 * yh + yl + step) % 4
        return (x, y % 2, z, y // 2, c)

    return goal


def along_z(step):
    return lambda x, yl, z, yh, c: (x, yl, z + step, yh, c)


def other_core(x, yl, z, yh, c):
    return (x, yl, z, yh, 1 - c)


def coordinates():
    row = lax.axis_index("row")
    col = lax.axis_index("col")
    x, y_lo = row // 2, row % 2
    z, y_hi, core = col // 4, (col // 2) % 2, col % 2
    return x, 2 * y_hi + y_lo, z, core


def quarters_of(block):
    n = block.shape[-1]
    cut = lambda a, b: block[a : a + 8, b : b + 8, :].reshape(QUAD, n).astype(BF16)
    return cut(0, 0), cut(0, 8), cut(8, 0), cut(8, 8)


def split_kernel(q_ref, k_ref, v_ref, tl_ref, tr_ref, bl_ref, br_ref):
    for which, ref in enumerate((q_ref, k_ref, v_ref)):
        for out, part in zip((tl_ref, tr_ref, bl_ref, br_ref), quarters_of(ref[...].astype(F32))):
            out[which] = part


def split_maps(query_map, key_map, value_map):
    spec = pl.BlockSpec((16, 16, 256), lambda t: (0, 0, t))
    out = pl.BlockSpec((3, QUAD, 256), lambda t: (0, 0, t))
    return pl.pallas_call(
        split_kernel,
        grid=(INNER // 256,),
        in_specs=[spec] * 3,
        out_specs=[out] * 4,
        out_shape=[jax.ShapeDtypeStruct((3, QUAD, INNER), BF16)] * 4,
        compiler_params=params(),
        name="split_maps",
    )(query_map, key_map, value_map)


def drop_kernel(grad_ref, keep_ref, tl_ref, tr_ref, bl_ref, br_ref):
    dropped = grad_ref[...].astype(F32) * keep_ref[...].astype(F32) * (1.0 / KEEP_RATE)
    for out, part in zip((tl_ref, tr_ref, bl_ref, br_ref), quarters_of(dropped)):
        out[...] = part


def split_dropped(out_grad, keep_mask):
    spec = pl.BlockSpec((16, 16, 512), lambda t: (0, 0, t))
    out = pl.BlockSpec((QUAD, 512), lambda t: (0, t))
    return pl.pallas_call(
        drop_kernel,
        grid=(D // 512,),
        in_specs=[spec] * 2,
        out_specs=[out] * 4,
        out_shape=[jax.ShapeDtypeStruct((QUAD, D), BF16)] * 4,
        compiler_params=params(),
        name="split_dropped",
    )(out_grad, keep_mask)


def join_kernel(tl_ref, tr_ref, bl_ref, br_ref, *outs):
    for which, out in enumerate(outs):
        part = lambda ref: ref[which].astype(F32).reshape(8, 8, ref.shape[-1])
        out[:8] = jnp.concatenate([part(tl_ref), part(tr_ref)], axis=1).astype(BF16)
        out[8:] = jnp.concatenate([part(bl_ref), part(br_ref)], axis=1).astype(BF16)


def join_maps(tl, tr, bl, br):
    spec = pl.BlockSpec((3, QUAD, 256), lambda t: (0, 0, t))
    out = pl.BlockSpec((16, 16, 256), lambda t: (0, 0, t))
    return pl.pallas_call(
        join_kernel,
        grid=(INNER // 256,),
        in_specs=[spec] * 4,
        out_specs=[out] * 3,
        out_shape=[jax.ShapeDtypeStruct((16, 16, INNER), BF16)] * 3,
        compiler_params=params(),
        name="join_maps",
    )(tl, tr, bl, br)


def bias_kernel(table_ref, out_ref):
    lane = iota((PER_TILE, 8, 256), 2)
    spread = jnp.where(iota((32, 256), 1) // 8 == iota((32, 256), 0), 1.0, 0.0)
    wide = jnp.dot(
        table_ref[...].reshape(PER_TILE * 32, 32),
        spread,
        precision=lax.Precision.HIGHEST,
        preferred_element_type=F32,
    ).reshape(PER_TILE, 32, 256)
    for d in range(3):
        strip = jnp.zeros((PER_TILE, 8, 256), F32)
        for xi in range(8):
            first = 23 - 8 * d - xi
            strip = jnp.where(lane % 8 == xi, wide[:, first : first + 8, :], strip)
        strip = strip.reshape(PER_TILE * 8, 256)
        for yj in range(16):
            start = 8 * (15 - yj)
            moved = strip if start == 0 else pltpu.roll(strip, 256 - start, 1)
            out_ref[:, d, 8 * yj : 8 * yj + 8, :] = moved[:, :128].reshape(PER_TILE, 8, 128)


def bias_blocks(bias_table):
    table = jnp.pad(bias_table * LOG2E, ((0, 0), (0, 1), (0, 0)))
    table = jnp.pad(jnp.flip(table.transpose(0, 2, 1), 1), ((0, 0), (0, 1), (0, 0)))
    return pl.pallas_call(
        bias_kernel,
        grid=(HEADS // PER_TILE,),
        in_specs=[pl.BlockSpec((PER_TILE, 32, 32), lambda t: (t, 0, 0))],
        out_specs=pl.BlockSpec((PER_TILE, 3, 128, 128), lambda t: (t, 0, 0, 0)),
        out_shape=jax.ShapeDtypeStruct((HEADS, 3, 128, 128), F32),
        compiler_params=params(),
        cost_estimate=cost(1e7, 8e6),
        name="bias_blocks",
    )(table)


def iota(shape, dim):
    return lax.broadcasted_iota(jnp.int32, shape, dim)


def per_head_sum(value):
    high = value.astype(BF16)
    low = (value - high.astype(F32)).astype(BF16)
    shape = (2 * TILE, TILE)
    same = (iota(shape, 0) % TILE) // HEAD_DIM == iota(shape, 1) // HEAD_DIM
    ones = jnp.where(same, 1.0, 0.0).astype(BF16)
    both = jnp.concatenate([high, low], axis=1)
    return jnp.dot(both, ones, preferred_element_type=F32)


def normalize(rows):
    value = rows.astype(F32)
    length = jnp.sqrt(per_head_sum(value * value))
    inverse = 1.0 / jnp.maximum(length, 1.0)
    return value * inverse, length, inverse


def normalize_back(unit, length, inverse, grad):
    projection = per_head_sum(unit * grad)
    return jnp.where(length > 1.0, (grad - unit * projection) * inverse, grad)


def of_head(rows, head):
    keep = iota(rows.shape, 1) // HEAD_DIM == head
    return jnp.where(keep, rows, jnp.zeros_like(rows))


def rows_of(refs, which, tile):
    lanes = slice(TILE * tile, TILE * tile + TILE)
    return jnp.concatenate([ref[which, :, lanes] for ref in refs], axis=0)


def mul(left, right):
    return jnp.dot(left, right, preferred_element_type=F32)


def head_rows(head):
    return slice(HEAD_DIM * head, HEAD_DIM * head + HEAD_DIM)


def cosines_of(k_round, q_round):
    q_t = q_round.T
    return [mul(of_head(k_round, head), q_t) for head in range(PER_TILE)]


def forward_kernel(scale_ref, tl_ref, bl_ref, tr_ref, br_ref, bias_ref, attn_ref, probs_ref):
    step = pl.program_id(0)
    quads = (tl_ref, bl_ref, tr_ref, br_ref)
    cosines, values_t = [], []
    for tile in range(GROUP):
        q_round = normalize(rows_of(quads, 0, tile))[0].astype(BF16)
        k_round = normalize(rows_of(quads, 1, tile))[0].astype(BF16)
        values_t.append(rows_of(quads, 2, tile).T)
        cosines += cosines_of(k_round, q_round)
    rounded = []
    for head in range(GROUP * PER_TILE):
        scale = scale_ref[step * GROUP * PER_TILE + head]
        halves = []
        for half in range(2):
            lanes = slice(128 * half, 128 * half + 128)
            bias = jnp.concatenate([bias_ref[head, 1 + half], bias_ref[head, half]], axis=0)
            scores = cosines[head][:, lanes] * scale + bias
            weights = jnp.exp2(scores - jnp.max(scores, axis=0, keepdims=True))
            probs = weights * (1.0 / jnp.sum(weights, axis=0, keepdims=True))
            probs_ref[head, :, lanes] = probs
            halves.append(probs.astype(BF16))
        rounded.append(jnp.concatenate(halves, axis=1))
    for head in range(GROUP * PER_TILE):
        value_t = values_t[head // PER_TILE][head_rows(head % PER_TILE)]
        attn_ref[head_rows(head), :] = mul(value_t, rounded[head]).astype(BF16)


def quad_spec():
    return pl.BlockSpec((3, QUAD, GROUP * TILE), lambda t: (0, 0, t))


def probs_spec():
    return pl.BlockSpec((GROUP * PER_TILE, TOKENS, TOKENS), lambda t: (t, 0, 0))


def forward(scales, quads, bias):
    return pl.pallas_call(
        forward_kernel,
        grid=(INNER // TILE // GROUP,),
        in_specs=[pl.BlockSpec(memory_space=pltpu.SMEM)]
        + [quad_spec()] * 4
        + [pl.BlockSpec((GROUP * PER_TILE, 3, 128, 128), lambda t: (t, 0, 0, 0))],
        out_specs=[pl.BlockSpec((GROUP * TILE, TOKENS), lambda t: (t, 0)), probs_spec()],
        out_shape=[
            jax.ShapeDtypeStruct((INNER, TOKENS), BF16),
            jax.ShapeDtypeStruct((HEADS, TOKENS, TOKENS), F32),
        ],
        compiler_params=params(),
        cost_estimate=cost(8e9, 16e6),
        name="forward",
    )(scales, *quads, bias)


def diagonal_sums(blocks):
    lane = iota((8, 128), 1)
    strips = []
    for block in blocks:
        total = jnp.zeros((8, 128), F32)
        first = jnp.zeros((8, 128), F32)
        for yj in range(16):
            start = 8 * (15 - yj)
            piece = block[8 * yj : 8 * yj + 8]
            if start:
                piece = pltpu.roll(piece, start, 1)
                first = first + jnp.where(lane >= start, piece, 0.0)
            else:
                first = first + piece
            total = total + piece
        strips.append(jnp.concatenate([first, total - first], axis=1))
    return strips


def offset_sums(strips):
    shape = strips[0].shape
    xj, lane = iota(shape, 0) % 8, iota(shape, 1)
    even = ((lane + xj) // 8) % 2 == 0
    sums = []
    for strip in strips:
        for bit in range(3):
            moved = pltpu.roll(strip, 256 - (1 << bit), 1)
            strip = jnp.where((xj // (1 << bit)) % 2 == 1, moved, strip)
        part = jnp.where(even, strip, 0.0)
        total = lambda v: jnp.sum(v.reshape(PER_TILE, 8, 256), axis=1)
        sums.append((pltpu.roll(total(part), 7, 1), pltpu.roll(total(strip - part), 255, 1)))
    inner = iota((PER_TILE, 256), 1) % 16
    result = []
    for parity in range(2):
        left, middle, right = (pair[parity] for pair in sums)
        result.append(left + jnp.where(inner >= 8, pltpu.roll(middle, 8, 1), 0.0))
        result.append(right + jnp.where(inner < 8, pltpu.roll(middle, 248, 1), 0.0))
    return result


def table_of(strips, log_sums):
    rows = offset_sums(strips)
    spot = iota((PER_TILE, 256), 1) == 240
    rows[2] = jnp.where(spot, jnp.concatenate(log_sums, axis=0), rows[2])
    shape = (32, 256)
    k, lane = iota(shape, 0), iota(shape, 1)
    mine, odd = lane // 16 == k // 2, k % 2 == 1
    total = jnp.zeros((PER_TILE * 32, TILE), F32)
    for half in range(2):
        picked = []
        for head in range(PER_TILE):
            both = jnp.where(odd, rows[2 + half][head : head + 1], rows[half][head : head + 1])
            picked.append(jnp.where(mine, both, 0.0).astype(BF16))
        source, goal = iota((256, TILE), 0), iota((256, TILE), 1)
        place = jnp.where(goal == 16 * half + source % 16, 1.0, 0.0).astype(BF16)
        total = total + mul(jnp.concatenate(picked, axis=0), place)
    table = total[:32]
    for head in range(1, PER_TILE):
        table = table + pltpu.roll(total[32 * head : 32 * head + 32], 32 * head, 1)
    return table


def backward_kernel(
    first_step,
    scale_ref,
    tl_ref,
    bl_ref,
    tr_ref,
    br_ref,
    grad_ref,
    probs_ref,
    *refs,
):
    gtl_ref, gbl_ref, gtr_ref, gbr_ref, table_ref = refs[-5:]
    step = pl.program_id(0) + first_step
    quads = (tl_ref, bl_ref, tr_ref, br_ref)
    heads = range(GROUP * PER_TILE)
    queries, keys, grads, grad_probs, cosines = [], [], [], [], []
    for tile in range(GROUP):
        queries.append(normalize(rows_of(quads, 0, tile)))
        keys.append(normalize(rows_of(quads, 1, tile)))
        grads.append(grad_ref[:, TILE * tile : TILE * tile + TILE])
        value, grad_t = rows_of(quads, 2, tile), grads[-1].T
        grad_probs += [mul(of_head(value, head), grad_t) for head in range(PER_TILE)]
        cosines += cosines_of(keys[-1][0].astype(BF16), queries[-1][0].astype(BF16))
    prob_rounds, grad_coss, blocks, log_sums = [], [], [], []
    for head in heads:
        scale = scale_ref[step * GROUP * PER_TILE + head]
        log_sum = jnp.zeros((1, 128), F32)
        halves, rounded, cos_grads = [], [], []
        for half in range(2):
            lanes = slice(128 * half, 128 * half + 128)
            probs = probs_ref[head, :, lanes]
            part = grad_probs[head][:, lanes]
            inner = jnp.sum(probs * part, axis=0, keepdims=True)
            score_grad = probs * (part - inner)
            halves.append(score_grad)
            log_sum = log_sum + jnp.sum(
                score_grad * cosines[head][:, lanes], axis=0, keepdims=True
            )
            rounded.append(probs.astype(BF16))
            cos_grads.append((score_grad * scale).astype(BF16))
        blocks.append((halves[0][128:], halves[0][:128] + halves[1][128:], halves[1][:128]))
        prob_rounds.append(jnp.concatenate(rounded, axis=1))
        grad_coss.append(jnp.concatenate(cos_grads, axis=1))
        log_sums.append(scale * jnp.sum(log_sum, axis=1, keepdims=True))
    for tile in range(GROUP):
        grad_v = jnp.zeros((TOKENS, TILE), F32)
        grad_k = jnp.zeros((TOKENS, TILE), F32)
        grad_q = []
        q_round, key_t = queries[tile][0].astype(BF16), keys[tile][0].astype(BF16).T
        for head in range(PER_TILE):
            grad_cos = grad_coss[PER_TILE * tile + head]
            grad_q.append(mul(key_t[head_rows(head)], grad_cos))
            grad_v = grad_v + mul(prob_rounds[PER_TILE * tile + head], of_head(grads[tile], head))
            grad_k = grad_k + mul(grad_cos, of_head(q_round, head))
        results = (
            normalize_back(*queries[tile], jnp.concatenate(grad_q, axis=0).T).astype(BF16),
            normalize_back(*keys[tile], grad_k).astype(BF16),
            grad_v.astype(BF16),
        )
        lanes = slice(TILE * tile, TILE * tile + TILE)
        for part, ref in enumerate((gtl_ref, gbl_ref, gtr_ref, gbr_ref)):
            for which, result in enumerate(results):
                ref[which, :, lanes] = result[QUAD * part : QUAD * part + QUAD]
    for tile in range(GROUP):
        mine = range(PER_TILE * tile, PER_TILE * tile + PER_TILE)
        found = [diagonal_sums(blocks[head]) for head in mine]
        strips = [jnp.concatenate([strip[d] for strip in found], axis=0) for d in range(3)]
        table_ref[tile] = table_of(strips, [log_sums[head] for head in mine]).astype(BF16)


def backward(scales, quads, grad_attn, probs, half, earlier=()):
    steps = INNER // TILE // GROUP // 2
    first = half * steps
    quad = pl.BlockSpec((3, QUAD, GROUP * TILE), lambda t: (0, 0, t + first))
    return pl.pallas_call(
        functools.partial(backward_kernel, first),
        grid=(steps,),
        in_specs=[pl.BlockSpec(memory_space=pltpu.SMEM)]
        + [quad] * 4
        + [
            pl.BlockSpec((TOKENS, GROUP * TILE), lambda t: (0, t + first)),
            pl.BlockSpec((GROUP * PER_TILE, TOKENS, TOKENS), lambda t: (t + first, 0, 0)),
        ]
        + [pl.BlockSpec(memory_space=pl.ANY)] * len(earlier),
        out_specs=[quad] * 4 + [pl.BlockSpec((GROUP, 32, TILE), lambda t: (t + first, 0, 0))],
        out_shape=[jax.ShapeDtypeStruct((3, QUAD, INNER), BF16)] * 4
        + [jax.ShapeDtypeStruct((INNER // TILE, 32, TILE), BF16)],
        input_output_aliases={7 + i: i for i in range(len(earlier))},
        compiler_params=params(),
        cost_estimate=cost(8e9, 10e6),
        name="backward",
    )(scales, *quads, grad_attn, probs, *earlier)


def outer_kernel(place_ref, own_ref, other_ref, drop_ref, drop_other_ref, *refs):
    outs, left_ref = refs[:NX], refs[NX]
    goal, source = iota((64, TILE), 0), iota((64, TILE), 1)
    wanted = ((goal // 4) % NZ) * 16 + (goal // 32) * 8 + place_ref[3] * 4 + goal % 4
    pick = jnp.where(source == wanted, 1.0, 0.0).astype(BF16)
    for tile in range(INNER // TILE):
        rows, goals = slice(TILE * tile, TILE * tile + TILE), slice(64 * tile, 64 * tile + 64)
        left_ref[goals, :TOKENS] = mul(pick, own_ref[rows, :]).astype(BF16)
        left_ref[goals, TOKENS:] = mul(pick, other_ref[rows, :]).astype(BF16)
    for step, out in enumerate(outs):
        start = pl.multiple_of(((place_ref[0] + step) % NX) * 128, 128)
        left = left_ref[pl.ds(start, 128), :]
        for col in range(0, D, 512):
            part = mul(left[:, :TOKENS], drop_ref[:, col : col + 512])
            part = part + mul(left[:, TOKENS:], drop_other_ref[:, col : col + 512])
            out[:, col : col + 512] = part.astype(out.dtype)


def outer_terms(place, own, other, dropped, dropped_other):
    whole = pl.BlockSpec(memory_space=pltpu.VMEM)
    return pl.pallas_call(
        outer_kernel,
        in_specs=[pl.BlockSpec(memory_space=pltpu.SMEM)] + [whole] * 4,
        out_specs=[whole] * NX,
        out_shape=[jax.ShapeDtypeStruct((128, D), F32 if s == 0 else BF16) for s in range(NX)],
        scratch_shapes=[pltpu.VMEM((512, 2 * TOKENS), BF16)],
        compiler_params=params(),
        cost_estimate=cost(1.1e9, 6e6),
        name="outer_terms",
    )(place, own, other, dropped, dropped_other)


def sum_y_kernel(place_ref, *refs):
    terms, outs = refs[:4], refs[4:8]
    for step, out in enumerate(outs):
        y = (place_ref[1] + step) % 4
        start = pl.multiple_of(((y % 2) * 2 + y // 2) * 32, 32)
        rows = pl.ds(start, 32)
        total = terms[0][rows, :]
        for term in terms[1:]:
            total = total + term[rows, :].astype(F32)
        out[...] = total.astype(out.dtype)


def sum_for_y(place, terms):
    whole = pl.BlockSpec(memory_space=pltpu.VMEM)
    return pl.pallas_call(
        sum_y_kernel,
        in_specs=[pl.BlockSpec(memory_space=pltpu.SMEM)] + [whole] * 4,
        out_specs=[whole] * 4,
        out_shape=[jax.ShapeDtypeStruct((32, D), F32 if s == 0 else BF16) for s in range(4)],
        compiler_params=params(),
        name="sum_for_y",
    )(place, *terms)


def sum_z_kernel(*refs):
    terms, out = refs[:4], refs[4]
    total = terms[0][...]
    for term in terms[1:]:
        total = total + term[...].astype(F32)
    for z in range(NZ):
        out[z] = total[4 * z : 4 * z + 4].astype(BF16)


def sum_for_z(terms):
    whole = pl.BlockSpec(memory_space=pltpu.VMEM)
    return pl.pallas_call(
        sum_z_kernel,
        in_specs=[whole] * 4,
        out_specs=whole,
        out_shape=jax.ShapeDtypeStruct((NZ, 4, D), BF16),
        compiler_params=params(),
        name="sum_for_z",
    )(*terms)


def place_scalars():
    x, y, z, core = coordinates()
    return jnp.stack([x, y, z, core]).astype(jnp.int32)


def weight_total(place, terms):
    terms = sum_for_y(place, terms)
    terms = [terms[0]] + [move(terms[s], along_y(s)) for s in range(1, 4)]
    rest = NYH * NCORE
    groups = [[rest * z + one for z in range(NZ)] for one in range(rest)]
    found = lax.all_to_all(
        sum_for_z(terms), "col", 0, 0, axis_index_groups=groups, tiled=True
    )
    return jnp.sum(found.astype(F32), axis=0)


def table_pieces(part):
    found = lax.all_to_all(part.reshape(WINDOWS, 1, TILE), ("row", "col"), 0, 0, tiled=True)
    return jnp.sum(found.astype(F32), axis=0, keepdims=True) / WINDOWS


def table_whole(piece):
    same = jnp.broadcast_to(piece, (WINDOWS, 1, TILE))
    return lax.all_to_all(same, ("row", "col"), 0, 0, tiled=True)


def unpack_kernel(total_ref, table_ref):
    for tile in range(INNER // TILE):
        for head in range(PER_TILE):
            rows = total_ref[32 * tile : 32 * tile + 32, 32 * head : 32 * head + 32]
            table_ref[PER_TILE * tile + head] = rows[:SIDE, :SIDE]


def unpack_table(total):
    whole = pl.BlockSpec(memory_space=pltpu.VMEM)
    total = total.reshape(WINDOWS, TILE)
    table = pl.pallas_call(
        unpack_kernel,
        in_specs=[whole],
        out_specs=whole,
        out_shape=jax.ShapeDtypeStruct((HEADS, SIDE, SIDE), F32),
        compiler_params=params(),
        name="unpack_table",
    )(total)
    return table, total[31::32, ::32].reshape(HEADS)


def per_device(
    query_map, key_map, value_map, out_grad, keep_mask, log_scale, bias_table, proj_weight
):
    logit_scale = jnp.exp(log_scale)
    tl, tr, bl, br = split_maps(query_map, key_map, value_map)
    quads = (br, move_map(tr, -1, 0), move_map(bl, 0, -1), move_map(tl, -1, -1))
    bias = bias_blocks(bias_table)
    tl, tr, bl, br = split_dropped(out_grad, keep_mask)
    bias, tr, bl = lax.optimization_barrier((bias, tr, bl))
    up, left = move_map(tr, -1, 0), move_map(bl, 0, -1)
    quads, tl = lax.optimization_barrier((quads, tl))
    attn_t, probs = forward(logit_scale * LOG2E, quads, bias)
    pieces = (br, up, left, move_map(tl, -1, -1))
    attn_t, pieces = lax.optimization_barrier((attn_t, pieces))
    dropped = jnp.concatenate(pieces, axis=0)
    other, dropped_other = move(attn_t, other_core), move(dropped, other_core)
    grad_attn = lax.dot_general(
        dropped, proj_weight, (((1,), (1,)), ((), ())), preferred_element_type=F32
    ).astype(BF16)
    found = backward(logit_scale, quads, grad_attn, probs, 0)
    found, other, dropped_other = lax.optimization_barrier((found, other, dropped_other))
    place = place_scalars()
    terms = outer_terms(place, attn_t, other, dropped, dropped_other)
    terms, found = lax.optimization_barrier((terms, found))
    g_tl, g_bl, g_tr, g_br, table_part = backward(
        logit_scale, quads, grad_attn, probs, 1, found
    )
    arrived = (move_map(g_br, 1, 1), move_map(g_bl, 1, 0), move_map(g_tr, 0, 1))
    near = [move(terms[s], along_x(s)) for s in (1, 3)]
    near, table_part, across = lax.optimization_barrier((near, table_part, terms[2]))
    terms = (terms[0], near[0], move(across, along_x(2)), near[1])
    piece = table_pieces(table_part)
    piece, arrived = lax.optimization_barrier((piece, arrived))
    grads = join_maps(*arrived, g_tl)
    piece, grads = lax.optimization_barrier((piece, grads))
    table_grad, log_grad = unpack_table(table_whole(piece))
    weight_grad = weight_total(place, terms)
    return (*grads, weight_grad / WINDOWS, table_grad, log_grad)


def solution(mesh):
    return jax.shard_map(
        per_device,
        mesh=mesh,
        in_specs=(
            P("row", "col", None),
            P("row", "col", None),
            P("row", "col", None),
            P("row", "col", None),
            P("row", "col", None),
            P(),
            P(),
            P(),
        ),
        out_specs=(
            P("row", "col", None),
            P("row", "col", None),
            P("row", "col", None),
            P(("row", "col"), None),
            P(),
            P(),
        ),
        check_vma=False,
    )
```

```python
import functools

import jax
import jax.numpy as jnp
import numpy as np
from jax import lax
from jax.experimental import pallas as pl
from jax.experimental.pallas import tpu as pltpu
from jax.sharding import PartitionSpec as P

D = 2048
HEADS = 32
HEAD_DIM = 32
INNER = 1024
WINDOWS = 256
KEEP_RATE = 0.9
SIDE = 31
LOG2E = 1.4426950408889634

NX, NYL, NZ, NYH, NCORE = 4, 2, 8, 2, 2

F32 = jnp.float32
BF16 = jnp.bfloat16
TILE = 128
PER_TILE = TILE // HEAD_DIM
GROUP = 2
BIAS_HEADS = 8
EARLY = 1
QUAD = 64
TOKENS = 256

VMEM_BYTES = 48 * 1024 * 1024


def params(vmem=VMEM_BYTES):
    return pltpu.CompilerParams(vmem_limit_bytes=vmem)


def cost(flops, nbytes):
    return pl.CostEstimate(flops=int(flops), bytes_accessed=int(nbytes), transcendentals=0)


def move(value, target):
    sizes = (NX, NYL, NZ, NYH, NCORE)
    pairs = []
    for src in range(NX * NYL * NZ * NYH * NCORE):
        place = np.unravel_index(src, sizes)
        goal = [int(g) % s for g, s in zip(target(*[int(p) for p in place]), sizes)]
        pairs.append((src, int(np.ravel_multi_index(goal, sizes))))
    return lax.ppermute(value, ("row", "col"), pairs)


def move_map(value, d_row, d_col):
    rows, cols = NX * NYL, NZ * NYH * NCORE
    pairs = [
        (r * cols + c, ((r + d_row) % rows) * cols + (c + d_col) % cols)
        for r in range(rows)
        for c in range(cols)
    ]
    return lax.ppermute(value, ("row", "col"), pairs)


def along_x(step):
    return lambda x, yl, z, yh, c: (x + step, yl, z, yh, c)


def along_y(step):
    def goal(x, yl, z, yh, c):
        y = (2 * yh + yl + step) % 4
        return (x, y % 2, z, y // 2, c)

    return goal


def along_z(step):
    return lambda x, yl, z, yh, c: (x, yl, z + step, yh, c)


def other_core(x, yl, z, yh, c):
    return (x, yl, z, yh, 1 - c)


def coordinates():
    row = lax.axis_index("row")
    col = lax.axis_index("col")
    x, y_lo = row // 2, row % 2
    z, y_hi, core = col // 4, (col // 2) % 2, col % 2
    return x, 2 * y_hi + y_lo, z, core


def quarters_of(block):
    n = block.shape[-1]
    cut = lambda a, b: block[a : a + 8, b : b + 8, :].reshape(QUAD, n).astype(BF16)
    return cut(0, 0), cut(0, 8), cut(8, 0), cut(8, 8)


def split_kernel(q_ref, k_ref, v_ref, tl_ref, tr_ref, bl_ref, br_ref):
    for which, ref in enumerate((q_ref, k_ref, v_ref)):
        for out, part in zip((tl_ref, tr_ref, bl_ref, br_ref), quarters_of(ref[...].astype(F32))):
            out[which] = part


def split_maps(query_map, key_map, value_map):
    spec = pl.BlockSpec((16, 16, 256), lambda t: (0, 0, t))
    out = pl.BlockSpec((3, QUAD, 256), lambda t: (0, 0, t))
    return pl.pallas_call(
        split_kernel,
        grid=(INNER // 256,),
        in_specs=[spec] * 3,
        out_specs=[out] * 4,
        out_shape=[jax.ShapeDtypeStruct((3, QUAD, INNER), BF16)] * 4,
        compiler_params=params(60 * 1024 * 1024),
        name="split_maps",
    )(query_map, key_map, value_map)


def drop_kernel(grad_ref, keep_ref, tl_ref, tr_ref, bl_ref, br_ref):
    dropped = grad_ref[...].astype(F32) * keep_ref[...].astype(F32) * (1.0 / KEEP_RATE)
    for out, part in zip((tl_ref, tr_ref, bl_ref, br_ref), quarters_of(dropped)):
        out[...] = part


def split_dropped(out_grad, keep_mask):
    spec = pl.BlockSpec((16, 16, 512), lambda t: (0, 0, t))
    out = pl.BlockSpec((QUAD, 512), lambda t: (0, t))
    return pl.pallas_call(
        drop_kernel,
        grid=(D // 512,),
        in_specs=[spec] * 2,
        out_specs=[out] * 4,
        out_shape=[jax.ShapeDtypeStruct((QUAD, D), BF16)] * 4,
        compiler_params=params(60 * 1024 * 1024),
        name="split_dropped",
    )(out_grad, keep_mask)


def join_kernel(tl_ref, tr_ref, bl_ref, br_ref, *outs):
    for which, out in enumerate(outs):
        part = lambda ref: ref[which].astype(F32).reshape(8, 8, ref.shape[-1])
        out[:8] = jnp.concatenate([part(tl_ref), part(tr_ref)], axis=1).astype(BF16)
        out[8:] = jnp.concatenate([part(bl_ref), part(br_ref)], axis=1).astype(BF16)


def join_maps(tl, tr, bl, br):
    spec = pl.BlockSpec((3, QUAD, 256), lambda t: (0, 0, t))
    out = pl.BlockSpec((16, 16, 256), lambda t: (0, 0, t))
    return pl.pallas_call(
        join_kernel,
        grid=(INNER // 256,),
        in_specs=[spec] * 4,
        out_specs=[out] * 3,
        out_shape=[jax.ShapeDtypeStruct((16, 16, INNER), BF16)] * 3,
        compiler_params=params(),
        name="join_maps",
    )(tl, tr, bl, br)


def bias_kernel(table_ref, out_ref):
    lane = iota((BIAS_HEADS, 8, 256), 2)
    turn = jnp.where(iota((SIDE, 32), 0) + iota((SIDE, 32), 1) == 30, LOG2E, 0.0)
    spread = jnp.where(iota((SIDE, 256), 1) // 8 == iota((SIDE, 256), 0), 1.0, 0.0)
    exact = dict(precision=lax.Precision.HIGHEST, preferred_element_type=F32)
    turned = [jnp.dot(table_ref[head], turn, **exact) for head in range(BIAS_HEADS)]
    wide = jnp.stack(
        [lax.dot_general(rows, spread, (((0,), (0,)), ((), ())), **exact) for rows in turned]
    )
    for d in range(3):
        strip = jnp.zeros((BIAS_HEADS, 8, 256), F32)
        for xi in range(8):
            first = 23 - 8 * d - xi
            strip = jnp.where(lane % 8 == xi, wide[:, first : first + 8, :], strip)
        strip = strip.reshape(BIAS_HEADS * 8, 256)
        for yj in range(16):
            start = 8 * (15 - yj)
            moved = strip if start == 0 else pltpu.roll(strip, 256 - start, 1)
            out_ref[:, d, 8 * yj : 8 * yj + 8, :] = moved[:, :128].reshape(BIAS_HEADS, 8, 128)


def bias_blocks(bias_table):
    return pl.pallas_call(
        bias_kernel,
        grid=(HEADS // BIAS_HEADS,),
        in_specs=[pl.BlockSpec((BIAS_HEADS, SIDE, SIDE), lambda t: (t, 0, 0))],
        out_specs=pl.BlockSpec((BIAS_HEADS, 3, 128, 128), lambda t: (t, 0, 0, 0)),
        out_shape=jax.ShapeDtypeStruct((HEADS, 3, 128, 128), F32),
        compiler_params=params(),
        cost_estimate=cost(1e7, 8e6),
        name="bias_blocks",
    )(bias_table)


def iota(shape, dim):
    return lax.broadcasted_iota(jnp.int32, shape, dim)


def per_head_sum(value):
    high = value.astype(BF16)
    low = (value - high.astype(F32)).astype(BF16)
    shape = (2 * TILE, TILE)
    same = (iota(shape, 0) % TILE) // HEAD_DIM == iota(shape, 1) // HEAD_DIM
    ones = jnp.where(same, 1.0, 0.0).astype(BF16)
    both = jnp.concatenate([high, low], axis=1)
    return jnp.dot(both, ones, preferred_element_type=F32)


def normalize(rows):
    value = rows.astype(F32)
    length = jnp.sqrt(per_head_sum(value * value))
    inverse = 1.0 / jnp.maximum(length, 1.0)
    return value * inverse, length, inverse


def normalize_back(unit, length, inverse, grad):
    projection = per_head_sum(unit * grad)
    return jnp.where(length > 1.0, (grad - unit * projection) * inverse, grad)


def of_head(rows, head):
    keep = iota(rows.shape, 1) // HEAD_DIM == head
    return jnp.where(keep, rows, jnp.zeros_like(rows))


def rows_of(refs, which, tile):
    lanes = slice(TILE * tile, TILE * tile + TILE)
    return jnp.concatenate([ref[which, :, lanes] for ref in refs], axis=0)


def mul(left, right):
    return jnp.dot(left, right, preferred_element_type=F32)


def head_rows(head):
    return slice(HEAD_DIM * head, HEAD_DIM * head + HEAD_DIM)


def cosines_of(k_round, q_round):
    q_t = q_round.T
    return [mul(of_head(k_round, head), q_t) for head in range(PER_TILE)]


def forward_kernel(scale_ref, tl_ref, bl_ref, tr_ref, br_ref, bias_ref, attn_ref, probs_ref):
    step = pl.program_id(0)
    quads = (tl_ref, bl_ref, tr_ref, br_ref)
    cosines, values_t = [], []
    for tile in range(GROUP):
        q_round = normalize(rows_of(quads, 0, tile))[0].astype(BF16)
        k_round = normalize(rows_of(quads, 1, tile))[0].astype(BF16)
        values_t.append(rows_of(quads, 2, tile).T)
        cosines += cosines_of(k_round, q_round)
    rounded = []
    for head in range(GROUP * PER_TILE):
        scale = scale_ref[step * GROUP * PER_TILE + head]
        halves = []
        for half in range(2):
            lanes = slice(128 * half, 128 * half + 128)
            bias = jnp.concatenate([bias_ref[head, 1 + half], bias_ref[head, half]], axis=0)
            scores = cosines[head][:, lanes] * scale + bias
            weights = jnp.exp2(scores - jnp.max(scores, axis=0, keepdims=True))
            probs = weights * (1.0 / jnp.sum(weights, axis=0, keepdims=True))
            probs_ref[head, :, lanes] = probs
            halves.append(probs.astype(BF16))
        rounded.append(jnp.concatenate(halves, axis=1))
    for head in range(GROUP * PER_TILE):
        value_t = values_t[head // PER_TILE][head_rows(head % PER_TILE)]
        attn_ref[head_rows(head), :] = mul(value_t, rounded[head]).astype(BF16)


def quad_spec():
    return pl.BlockSpec((3, QUAD, GROUP * TILE), lambda t: (0, 0, t))


def probs_spec():
    return pl.BlockSpec((GROUP * PER_TILE, TOKENS, TOKENS), lambda t: (t, 0, 0))


def forward(scales, quads, bias):
    return pl.pallas_call(
        forward_kernel,
        grid=(INNER // TILE // GROUP,),
        in_specs=[pl.BlockSpec(memory_space=pltpu.SMEM)]
        + [quad_spec()] * 4
        + [pl.BlockSpec((GROUP * PER_TILE, 3, 128, 128), lambda t: (t, 0, 0, 0))],
        out_specs=[pl.BlockSpec((GROUP * TILE, TOKENS), lambda t: (t, 0)), probs_spec()],
        out_shape=[
            jax.ShapeDtypeStruct((INNER, TOKENS), BF16),
            jax.ShapeDtypeStruct((HEADS, TOKENS, TOKENS), F32),
        ],
        compiler_params=params(),
        cost_estimate=cost(8e9, 16e6),
        name="forward",
    )(scales, *quads, bias)


def diagonal_sums(blocks):
    lane = iota((8, 128), 1)
    strips = []
    for block in blocks:
        total = jnp.zeros((8, 128), F32)
        first = jnp.zeros((8, 128), F32)
        for yj in range(16):
            start = 8 * (15 - yj)
            piece = block[8 * yj : 8 * yj + 8]
            if start:
                piece = pltpu.roll(piece, start, 1)
                first = first + jnp.where(lane >= start, piece, 0.0)
            else:
                first = first + piece
            total = total + piece
        strips.append(jnp.concatenate([first, total - first], axis=1))
    return strips


def offset_sums(strips):
    shape = strips[0].shape
    xj, lane = iota(shape, 0) % 8, iota(shape, 1)
    even = ((lane + xj) // 8) % 2 == 0
    sums = []
    for strip in strips:
        for bit in range(3):
            moved = pltpu.roll(strip, 256 - (1 << bit), 1)
            strip = jnp.where((xj // (1 << bit)) % 2 == 1, moved, strip)
        part = jnp.where(even, strip, 0.0)
        total = lambda v: jnp.sum(v.reshape(PER_TILE, 8, 256), axis=1)
        sums.append((pltpu.roll(total(part), 7, 1), pltpu.roll(total(strip - part), 255, 1)))
    inner = iota((PER_TILE, 256), 1) % 16
    result = []
    for parity in range(2):
        left, middle, right = (pair[parity] for pair in sums)
        result.append(left + jnp.where(inner >= 8, pltpu.roll(middle, 8, 1), 0.0))
        result.append(right + jnp.where(inner < 8, pltpu.roll(middle, 248, 1), 0.0))
    return result


def table_of(strips, log_sums):
    rows = offset_sums(strips)
    spot = iota((PER_TILE, 256), 1) == 240
    rows[2] = jnp.where(spot, jnp.concatenate(log_sums, axis=0), rows[2])
    shape = (32, 256)
    k, lane = iota(shape, 0), iota(shape, 1)
    mine, odd = lane // 16 == k // 2, k % 2 == 1
    total = jnp.zeros((PER_TILE * 32, TILE), F32)
    for half in range(2):
        picked = []
        for head in range(PER_TILE):
            both = jnp.where(odd, rows[2 + half][head : head + 1], rows[half][head : head + 1])
            picked.append(jnp.where(mine, both, 0.0).astype(BF16))
        source, goal = iota((256, TILE), 0), iota((256, TILE), 1)
        place = jnp.where(goal == 16 * half + source % 16, 1.0, 0.0).astype(BF16)
        total = total + mul(jnp.concatenate(picked, axis=0), place)
    table = total[:32]
    for head in range(1, PER_TILE):
        table = table + pltpu.roll(total[32 * head : 32 * head + 32], 32 * head, 1)
    return table


def backward_kernel(
    first_step,
    scale_ref,
    tl_ref,
    bl_ref,
    tr_ref,
    br_ref,
    grad_ref,
    probs_ref,
    *refs,
):
    gtl_ref, gbl_ref, gtr_ref, gbr_ref, table_ref = refs[-5:]
    step = pl.program_id(0) + first_step
    quads = (tl_ref, bl_ref, tr_ref, br_ref)
    heads = range(GROUP * PER_TILE)
    queries, keys, grads, grad_probs, cosines = [], [], [], [], []
    for tile in range(GROUP):
        queries.append(normalize(rows_of(quads, 0, tile)))
        keys.append(normalize(rows_of(quads, 1, tile)))
        grads.append(grad_ref[:, TILE * tile : TILE * tile + TILE])
        value, grad_t = rows_of(quads, 2, tile), grads[-1].T
        grad_probs += [mul(of_head(value, head), grad_t) for head in range(PER_TILE)]
        cosines += cosines_of(keys[-1][0].astype(BF16), queries[-1][0].astype(BF16))
    prob_rounds, grad_coss, blocks, log_sums = [], [], [], []
    for head in heads:
        scale = scale_ref[step * GROUP * PER_TILE + head]
        log_sum = jnp.zeros((1, 128), F32)
        halves, rounded, cos_grads = [], [], []
        for half in range(2):
            lanes = slice(128 * half, 128 * half + 128)
            probs = probs_ref[head, :, lanes]
            part = grad_probs[head][:, lanes]
            inner = jnp.sum(probs * part, axis=0, keepdims=True)
            score_grad = probs * (part - inner)
            halves.append(score_grad)
            log_sum = log_sum + jnp.sum(
                score_grad * cosines[head][:, lanes], axis=0, keepdims=True
            )
            rounded.append(probs.astype(BF16))
            cos_grads.append((score_grad * scale).astype(BF16))
        blocks.append((halves[0][128:], halves[0][:128] + halves[1][128:], halves[1][:128]))
        prob_rounds.append(jnp.concatenate(rounded, axis=1))
        grad_coss.append(jnp.concatenate(cos_grads, axis=1))
        log_sums.append(scale * jnp.sum(log_sum, axis=1, keepdims=True))
    for tile in range(GROUP):
        grad_v = jnp.zeros((TOKENS, TILE), F32)
        grad_k = jnp.zeros((TOKENS, TILE), F32)
        grad_q = []
        q_round, key_t = queries[tile][0].astype(BF16), keys[tile][0].astype(BF16).T
        for head in range(PER_TILE):
            grad_cos = grad_coss[PER_TILE * tile + head]
            grad_q.append(mul(key_t[head_rows(head)], grad_cos))
            grad_v = grad_v + mul(prob_rounds[PER_TILE * tile + head], of_head(grads[tile], head))
            grad_k = grad_k + mul(grad_cos, of_head(q_round, head))
        results = (
            normalize_back(*queries[tile], jnp.concatenate(grad_q, axis=0).T).astype(BF16),
            normalize_back(*keys[tile], grad_k).astype(BF16),
            grad_v.astype(BF16),
        )
        lanes = slice(TILE * tile, TILE * tile + TILE)
        for part, ref in enumerate((gtl_ref, gbl_ref, gtr_ref, gbr_ref)):
            for which, result in enumerate(results):
                ref[which, :, lanes] = result[QUAD * part : QUAD * part + QUAD]
    for tile in range(GROUP):
        mine = range(PER_TILE * tile, PER_TILE * tile + PER_TILE)
        found = [diagonal_sums(blocks[head]) for head in mine]
        strips = [jnp.concatenate([strip[d] for strip in found], axis=0) for d in range(3)]
        table_ref[tile] = table_of(strips, [log_sums[head] for head in mine]).astype(BF16)


def backward(scales, quads, grad_attn, probs, first, steps, earlier=()):
    quad = pl.BlockSpec((3, QUAD, GROUP * TILE), lambda t: (0, 0, t + first))
    return pl.pallas_call(
        functools.partial(backward_kernel, first),
        grid=(steps,),
        in_specs=[pl.BlockSpec(memory_space=pltpu.SMEM)]
        + [quad] * 4
        + [
            pl.BlockSpec((TOKENS, GROUP * TILE), lambda t: (0, t + first)),
            pl.BlockSpec((GROUP * PER_TILE, TOKENS, TOKENS), lambda t: (t + first, 0, 0)),
        ]
        + [pl.BlockSpec(memory_space=pl.ANY)] * len(earlier),
        out_specs=[quad] * 4 + [pl.BlockSpec((GROUP, 32, TILE), lambda t: (t + first, 0, 0))],
        out_shape=[jax.ShapeDtypeStruct((3, QUAD, INNER), BF16)] * 4
        + [jax.ShapeDtypeStruct((INNER // TILE, 32, TILE), BF16)],
        input_output_aliases={7 + i: i for i in range(len(earlier))},
        compiler_params=params(),
        cost_estimate=cost(8e9, 10e6),
        name="backward",
    )(scales, *quads, grad_attn, probs, *earlier)


def outer_kernel(place_ref, own_ref, other_ref, drop_ref, drop_other_ref, *refs):
    outs, left_ref = refs[:NX], refs[NX]
    goal, source = iota((64, TILE), 0), iota((64, TILE), 1)
    wanted = ((goal // 4) % NZ) * 16 + (goal // 32) * 8 + place_ref[3] * 4 + goal % 4
    pick = jnp.where(source == wanted, 1.0, 0.0).astype(BF16)
    for tile in range(INNER // TILE):
        rows, goals = slice(TILE * tile, TILE * tile + TILE), slice(64 * tile, 64 * tile + 64)
        left_ref[goals, :TOKENS] = mul(pick, own_ref[rows, :]).astype(BF16)
        left_ref[goals, TOKENS:] = mul(pick, other_ref[rows, :]).astype(BF16)
    for step, out in enumerate(outs):
        start = pl.multiple_of(((place_ref[0] + step) % NX) * 128, 128)
        left = left_ref[pl.ds(start, 128), :]
        for col in range(0, D, 512):
            part = mul(left[:, :TOKENS], drop_ref[:, col : col + 512])
            part = part + mul(left[:, TOKENS:], drop_other_ref[:, col : col + 512])
            out[:, col : col + 512] = part.astype(out.dtype)


def outer_terms(place, own, other, dropped, dropped_other):
    whole = pl.BlockSpec(memory_space=pltpu.VMEM)
    return pl.pallas_call(
        outer_kernel,
        in_specs=[pl.BlockSpec(memory_space=pltpu.SMEM)] + [whole] * 4,
        out_specs=[whole] * NX,
        out_shape=[jax.ShapeDtypeStruct((128, D), F32 if s == 0 else BF16) for s in range(NX)],
        scratch_shapes=[pltpu.VMEM((512, 2 * TOKENS), BF16)],
        compiler_params=params(),
        cost_estimate=cost(1.1e9, 6e6),
        name="outer_terms",
    )(place, own, other, dropped, dropped_other)


def sum_y_kernel(place_ref, *refs):
    terms, outs = refs[:4], refs[4:8]
    for step, out in enumerate(outs):
        y = (place_ref[1] + step) % 4
        start = pl.multiple_of(((y % 2) * 2 + y // 2) * 32, 32)
        rows = pl.ds(start, 32)
        total = terms[0][rows, :]
        for term in terms[1:]:
            total = total + term[rows, :].astype(F32)
        out[...] = total.astype(out.dtype)


def sum_for_y(place, terms):
    whole = pl.BlockSpec(memory_space=pltpu.VMEM)
    return pl.pallas_call(
        sum_y_kernel,
        in_specs=[pl.BlockSpec(memory_space=pltpu.SMEM)] + [whole] * 4,
        out_specs=[whole] * 4,
        out_shape=[jax.ShapeDtypeStruct((32, D), F32 if s == 0 else BF16) for s in range(4)],
        compiler_params=params(),
        name="sum_for_y",
    )(place, *terms)


def sum_z_kernel(*refs):
    terms, out = refs[:4], refs[4]
    total = terms[0][...]
    for term in terms[1:]:
        total = total + term[...].astype(F32)
    for z in range(NZ):
        out[z] = total[4 * z : 4 * z + 4].astype(BF16)


def sum_for_z(terms):
    whole = pl.BlockSpec(memory_space=pltpu.VMEM)
    return pl.pallas_call(
        sum_z_kernel,
        in_specs=[whole] * 4,
        out_specs=whole,
        out_shape=jax.ShapeDtypeStruct((NZ, 4, D), BF16),
        compiler_params=params(),
        name="sum_for_z",
    )(*terms)


def place_scalars():
    x, y, z, core = coordinates()
    return jnp.stack([x, y, z, core]).astype(jnp.int32)


def weight_total(terms):
    terms = [terms[0]] + [move(terms[s], along_y(s)) for s in range(1, 4)]
    rest = NYH * NCORE
    groups = [[rest * z + one for z in range(NZ)] for one in range(rest)]
    found = lax.all_to_all(
        sum_for_z(terms), "col", 0, 0, axis_index_groups=groups, tiled=True
    )
    return jnp.sum(found.astype(F32), axis=0)


def row_exchange(value):
    return lax.all_to_all(value, "row", 0, 0, tiled=True)


def table_pieces(part):
    return jnp.sum(row_exchange(part).astype(F32), axis=0)


def table_column(piece):
    cols = NZ * NYH * NCORE
    same = jnp.broadcast_to(piece.astype(BF16), (cols, 32, TILE))
    found = lax.all_to_all(same, "col", 0, 0, tiled=True)
    return jnp.sum(found.astype(F32), axis=0) / WINDOWS


def table_whole(piece):
    return row_exchange(jnp.broadcast_to(piece, (NX * NYL, 32, TILE)))


def unpack_kernel(total_ref, table_ref):
    for tile in range(INNER // TILE):
        for head in range(PER_TILE):
            rows = total_ref[32 * tile : 32 * tile + 32, 32 * head : 32 * head + 32]
            table_ref[PER_TILE * tile + head] = rows[:SIDE, :SIDE]


def unpack_table(total):
    whole = pl.BlockSpec(memory_space=pltpu.VMEM)
    total = total.reshape(WINDOWS, TILE)
    table = pl.pallas_call(
        unpack_kernel,
        in_specs=[whole],
        out_specs=whole,
        out_shape=jax.ShapeDtypeStruct((HEADS, SIDE, SIDE), F32),
        compiler_params=params(),
        name="unpack_table",
    )(total)
    return table, total[31::32, ::32].reshape(HEADS)


def per_device(
    query_map, key_map, value_map, out_grad, keep_mask, log_scale, bias_table, proj_weight
):
    logit_scale = jnp.exp(log_scale)
    tl, tr, bl, br = split_maps(query_map, key_map, value_map)
    quads = (br, move_map(tr, -1, 0), move_map(bl, 0, -1), move_map(tl, -1, -1))
    bias = bias_blocks(bias_table)
    tl, tr, bl, br = split_dropped(out_grad, keep_mask)
    bias, tr, bl = lax.optimization_barrier((bias, tr, bl))
    up, left = move_map(tr, -1, 0), move_map(bl, 0, -1)
    quads, tl = lax.optimization_barrier((quads, tl))
    attn_t, probs = forward(logit_scale * LOG2E, quads, bias)
    pieces = (br, up, left, move_map(tl, -1, -1))
    attn_t, pieces = lax.optimization_barrier((attn_t, pieces))
    dropped = jnp.concatenate(pieces, axis=0)
    other, dropped_other = move(attn_t, other_core), move(dropped, other_core)
    grad_attn = lax.dot_general(
        dropped, proj_weight, (((1,), (1,)), ((), ())), preferred_element_type=F32
    ).astype(BF16)
    found = backward(logit_scale, quads, grad_attn, probs, 0, EARLY)
    found, other, dropped_other = lax.optimization_barrier((found, other, dropped_other))
    place = place_scalars()
    terms = outer_terms(place, attn_t, other, dropped, dropped_other)
    terms, found = lax.optimization_barrier((terms, found))
    g_tl, g_bl, g_tr, g_br, table_part = backward(
        logit_scale, quads, grad_attn, probs, EARLY, INNER // TILE // GROUP - EARLY, found
    )
    arrived = (move_map(g_br, 1, 1), move_map(g_bl, 1, 0), move_map(g_tr, 0, 1))
    near = [move(terms[s], along_x(s)) for s in (1, 3)]
    across = move(terms[2], along_x(2))
    near, table_part = lax.optimization_barrier((near, table_part))
    piece = table_pieces(table_part)
    terms = sum_for_y(place, (terms[0], near[0], across, near[1]))
    terms, piece = lax.optimization_barrier((terms, piece))
    piece = table_column(piece)
    arrived, piece = lax.optimization_barrier((arrived, piece))
    grads = join_maps(*arrived, g_tl)
    table_grad, log_grad = unpack_table(table_whole(piece))
    weight_grad = weight_total(terms)
    return (*grads, weight_grad / WINDOWS, table_grad, log_grad)


def solution(mesh):
    return jax.shard_map(
        per_device,
        mesh=mesh,
        in_specs=(
            P("row", "col", None),
            P("row", "col", None),
            P("row", "col", None),
            P("row", "col", None),
            P("row", "col", None),
            P(),
            P(),
            P(),
        ),
        out_specs=(
            P("row", "col", None),
            P("row", "col", None),
            P("row", "col", None),
            P(("row", "col"), None),
            P(),
            P(),
        ),
        check_vma=False,
    )
```

```python
import functools

import jax
import jax.numpy as jnp
import numpy as np
from jax import lax
from jax.experimental import pallas as pl
from jax.experimental.pallas import tpu as pltpu
from jax.sharding import PartitionSpec as P

D = 2048
HEADS = 32
HEAD_DIM = 32
INNER = 1024
WINDOWS = 256
KEEP_RATE = 0.9
SIDE = 31
LOG2E = 1.4426950408889634

NX, NYL, NZ, NYH, NCORE = 4, 2, 8, 2, 2

F32 = jnp.float32
BF16 = jnp.bfloat16
TILE = 128
PER_TILE = TILE // HEAD_DIM
GROUP = 2
BIAS_HEADS = 8
EARLY = 1
QUAD = 64
TOKENS = 256

VMEM_BYTES = 48 * 1024 * 1024


def params(vmem=VMEM_BYTES):
    return pltpu.CompilerParams(vmem_limit_bytes=vmem)


def cost(flops, nbytes):
    return pl.CostEstimate(flops=int(flops), bytes_accessed=int(nbytes), transcendentals=0)


def move(value, target):
    sizes = (NX, NYL, NZ, NYH, NCORE)
    pairs = []
    for src in range(NX * NYL * NZ * NYH * NCORE):
        place = np.unravel_index(src, sizes)
        goal = [int(g) % s for g, s in zip(target(*[int(p) for p in place]), sizes)]
        pairs.append((src, int(np.ravel_multi_index(goal, sizes))))
    return lax.ppermute(value, ("row", "col"), pairs)


def move_map(value, d_row, d_col):
    rows, cols = NX * NYL, NZ * NYH * NCORE
    pairs = [
        (r * cols + c, ((r + d_row) % rows) * cols + (c + d_col) % cols)
        for r in range(rows)
        for c in range(cols)
    ]
    return lax.ppermute(value, ("row", "col"), pairs)


def along_x(step):
    return lambda x, yl, z, yh, c: (x + step, yl, z, yh, c)


def along_y(step):
    def goal(x, yl, z, yh, c):
        y = (2 * yh + yl + step) % 4
        return (x, y % 2, z, y // 2, c)

    return goal


def along_z(step):
    return lambda x, yl, z, yh, c: (x, yl, z + step, yh, c)


def other_core(x, yl, z, yh, c):
    return (x, yl, z, yh, 1 - c)


def coordinates():
    row = lax.axis_index("row")
    col = lax.axis_index("col")
    x, y_lo = row // 2, row % 2
    z, y_hi, core = col // 4, (col // 2) % 2, col % 2
    return x, 2 * y_hi + y_lo, z, core


def quarters_of(block):
    n = block.shape[-1]
    cut = lambda a, b: block[a : a + 8, b : b + 8, :].reshape(QUAD, n).astype(BF16)
    return cut(0, 0), cut(0, 8), cut(8, 0), cut(8, 8)


def split_kernel(q_ref, k_ref, v_ref, tl_ref, tr_ref, bl_ref, br_ref):
    for which, ref in enumerate((q_ref, k_ref, v_ref)):
        for out, part in zip((tl_ref, tr_ref, bl_ref, br_ref), quarters_of(ref[...].astype(F32))):
            out[which] = part


def split_maps(query_map, key_map, value_map):
    spec = pl.BlockSpec((16, 16, 256), lambda t: (0, 0, t))
    out = pl.BlockSpec((3, QUAD, 256), lambda t: (0, 0, t))
    return pl.pallas_call(
        split_kernel,
        grid=(INNER // 256,),
        in_specs=[spec] * 3,
        out_specs=[out] * 4,
        out_shape=[jax.ShapeDtypeStruct((3, QUAD, INNER), BF16)] * 4,
        compiler_params=params(60 * 1024 * 1024),
        name="split_maps",
    )(query_map, key_map, value_map)


def drop_kernel(grad_ref, keep_ref, tl_ref, tr_ref, bl_ref, br_ref):
    dropped = grad_ref[...].astype(F32) * keep_ref[...].astype(F32) * (1.0 / KEEP_RATE)
    for out, part in zip((tl_ref, tr_ref, bl_ref, br_ref), quarters_of(dropped)):
        out[...] = part


def split_dropped(out_grad, keep_mask):
    spec = pl.BlockSpec((16, 16, 512), lambda t: (0, 0, t))
    out = pl.BlockSpec((QUAD, 512), lambda t: (0, t))
    return pl.pallas_call(
        drop_kernel,
        grid=(D // 512,),
        in_specs=[spec] * 2,
        out_specs=[out] * 4,
        out_shape=[jax.ShapeDtypeStruct((QUAD, D), BF16)] * 4,
        compiler_params=params(60 * 1024 * 1024),
        name="split_dropped",
    )(out_grad, keep_mask)


def join_kernel(tl_ref, tr_ref, bl_ref, br_ref, *outs):
    for which, out in enumerate(outs):
        part = lambda ref: ref[which].astype(F32).reshape(8, 8, ref.shape[-1])
        out[:8] = jnp.concatenate([part(tl_ref), part(tr_ref)], axis=1).astype(BF16)
        out[8:] = jnp.concatenate([part(bl_ref), part(br_ref)], axis=1).astype(BF16)


def join_maps(tl, tr, bl, br):
    spec = pl.BlockSpec((3, QUAD, 256), lambda t: (0, 0, t))
    out = pl.BlockSpec((16, 16, 256), lambda t: (0, 0, t))
    return pl.pallas_call(
        join_kernel,
        grid=(INNER // 256,),
        in_specs=[spec] * 4,
        out_specs=[out] * 3,
        out_shape=[jax.ShapeDtypeStruct((16, 16, INNER), BF16)] * 3,
        compiler_params=params(),
        name="join_maps",
    )(tl, tr, bl, br)


def bias_kernel(table_ref, out_ref):
    lane = iota((BIAS_HEADS, 8, 256), 2)
    turn = jnp.where(iota((SIDE, 32), 0) + iota((SIDE, 32), 1) == 30, LOG2E, 0.0)
    spread = jnp.where(iota((SIDE, 256), 1) // 8 == iota((SIDE, 256), 0), 1.0, 0.0)
    exact = dict(precision=lax.Precision.HIGHEST, preferred_element_type=F32)
    turned = [jnp.dot(table_ref[head], turn, **exact) for head in range(BIAS_HEADS)]
    wide = jnp.stack(
        [lax.dot_general(rows, spread, (((0,), (0,)), ((), ())), **exact) for rows in turned]
    )
    for d in range(3):
        strip = jnp.zeros((BIAS_HEADS, 8, 256), F32)
        for xi in range(8):
            first = 23 - 8 * d - xi
            strip = jnp.where(lane % 8 == xi, wide[:, first : first + 8, :], strip)
        strip = strip.reshape(BIAS_HEADS * 8, 256)
        for yj in range(16):
            start = 8 * (15 - yj)
            moved = strip if start == 0 else pltpu.roll(strip, 256 - start, 1)
            out_ref[:, d, 8 * yj : 8 * yj + 8, :] = moved[:, :128].reshape(BIAS_HEADS, 8, 128)


def bias_blocks(bias_table):
    return pl.pallas_call(
        bias_kernel,
        grid=(HEADS // BIAS_HEADS,),
        in_specs=[pl.BlockSpec((BIAS_HEADS, SIDE, SIDE), lambda t: (t, 0, 0))],
        out_specs=pl.BlockSpec((BIAS_HEADS, 3, 128, 128), lambda t: (t, 0, 0, 0)),
        out_shape=jax.ShapeDtypeStruct((HEADS, 3, 128, 128), F32),
        compiler_params=params(),
        cost_estimate=cost(1e7, 8e6),
        name="bias_blocks",
    )(bias_table)


def iota(shape, dim):
    return lax.broadcasted_iota(jnp.int32, shape, dim)


def per_head_sum(value):
    high = value.astype(BF16)
    low = (value - high.astype(F32)).astype(BF16)
    shape = (2 * TILE, TILE)
    same = (iota(shape, 0) % TILE) // HEAD_DIM == iota(shape, 1) // HEAD_DIM
    ones = jnp.where(same, 1.0, 0.0).astype(BF16)
    both = jnp.concatenate([high, low], axis=1)
    return jnp.dot(both, ones, preferred_element_type=F32)


def normalize(rows):
    value = rows.astype(F32)
    length = jnp.sqrt(per_head_sum(value * value))
    inverse = 1.0 / jnp.maximum(length, 1.0)
    return value * inverse, length, inverse


def normalize_back(unit, length, inverse, grad):
    projection = per_head_sum(unit * grad)
    return jnp.where(length > 1.0, (grad - unit * projection) * inverse, grad)


def of_head(rows, head):
    keep = iota(rows.shape, 1) // HEAD_DIM == head
    return jnp.where(keep, rows, jnp.zeros_like(rows))


def rows_of(refs, which, tile):
    lanes = slice(TILE * tile, TILE * tile + TILE)
    return jnp.concatenate([ref[which, :, lanes] for ref in refs], axis=0)


def mul(left, right):
    return jnp.dot(left, right, preferred_element_type=F32)


def head_rows(head):
    return slice(HEAD_DIM * head, HEAD_DIM * head + HEAD_DIM)


def cosines_of(k_round, q_round):
    q_t = q_round.T
    return [mul(of_head(k_round, head), q_t) for head in range(PER_TILE)]


def forward_kernel(scale_ref, tl_ref, bl_ref, tr_ref, br_ref, bias_ref, attn_ref, probs_ref):
    step = pl.program_id(0)
    quads = (tl_ref, bl_ref, tr_ref, br_ref)
    cosines, values_t = [], []
    for tile in range(GROUP):
        q_round = normalize(rows_of(quads, 0, tile))[0].astype(BF16)
        k_round = normalize(rows_of(quads, 1, tile))[0].astype(BF16)
        values_t.append(rows_of(quads, 2, tile).T)
        cosines += cosines_of(k_round, q_round)
    rounded = []
    for head in range(GROUP * PER_TILE):
        scale = scale_ref[step * GROUP * PER_TILE + head]
        halves = []
        for half in range(2):
            lanes = slice(128 * half, 128 * half + 128)
            bias = jnp.concatenate([bias_ref[head, 1 + half], bias_ref[head, half]], axis=0)
            scores = cosines[head][:, lanes] * scale + bias
            weights = jnp.exp2(scores - jnp.max(scores, axis=0, keepdims=True))
            probs = weights * (1.0 / jnp.sum(weights, axis=0, keepdims=True))
            probs_ref[head, :, lanes] = probs
            halves.append(probs.astype(BF16))
        rounded.append(jnp.concatenate(halves, axis=1))
    for head in range(GROUP * PER_TILE):
        value_t = values_t[head // PER_TILE][head_rows(head % PER_TILE)]
        attn_ref[head_rows(head), :] = mul(value_t, rounded[head]).astype(BF16)


def quad_spec():
    return pl.BlockSpec((3, QUAD, GROUP * TILE), lambda t: (0, 0, t))


def probs_spec():
    return pl.BlockSpec((GROUP * PER_TILE, TOKENS, TOKENS), lambda t: (t, 0, 0))


def forward(scales, quads, bias):
    return pl.pallas_call(
        forward_kernel,
        grid=(INNER // TILE // GROUP,),
        in_specs=[pl.BlockSpec(memory_space=pltpu.SMEM)]
        + [quad_spec()] * 4
        + [pl.BlockSpec((GROUP * PER_TILE, 3, 128, 128), lambda t: (t, 0, 0, 0))],
        out_specs=[pl.BlockSpec((GROUP * TILE, TOKENS), lambda t: (t, 0)), probs_spec()],
        out_shape=[
            jax.ShapeDtypeStruct((INNER, TOKENS), BF16),
            jax.ShapeDtypeStruct((HEADS, TOKENS, TOKENS), F32),
        ],
        compiler_params=params(),
        cost_estimate=cost(8e9, 16e6),
        name="forward",
    )(scales, *quads, bias)


def diagonal_sums(blocks):
    lane = iota((8, 128), 1)
    strips = []
    for block in blocks:
        total = jnp.zeros((8, 128), F32)
        first = jnp.zeros((8, 128), F32)
        for yj in range(16):
            start = 8 * (15 - yj)
            piece = block[8 * yj : 8 * yj + 8]
            if start:
                piece = pltpu.roll(piece, start, 1)
                first = first + jnp.where(lane >= start, piece, 0.0)
            else:
                first = first + piece
            total = total + piece
        strips.append(jnp.concatenate([first, total - first], axis=1))
    return strips


def offset_sums(strips):
    shape = strips[0].shape
    xj, lane = iota(shape, 0) % 8, iota(shape, 1)
    even = ((lane + xj) // 8) % 2 == 0
    sums = []
    for strip in strips:
        for bit in range(3):
            moved = pltpu.roll(strip, 256 - (1 << bit), 1)
            strip = jnp.where((xj // (1 << bit)) % 2 == 1, moved, strip)
        part = jnp.where(even, strip, 0.0)
        total = lambda v: jnp.sum(v.reshape(PER_TILE, 8, 256), axis=1)
        sums.append((pltpu.roll(total(part), 7, 1), pltpu.roll(total(strip - part), 255, 1)))
    inner = iota((PER_TILE, 256), 1) % 16
    result = []
    for parity in range(2):
        left, middle, right = (pair[parity] for pair in sums)
        result.append(left + jnp.where(inner >= 8, pltpu.roll(middle, 8, 1), 0.0))
        result.append(right + jnp.where(inner < 8, pltpu.roll(middle, 248, 1), 0.0))
    return result


def table_of(strips, log_sums):
    rows = offset_sums(strips)
    spot = iota((PER_TILE, 256), 1) == 240
    rows[2] = jnp.where(spot, jnp.concatenate(log_sums, axis=0), rows[2])
    shape = (32, 256)
    k, lane = iota(shape, 0), iota(shape, 1)
    mine, odd = lane // 16 == k // 2, k % 2 == 1
    total = jnp.zeros((PER_TILE * 32, TILE), F32)
    for half in range(2):
        picked = []
        for head in range(PER_TILE):
            both = jnp.where(odd, rows[2 + half][head : head + 1], rows[half][head : head + 1])
            picked.append(jnp.where(mine, both, 0.0).astype(BF16))
        source, goal = iota((256, TILE), 0), iota((256, TILE), 1)
        place = jnp.where(goal == 16 * half + source % 16, 1.0, 0.0).astype(BF16)
        total = total + mul(jnp.concatenate(picked, axis=0), place)
    table = total[:32]
    for head in range(1, PER_TILE):
        table = table + pltpu.roll(total[32 * head : 32 * head + 32], 32 * head, 1)
    return table


def backward_kernel(
    first_step,
    scale_ref,
    tl_ref,
    bl_ref,
    tr_ref,
    br_ref,
    grad_ref,
    probs_ref,
    *refs,
):
    gtl_ref, gbl_ref, gtr_ref, gbr_ref, table_ref = refs[-5:]
    step = pl.program_id(0) + first_step
    quads = (tl_ref, bl_ref, tr_ref, br_ref)
    heads = range(GROUP * PER_TILE)
    queries, keys, grads, grad_probs, cosines = [], [], [], [], []
    for tile in range(GROUP):
        queries.append(normalize(rows_of(quads, 0, tile)))
        keys.append(normalize(rows_of(quads, 1, tile)))
        grads.append(grad_ref[:, TILE * tile : TILE * tile + TILE])
        value, grad_t = rows_of(quads, 2, tile), grads[-1].T
        grad_probs += [mul(of_head(value, head), grad_t) for head in range(PER_TILE)]
        cosines += cosines_of(keys[-1][0].astype(BF16), queries[-1][0].astype(BF16))
    prob_rounds, grad_coss, blocks, log_sums = [], [], [], []
    for head in heads:
        scale = scale_ref[step * GROUP * PER_TILE + head]
        log_sum = jnp.zeros((1, 128), F32)
        halves, rounded, cos_grads = [], [], []
        for half in range(2):
            lanes = slice(128 * half, 128 * half + 128)
            probs = probs_ref[head, :, lanes]
            part = grad_probs[head][:, lanes]
            inner = jnp.sum(probs * part, axis=0, keepdims=True)
            score_grad = probs * (part - inner)
            halves.append(score_grad)
            log_sum = log_sum + jnp.sum(
                score_grad * cosines[head][:, lanes], axis=0, keepdims=True
            )
            rounded.append(probs.astype(BF16))
            cos_grads.append((score_grad * scale).astype(BF16))
        blocks.append((halves[0][128:], halves[0][:128] + halves[1][128:], halves[1][:128]))
        prob_rounds.append(jnp.concatenate(rounded, axis=1))
        grad_coss.append(jnp.concatenate(cos_grads, axis=1))
        log_sums.append(scale * jnp.sum(log_sum, axis=1, keepdims=True))
    for tile in range(GROUP):
        grad_v = jnp.zeros((TOKENS, TILE), F32)
        grad_k = jnp.zeros((TOKENS, TILE), F32)
        grad_q = []
        q_round, key_t = queries[tile][0].astype(BF16), keys[tile][0].astype(BF16).T
        for head in range(PER_TILE):
            grad_cos = grad_coss[PER_TILE * tile + head]
            grad_q.append(mul(key_t[head_rows(head)], grad_cos))
            grad_v = grad_v + mul(prob_rounds[PER_TILE * tile + head], of_head(grads[tile], head))
            grad_k = grad_k + mul(grad_cos, of_head(q_round, head))
        results = (
            normalize_back(*queries[tile], jnp.concatenate(grad_q, axis=0).T).astype(BF16),
            normalize_back(*keys[tile], grad_k).astype(BF16),
            grad_v.astype(BF16),
        )
        lanes = slice(TILE * tile, TILE * tile + TILE)
        for part, ref in enumerate((gtl_ref, gbl_ref, gtr_ref, gbr_ref)):
            for which, result in enumerate(results):
                ref[which, :, lanes] = result[QUAD * part : QUAD * part + QUAD]
    for tile in range(GROUP):
        mine = range(PER_TILE * tile, PER_TILE * tile + PER_TILE)
        found = [diagonal_sums(blocks[head]) for head in mine]
        strips = [jnp.concatenate([strip[d] for strip in found], axis=0) for d in range(3)]
        table_ref[tile] = table_of(strips, [log_sums[head] for head in mine]).astype(BF16)


def backward(scales, quads, grad_attn, probs, first, steps, earlier=()):
    quad = pl.BlockSpec((3, QUAD, GROUP * TILE), lambda t: (0, 0, t + first))
    return pl.pallas_call(
        functools.partial(backward_kernel, first),
        grid=(steps,),
        in_specs=[pl.BlockSpec(memory_space=pltpu.SMEM)]
        + [quad] * 4
        + [
            pl.BlockSpec((TOKENS, GROUP * TILE), lambda t: (0, t + first)),
            pl.BlockSpec((GROUP * PER_TILE, TOKENS, TOKENS), lambda t: (t + first, 0, 0)),
        ]
        + [pl.BlockSpec(memory_space=pl.ANY)] * len(earlier),
        out_specs=[quad] * 4 + [pl.BlockSpec((GROUP, 32, TILE), lambda t: (t + first, 0, 0))],
        out_shape=[jax.ShapeDtypeStruct((3, QUAD, INNER), BF16)] * 4
        + [jax.ShapeDtypeStruct((INNER // TILE, 32, TILE), BF16)],
        input_output_aliases={7 + i: i for i in range(len(earlier))},
        compiler_params=params(),
        cost_estimate=cost(8e9, 10e6),
        name="backward",
    )(scales, *quads, grad_attn, probs, *earlier)


def outer_kernel(place_ref, own_ref, other_ref, drop_ref, drop_other_ref, *refs):
    outs, left_ref = refs[:NX], refs[NX]
    goal, source = iota((64, TILE), 0), iota((64, TILE), 1)
    wanted = ((goal // 4) % NZ) * 16 + (goal // 32) * 8 + place_ref[3] * 4 + goal % 4
    pick = jnp.where(source == wanted, 1.0, 0.0).astype(BF16)
    for tile in range(INNER // TILE):
        rows, goals = slice(TILE * tile, TILE * tile + TILE), slice(64 * tile, 64 * tile + 64)
        left_ref[goals, :TOKENS] = mul(pick, own_ref[rows, :]).astype(BF16)
        left_ref[goals, TOKENS:] = mul(pick, other_ref[rows, :]).astype(BF16)
    for step, out in enumerate(outs):
        start = pl.multiple_of(((place_ref[0] + step) % NX) * 128, 128)
        left = left_ref[pl.ds(start, 128), :]
        for col in range(0, D, 512):
            part = mul(left[:, :TOKENS], drop_ref[:, col : col + 512])
            part = part + mul(left[:, TOKENS:], drop_other_ref[:, col : col + 512])
            out[:, col : col + 512] = part.astype(out.dtype)


def outer_terms(place, own, other, dropped, dropped_other):
    whole = pl.BlockSpec(memory_space=pltpu.VMEM)
    return pl.pallas_call(
        outer_kernel,
        in_specs=[pl.BlockSpec(memory_space=pltpu.SMEM)] + [whole] * 4,
        out_specs=[whole] * NX,
        out_shape=[jax.ShapeDtypeStruct((128, D), F32 if s == 0 else BF16) for s in range(NX)],
        scratch_shapes=[pltpu.VMEM((512, 2 * TOKENS), BF16)],
        compiler_params=params(),
        cost_estimate=cost(1.1e9, 6e6),
        name="outer_terms",
    )(place, own, other, dropped, dropped_other)


def sum_y_kernel(place_ref, *refs):
    terms, outs = refs[:4], refs[4:8]
    for step, out in enumerate(outs):
        y = (place_ref[1] + step) % 4
        start = pl.multiple_of(((y % 2) * 2 + y // 2) * 32, 32)
        rows = pl.ds(start, 32)
        total = terms[0][rows, :]
        for term in terms[1:]:
            total = total + term[rows, :].astype(F32)
        out[...] = total.astype(out.dtype)


def sum_for_y(place, terms):
    whole = pl.BlockSpec(memory_space=pltpu.VMEM)
    return pl.pallas_call(
        sum_y_kernel,
        in_specs=[pl.BlockSpec(memory_space=pltpu.SMEM)] + [whole] * 4,
        out_specs=[whole] * 4,
        out_shape=[jax.ShapeDtypeStruct((32, D), F32 if s == 0 else BF16) for s in range(4)],
        compiler_params=params(),
        name="sum_for_y",
    )(place, *terms)


def sum_z_kernel(*refs):
    terms, piece, out = refs[:4], refs[4], refs[5]
    total = terms[0][...]
    for term in terms[1:]:
        total = total + term[...].astype(F32)
    for z in range(NZ):
        out[z, :, :D] = total[4 * z : 4 * z + 4].astype(BF16)
        for part in range(8):
            lanes = slice(D + TILE * part, D + TILE * part + TILE)
            out[z, :, lanes] = piece[4 * part : 4 * part + 4].astype(BF16)


def sum_for_z(terms, piece):
    whole = pl.BlockSpec(memory_space=pltpu.VMEM)
    return pl.pallas_call(
        sum_z_kernel,
        in_specs=[whole] * 5,
        out_specs=whole,
        out_shape=jax.ShapeDtypeStruct((NZ, 4, D + 8 * TILE), BF16),
        compiler_params=params(),
        name="sum_for_z",
    )(*terms, piece)


def place_scalars():
    x, y, z, core = coordinates()
    return jnp.stack([x, y, z, core]).astype(jnp.int32)


def along_z_exchange(value):
    rest = NYH * NCORE
    groups = [[rest * z + one for z in range(NZ)] for one in range(rest)]
    return lax.all_to_all(value, "col", 0, 0, axis_index_groups=groups, tiled=True)


def table_pieces(part):
    return jnp.sum(along_z_exchange(part).astype(F32), axis=0)


def table_plane(piece):
    cols, rest = NZ * NYH * NCORE, NYH * NCORE
    groups = [
        [cols * row + rest * z + one for row in range(NX * NYL) for one in range(rest)]
        for z in range(NZ)
    ]
    same = jnp.broadcast_to(piece.astype(BF16), (len(groups[0]), 32, TILE))
    found = lax.all_to_all(
        same, ("row", "col"), 0, 0, axis_index_groups=groups, tiled=True
    )
    return jnp.sum(found.astype(F32), axis=0) / WINDOWS


def totals_kernel(found_ref, weight_ref, table_ref):
    total = found_ref[0, :, :D].astype(F32)
    for z in range(1, NZ):
        total = total + found_ref[z, :, :D].astype(F32)
    weight_ref[...] = total * (1.0 / WINDOWS)
    for tile in range(INNER // TILE):
        parts = [found_ref[tile, :, D + TILE * p : D + TILE * p + TILE] for p in range(8)]
        rows = jnp.concatenate([part.astype(F32) for part in parts], axis=0)
        for head in range(PER_TILE):
            place = rows[:, 32 * head : 32 * head + 32]
            table_ref[PER_TILE * tile + head] = place[:SIDE, :SIDE]


def totals(terms, piece):
    terms = [terms[0]] + [move(terms[s], along_y(s)) for s in range(1, 4)]
    found = along_z_exchange(sum_for_z(terms, piece))
    whole = pl.BlockSpec(memory_space=pltpu.VMEM)
    weight, table = pl.pallas_call(
        totals_kernel,
        in_specs=[whole],
        out_specs=[whole] * 2,
        out_shape=[
            jax.ShapeDtypeStruct((4, D), F32),
            jax.ShapeDtypeStruct((HEADS, SIDE, SIDE), F32),
        ],
        compiler_params=params(),
        name="totals",
    )(found)
    log_sum = found[:, 3, D + 7 * TILE :: 32].astype(F32)
    return weight, table, log_sum.reshape(HEADS)


def per_device(
    query_map, key_map, value_map, out_grad, keep_mask, log_scale, bias_table, proj_weight
):
    logit_scale = jnp.exp(log_scale)
    tl, tr, bl, br = split_maps(query_map, key_map, value_map)
    quads = (br, move_map(tr, -1, 0), move_map(bl, 0, -1), move_map(tl, -1, -1))
    bias = bias_blocks(bias_table)
    tl, tr, bl, br = split_dropped(out_grad, keep_mask)
    bias, tr, bl = lax.optimization_barrier((bias, tr, bl))
    up, left = move_map(tr, -1, 0), move_map(bl, 0, -1)
    quads, tl = lax.optimization_barrier((quads, tl))
    attn_t, probs = forward(logit_scale * LOG2E, quads, bias)
    pieces = (br, up, left, move_map(tl, -1, -1))
    attn_t, pieces = lax.optimization_barrier((attn_t, pieces))
    dropped = jnp.concatenate(pieces, axis=0)
    other, dropped_other = move(attn_t, other_core), move(dropped, other_core)
    grad_attn = lax.dot_general(
        dropped, proj_weight, (((1,), (1,)), ((), ())), preferred_element_type=F32
    ).astype(BF16)
    found = backward(logit_scale, quads, grad_attn, probs, 0, EARLY)
    found, other, dropped_other = lax.optimization_barrier((found, other, dropped_other))
    place = place_scalars()
    terms = outer_terms(place, attn_t, other, dropped, dropped_other)
    terms, found = lax.optimization_barrier((terms, found))
    g_tl, g_bl, g_tr, g_br, table_part = backward(
        logit_scale, quads, grad_attn, probs, EARLY, INNER // TILE // GROUP - EARLY, found
    )
    near = [move(terms[s], along_x(s)) for s in (1, 3)]
    across = move(terms[2], along_x(2))
    near, g_tl, g_bl, g_tr, g_br, table_part = lax.optimization_barrier(
        (near, g_tl, g_bl, g_tr, g_br, table_part)
    )
    arrived = (move_map(g_br, 1, 1), move_map(g_bl, 1, 0), move_map(g_tr, 0, 1))
    piece = table_plane(table_pieces(table_part))
    across, arrived = lax.optimization_barrier((across, arrived))
    terms = sum_for_y(place, (terms[0], near[0], across, near[1]))
    grads = join_maps(*arrived, g_tl)
    weight_grad, table_grad, log_grad = totals(terms, piece)
    return (*grads, weight_grad, table_grad, log_grad)


def solution(mesh):
    return jax.shard_map(
        per_device,
        mesh=mesh,
        in_specs=(
            P("row", "col", None),
            P("row", "col", None),
            P("row", "col", None),
            P("row", "col", None),
            P("row", "col", None),
            P(),
            P(),
            P(),
        ),
        out_specs=(
            P("row", "col", None),
            P("row", "col", None),
            P("row", "col", None),
            P(("row", "col"), None),
            P(),
            P(),
        ),
        check_vma=False,
    )
```

```python
import functools

import jax
import jax.numpy as jnp
import numpy as np
from jax import lax
from jax.experimental import pallas as pl
from jax.experimental.pallas import tpu as pltpu
from jax.sharding import PartitionSpec as P

D = 2048
HEADS = 32
HEAD_DIM = 32
INNER = 1024
WINDOWS = 256
KEEP_RATE = 0.9
SIDE = 31
LOG2E = 1.4426950408889634

NX, NYL, NZ, NYH, NCORE = 4, 2, 8, 2, 2

F32 = jnp.float32
BF16 = jnp.bfloat16
TILE = 128
PER_TILE = TILE // HEAD_DIM
GROUP = 2
BIAS_HEADS = 8
EARLY = 2
QUAD = 64
TOKENS = 256

VMEM_BYTES = 48 * 1024 * 1024


def params(vmem=VMEM_BYTES):
    return pltpu.CompilerParams(vmem_limit_bytes=vmem)


def cost(flops, nbytes):
    return pl.CostEstimate(flops=int(flops), bytes_accessed=int(nbytes), transcendentals=0)


def move(value, target):
    sizes = (NX, NYL, NZ, NYH, NCORE)
    pairs = []
    for src in range(NX * NYL * NZ * NYH * NCORE):
        place = np.unravel_index(src, sizes)
        goal = [int(g) % s for g, s in zip(target(*[int(p) for p in place]), sizes)]
        pairs.append((src, int(np.ravel_multi_index(goal, sizes))))
    return lax.ppermute(value, ("row", "col"), pairs)


def move_map(value, d_row, d_col):
    rows, cols = NX * NYL, NZ * NYH * NCORE
    pairs = [
        (r * cols + c, ((r + d_row) % rows) * cols + (c + d_col) % cols)
        for r in range(rows)
        for c in range(cols)
    ]
    return lax.ppermute(value, ("row", "col"), pairs)


def along_x(step):
    return lambda x, yl, z, yh, c: (x + step, yl, z, yh, c)


def along_y(step):
    def goal(x, yl, z, yh, c):
        y = (2 * yh + yl + step) % 4
        return (x, y % 2, z, y // 2, c)

    return goal


def along_z(step):
    return lambda x, yl, z, yh, c: (x, yl, z + step, yh, c)


def other_core(x, yl, z, yh, c):
    return (x, yl, z, yh, 1 - c)


def coordinates():
    row = lax.axis_index("row")
    col = lax.axis_index("col")
    x, y_lo = row // 2, row % 2
    z, y_hi, core = col // 4, (col // 2) % 2, col % 2
    return x, 2 * y_hi + y_lo, z, core


def quarters_of(block):
    n = block.shape[-1]
    cut = lambda a, b: block[a : a + 8, b : b + 8, :].reshape(QUAD, n).astype(BF16)
    return cut(0, 0), cut(0, 8), cut(8, 0), cut(8, 8)


def split_kernel(q_ref, k_ref, v_ref, tl_ref, tr_ref, bl_ref, br_ref):
    for which, ref in enumerate((q_ref, k_ref, v_ref)):
        for out, part in zip((tl_ref, tr_ref, bl_ref, br_ref), quarters_of(ref[...].astype(F32))):
            out[which] = part


def split_maps(query_map, key_map, value_map):
    spec = pl.BlockSpec((16, 16, 256), lambda t: (0, 0, t))
    out = pl.BlockSpec((3, QUAD, 256), lambda t: (0, 0, t))
    return pl.pallas_call(
        split_kernel,
        grid=(INNER // 256,),
        in_specs=[spec] * 3,
        out_specs=[out] * 4,
        out_shape=[jax.ShapeDtypeStruct((3, QUAD, INNER), BF16)] * 4,
        compiler_params=params(60 * 1024 * 1024),
        name="split_maps",
    )(query_map, key_map, value_map)


def drop_kernel(grad_ref, keep_ref, tl_ref, tr_ref, bl_ref, br_ref):
    dropped = grad_ref[...].astype(F32) * keep_ref[...].astype(F32) * (1.0 / KEEP_RATE)
    for out, part in zip((tl_ref, tr_ref, bl_ref, br_ref), quarters_of(dropped)):
        out[...] = part


def split_dropped(out_grad, keep_mask):
    spec = pl.BlockSpec((16, 16, 512), lambda t: (0, 0, t))
    out = pl.BlockSpec((QUAD, 512), lambda t: (0, t))
    return pl.pallas_call(
        drop_kernel,
        grid=(D // 512,),
        in_specs=[spec] * 2,
        out_specs=[out] * 4,
        out_shape=[jax.ShapeDtypeStruct((QUAD, D), BF16)] * 4,
        compiler_params=params(60 * 1024 * 1024),
        name="split_dropped",
    )(out_grad, keep_mask)


def join_kernel(tl_ref, tr_ref, bl_ref, br_ref, *outs):
    for which, out in enumerate(outs):
        part = lambda ref: ref[which].astype(F32).reshape(8, 8, ref.shape[-1])
        out[:8] = jnp.concatenate([part(tl_ref), part(tr_ref)], axis=1).astype(BF16)
        out[8:] = jnp.concatenate([part(bl_ref), part(br_ref)], axis=1).astype(BF16)


def join_maps(tl, tr, bl, br):
    spec = pl.BlockSpec((3, QUAD, 256), lambda t: (0, 0, t))
    out = pl.BlockSpec((16, 16, 256), lambda t: (0, 0, t))
    return pl.pallas_call(
        join_kernel,
        grid=(INNER // 256,),
        in_specs=[spec] * 4,
        out_specs=[out] * 3,
        out_shape=[jax.ShapeDtypeStruct((16, 16, INNER), BF16)] * 3,
        compiler_params=params(),
        name="join_maps",
    )(tl, tr, bl, br)


def bias_kernel(table_ref, out_ref):
    lane = iota((BIAS_HEADS, 8, 256), 2)
    turn = jnp.where(iota((SIDE, 32), 0) + iota((SIDE, 32), 1) == 30, LOG2E, 0.0)
    spread = jnp.where(iota((SIDE, 256), 1) // 8 == iota((SIDE, 256), 0), 1.0, 0.0)
    exact = dict(precision=lax.Precision.HIGHEST, preferred_element_type=F32)
    turned = [jnp.dot(table_ref[head], turn, **exact) for head in range(BIAS_HEADS)]
    wide = jnp.stack(
        [lax.dot_general(rows, spread, (((0,), (0,)), ((), ())), **exact) for rows in turned]
    )
    for d in range(3):
        strip = jnp.zeros((BIAS_HEADS, 8, 256), F32)
        for xi in range(8):
            first = 23 - 8 * d - xi
            strip = jnp.where(lane % 8 == xi, wide[:, first : first + 8, :], strip)
        strip = strip.reshape(BIAS_HEADS * 8, 256)
        for yj in range(16):
            start = 8 * (15 - yj)
            moved = strip if start == 0 else pltpu.roll(strip, 256 - start, 1)
            out_ref[:, d, 8 * yj : 8 * yj + 8, :] = moved[:, :128].reshape(BIAS_HEADS, 8, 128)


def bias_blocks(bias_table):
    return pl.pallas_call(
        bias_kernel,
        grid=(HEADS // BIAS_HEADS,),
        in_specs=[pl.BlockSpec((BIAS_HEADS, SIDE, SIDE), lambda t: (t, 0, 0))],
        out_specs=pl.BlockSpec((BIAS_HEADS, 3, 128, 128), lambda t: (t, 0, 0, 0)),
        out_shape=jax.ShapeDtypeStruct((HEADS, 3, 128, 128), F32),
        compiler_params=params(),
        cost_estimate=cost(1e7, 8e6),
        name="bias_blocks",
    )(bias_table)


def iota(shape, dim):
    return lax.broadcasted_iota(jnp.int32, shape, dim)


def per_head_sum(value):
    high = value.astype(BF16)
    low = (value - high.astype(F32)).astype(BF16)
    shape = (2 * TILE, TILE)
    same = (iota(shape, 0) % TILE) // HEAD_DIM == iota(shape, 1) // HEAD_DIM
    ones = jnp.where(same, 1.0, 0.0).astype(BF16)
    both = jnp.concatenate([high, low], axis=1)
    return jnp.dot(both, ones, preferred_element_type=F32)


def normalize(rows):
    value = rows.astype(F32)
    length = jnp.sqrt(per_head_sum(value * value))
    inverse = 1.0 / jnp.maximum(length, 1.0)
    return value * inverse, length, inverse


def normalize_back(unit, length, inverse, grad):
    projection = per_head_sum(unit * grad)
    return jnp.where(length > 1.0, (grad - unit * projection) * inverse, grad)


def of_head(rows, head):
    keep = iota(rows.shape, 1) // HEAD_DIM == head
    return jnp.where(keep, rows, jnp.zeros_like(rows))


def rows_of(refs, which, tile):
    lanes = slice(TILE * tile, TILE * tile + TILE)
    return jnp.concatenate([ref[which, :, lanes] for ref in refs], axis=0)


def mul(left, right):
    return jnp.dot(left, right, preferred_element_type=F32)


def head_rows(head):
    return slice(HEAD_DIM * head, HEAD_DIM * head + HEAD_DIM)


def cosines_of(k_round, q_round):
    q_t = q_round.T
    return [mul(of_head(k_round, head), q_t) for head in range(PER_TILE)]


def forward_kernel(scale_ref, tl_ref, bl_ref, tr_ref, br_ref, bias_ref, attn_ref, probs_ref):
    step = pl.program_id(0)
    quads = (tl_ref, bl_ref, tr_ref, br_ref)
    cosines, values_t = [], []
    for tile in range(GROUP):
        q_round = normalize(rows_of(quads, 0, tile))[0].astype(BF16)
        k_round = normalize(rows_of(quads, 1, tile))[0].astype(BF16)
        values_t.append(rows_of(quads, 2, tile).T)
        cosines += cosines_of(k_round, q_round)
    rounded = []
    for head in range(GROUP * PER_TILE):
        scale = scale_ref[step * GROUP * PER_TILE + head]
        halves = []
        for half in range(2):
            lanes = slice(128 * half, 128 * half + 128)
            bias = jnp.concatenate([bias_ref[head, 1 + half], bias_ref[head, half]], axis=0)
            scores = cosines[head][:, lanes] * scale + bias
            weights = jnp.exp2(scores - jnp.max(scores, axis=0, keepdims=True))
            probs = weights * (1.0 / jnp.sum(weights, axis=0, keepdims=True))
            probs_ref[head, :, lanes] = probs
            halves.append(probs.astype(BF16))
        rounded.append(jnp.concatenate(halves, axis=1))
    for head in range(GROUP * PER_TILE):
        value_t = values_t[head // PER_TILE][head_rows(head % PER_TILE)]
        attn_ref[head_rows(head), :] = mul(value_t, rounded[head]).astype(BF16)


def quad_spec():
    return pl.BlockSpec((3, QUAD, GROUP * TILE), lambda t: (0, 0, t))


def probs_spec():
    return pl.BlockSpec((GROUP * PER_TILE, TOKENS, TOKENS), lambda t: (t, 0, 0))


def forward(scales, quads, bias):
    return pl.pallas_call(
        forward_kernel,
        grid=(INNER // TILE // GROUP,),
        in_specs=[pl.BlockSpec(memory_space=pltpu.SMEM)]
        + [quad_spec()] * 4
        + [pl.BlockSpec((GROUP * PER_TILE, 3, 128, 128), lambda t: (t, 0, 0, 0))],
        out_specs=[pl.BlockSpec((GROUP * TILE, TOKENS), lambda t: (t, 0)), probs_spec()],
        out_shape=[
            jax.ShapeDtypeStruct((INNER, TOKENS), BF16),
            jax.ShapeDtypeStruct((HEADS, TOKENS, TOKENS), F32),
        ],
        compiler_params=params(),
        cost_estimate=cost(8e9, 16e6),
        name="forward",
    )(scales, *quads, bias)


def diagonal_sums(blocks):
    lane = iota((8, 128), 1)
    strips = []
    for block in blocks:
        total = jnp.zeros((8, 128), F32)
        first = jnp.zeros((8, 128), F32)
        for yj in range(16):
            start = 8 * (15 - yj)
            piece = block[8 * yj : 8 * yj + 8]
            if start:
                piece = pltpu.roll(piece, start, 1)
                first = first + jnp.where(lane >= start, piece, 0.0)
            else:
                first = first + piece
            total = total + piece
        strips.append(jnp.concatenate([first, total - first], axis=1))
    return strips


def offset_sums(strips):
    shape = strips[0].shape
    xj, lane = iota(shape, 0) % 8, iota(shape, 1)
    even = ((lane + xj) // 8) % 2 == 0
    sums = []
    for strip in strips:
        for bit in range(3):
            moved = pltpu.roll(strip, 256 - (1 << bit), 1)
            strip = jnp.where((xj // (1 << bit)) % 2 == 1, moved, strip)
        part = jnp.where(even, strip, 0.0)
        total = lambda v: jnp.sum(v.reshape(PER_TILE, 8, 256), axis=1)
        sums.append((pltpu.roll(total(part), 7, 1), pltpu.roll(total(strip - part), 255, 1)))
    inner = iota((PER_TILE, 256), 1) % 16
    result = []
    for parity in range(2):
        left, middle, right = (pair[parity] for pair in sums)
        result.append(left + jnp.where(inner >= 8, pltpu.roll(middle, 8, 1), 0.0))
        result.append(right + jnp.where(inner < 8, pltpu.roll(middle, 248, 1), 0.0))
    return result


def table_of(strips, log_sums):
    rows = offset_sums(strips)
    spot = iota((PER_TILE, 256), 1) == 240
    rows[2] = jnp.where(spot, jnp.concatenate(log_sums, axis=0), rows[2])
    shape = (32, 256)
    k, lane = iota(shape, 0), iota(shape, 1)
    mine, odd = lane // 16 == k // 2, k % 2 == 1
    total = jnp.zeros((PER_TILE * 32, TILE), F32)
    for half in range(2):
        picked = []
        for head in range(PER_TILE):
            both = jnp.where(odd, rows[2 + half][head : head + 1], rows[half][head : head + 1])
            picked.append(jnp.where(mine, both, 0.0).astype(BF16))
        source, goal = iota((256, TILE), 0), iota((256, TILE), 1)
        place = jnp.where(goal == 16 * half + source % 16, 1.0, 0.0).astype(BF16)
        total = total + mul(jnp.concatenate(picked, axis=0), place)
    table = total[:32]
    for head in range(1, PER_TILE):
        table = table + pltpu.roll(total[32 * head : 32 * head + 32], 32 * head, 1)
    return table


def backward_kernel(
    first_step,
    scale_ref,
    tl_ref,
    bl_ref,
    tr_ref,
    br_ref,
    grad_ref,
    probs_ref,
    *refs,
):
    gtl_ref, gbl_ref, gtr_ref, gbr_ref, table_ref = refs[-5:]
    step = pl.program_id(0) + first_step
    quads = (tl_ref, bl_ref, tr_ref, br_ref)
    heads = range(GROUP * PER_TILE)
    queries, keys, grads, grad_probs, cosines = [], [], [], [], []
    for tile in range(GROUP):
        queries.append(normalize(rows_of(quads, 0, tile)))
        keys.append(normalize(rows_of(quads, 1, tile)))
        grads.append(grad_ref[:, TILE * tile : TILE * tile + TILE])
        value, grad_t = rows_of(quads, 2, tile), grads[-1].T
        grad_probs += [mul(of_head(value, head), grad_t) for head in range(PER_TILE)]
        cosines += cosines_of(keys[-1][0].astype(BF16), queries[-1][0].astype(BF16))
    prob_rounds, grad_coss, blocks, log_sums = [], [], [], []
    for head in heads:
        scale = scale_ref[step * GROUP * PER_TILE + head]
        log_sum = jnp.zeros((1, 128), F32)
        halves, rounded, cos_grads = [], [], []
        for half in range(2):
            lanes = slice(128 * half, 128 * half + 128)
            probs = probs_ref[head, :, lanes]
            part = grad_probs[head][:, lanes]
            inner = jnp.sum(probs * part, axis=0, keepdims=True)
            score_grad = probs * (part - inner)
            halves.append(score_grad)
            log_sum = log_sum + jnp.sum(
                score_grad * cosines[head][:, lanes], axis=0, keepdims=True
            )
            rounded.append(probs.astype(BF16))
            cos_grads.append((score_grad * scale).astype(BF16))
        blocks.append((halves[0][128:], halves[0][:128] + halves[1][128:], halves[1][:128]))
        prob_rounds.append(jnp.concatenate(rounded, axis=1))
        grad_coss.append(jnp.concatenate(cos_grads, axis=1))
        log_sums.append(scale * jnp.sum(log_sum, axis=1, keepdims=True))
    for tile in range(GROUP):
        grad_v = jnp.zeros((TOKENS, TILE), F32)
        grad_k = jnp.zeros((TOKENS, TILE), F32)
        grad_q = []
        q_round, key_t = queries[tile][0].astype(BF16), keys[tile][0].astype(BF16).T
        for head in range(PER_TILE):
            grad_cos = grad_coss[PER_TILE * tile + head]
            grad_q.append(mul(key_t[head_rows(head)], grad_cos))
            grad_v = grad_v + mul(prob_rounds[PER_TILE * tile + head], of_head(grads[tile], head))
            grad_k = grad_k + mul(grad_cos, of_head(q_round, head))
        results = (
            normalize_back(*queries[tile], jnp.concatenate(grad_q, axis=0).T).astype(BF16),
            normalize_back(*keys[tile], grad_k).astype(BF16),
            grad_v.astype(BF16),
        )
        lanes = slice(TILE * tile, TILE * tile + TILE)
        for part, ref in enumerate((gtl_ref, gbl_ref, gtr_ref, gbr_ref)):
            for which, result in enumerate(results):
                ref[which, :, lanes] = result[QUAD * part : QUAD * part + QUAD]
    for tile in range(GROUP):
        mine = range(PER_TILE * tile, PER_TILE * tile + PER_TILE)
        found = [diagonal_sums(blocks[head]) for head in mine]
        strips = [jnp.concatenate([strip[d] for strip in found], axis=0) for d in range(3)]
        table_ref[tile] = table_of(strips, [log_sums[head] for head in mine]).astype(BF16)


def backward(scales, quads, grad_attn, probs, first, steps, earlier=()):
    quad = pl.BlockSpec((3, QUAD, GROUP * TILE), lambda t: (0, 0, t + first))
    return pl.pallas_call(
        functools.partial(backward_kernel, first),
        grid=(steps,),
        in_specs=[pl.BlockSpec(memory_space=pltpu.SMEM)]
        + [quad] * 4
        + [
            pl.BlockSpec((TOKENS, GROUP * TILE), lambda t: (0, t + first)),
            pl.BlockSpec((GROUP * PER_TILE, TOKENS, TOKENS), lambda t: (t + first, 0, 0)),
        ]
        + [pl.BlockSpec(memory_space=pl.ANY)] * len(earlier),
        out_specs=[quad] * 4 + [pl.BlockSpec((GROUP, 32, TILE), lambda t: (t + first, 0, 0))],
        out_shape=[jax.ShapeDtypeStruct((3, QUAD, INNER), BF16)] * 4
        + [jax.ShapeDtypeStruct((INNER // TILE, 32, TILE), BF16)],
        input_output_aliases={7 + i: i for i in range(len(earlier))},
        compiler_params=params(),
        cost_estimate=cost(8e9, 10e6),
        name="backward",
    )(scales, *quads, grad_attn, probs, *earlier)


def outer_kernel(place_ref, own_ref, other_ref, drop_ref, drop_other_ref, *refs):
    outs, left_ref = refs[:NX], refs[NX]
    goal, source = iota((64, TILE), 0), iota((64, TILE), 1)
    wanted = ((goal // 4) % NZ) * 16 + (goal // 32) * 8 + place_ref[3] * 4 + goal % 4
    pick = jnp.where(source == wanted, 1.0, 0.0).astype(BF16)
    for tile in range(INNER // TILE):
        rows, goals = slice(TILE * tile, TILE * tile + TILE), slice(64 * tile, 64 * tile + 64)
        left_ref[goals, :TOKENS] = mul(pick, own_ref[rows, :]).astype(BF16)
        left_ref[goals, TOKENS:] = mul(pick, other_ref[rows, :]).astype(BF16)
    for step, out in enumerate(outs):
        start = pl.multiple_of(((place_ref[0] + step) % NX) * 128, 128)
        left = left_ref[pl.ds(start, 128), :]
        for col in range(0, D, 512):
            part = mul(left[:, :TOKENS], drop_ref[:, col : col + 512])
            part = part + mul(left[:, TOKENS:], drop_other_ref[:, col : col + 512])
            out[:, col : col + 512] = part.astype(out.dtype)


def outer_terms(place, own, other, dropped, dropped_other):
    whole = pl.BlockSpec(memory_space=pltpu.VMEM)
    return pl.pallas_call(
        outer_kernel,
        in_specs=[pl.BlockSpec(memory_space=pltpu.SMEM)] + [whole] * 4,
        out_specs=[whole] * NX,
        out_shape=[jax.ShapeDtypeStruct((128, D), F32 if s == 0 else BF16) for s in range(NX)],
        scratch_shapes=[pltpu.VMEM((512, 2 * TOKENS), BF16)],
        compiler_params=params(),
        cost_estimate=cost(1.1e9, 6e6),
        name="outer_terms",
    )(place, own, other, dropped, dropped_other)


def sum_y_kernel(place_ref, *refs):
    terms, outs = refs[:4], refs[4:8]
    for step, out in enumerate(outs):
        y = (place_ref[1] + step) % 4
        start = pl.multiple_of(((y % 2) * 2 + y // 2) * 32, 32)
        rows = pl.ds(start, 32)
        total = terms[0][rows, :]
        for term in terms[1:]:
            total = total + term[rows, :].astype(F32)
        out[...] = total.astype(out.dtype)


def sum_for_y(place, terms):
    whole = pl.BlockSpec(memory_space=pltpu.VMEM)
    return pl.pallas_call(
        sum_y_kernel,
        in_specs=[pl.BlockSpec(memory_space=pltpu.SMEM)] + [whole] * 4,
        out_specs=[whole] * 4,
        out_shape=[jax.ShapeDtypeStruct((32, D), F32 if s == 0 else BF16) for s in range(4)],
        compiler_params=params(),
        name="sum_for_y",
    )(place, *terms)


def sum_z_kernel(*refs):
    terms, piece, out = refs[:4], refs[4], refs[5]
    total = terms[0][...]
    for term in terms[1:]:
        total = total + term[...].astype(F32)
    for z in range(NZ):
        out[z, :, :D] = total[4 * z : 4 * z + 4].astype(BF16)
        for part in range(8):
            lanes = slice(D + TILE * part, D + TILE * part + TILE)
            out[z, :, lanes] = piece[4 * part : 4 * part + 4].astype(BF16)


def sum_for_z(terms, piece):
    whole = pl.BlockSpec(memory_space=pltpu.VMEM)
    return pl.pallas_call(
        sum_z_kernel,
        in_specs=[whole] * 5,
        out_specs=whole,
        out_shape=jax.ShapeDtypeStruct((NZ, 4, D + 8 * TILE), BF16),
        compiler_params=params(),
        name="sum_for_z",
    )(*terms, piece)


def place_scalars():
    x, y, z, core = coordinates()
    return jnp.stack([x, y, z, core]).astype(jnp.int32)


def along_z_exchange(value):
    rest = NYH * NCORE
    groups = [[rest * z + one for z in range(NZ)] for one in range(rest)]
    return lax.all_to_all(value, "col", 0, 0, axis_index_groups=groups, tiled=True)


def table_pieces(part):
    return jnp.sum(along_z_exchange(part).astype(F32), axis=0)


def table_plane(piece):
    cols, rest = NZ * NYH * NCORE, NYH * NCORE
    groups = [
        [cols * row + rest * z + one for row in range(NX * NYL) for one in range(rest)]
        for z in range(NZ)
    ]
    same = jnp.broadcast_to(piece.astype(BF16), (len(groups[0]), 32, TILE))
    found = lax.all_to_all(
        same, ("row", "col"), 0, 0, axis_index_groups=groups, tiled=True
    )
    return jnp.sum(found.astype(F32), axis=0) / WINDOWS


def totals_kernel(found_ref, weight_ref, table_ref):
    total = found_ref[0, :, :D].astype(F32)
    for z in range(1, NZ):
        total = total + found_ref[z, :, :D].astype(F32)
    weight_ref[...] = total * (1.0 / WINDOWS)
    for tile in range(INNER // TILE):
        parts = [found_ref[tile, :, D + TILE * p : D + TILE * p + TILE] for p in range(8)]
        rows = jnp.concatenate([part.astype(F32) for part in parts], axis=0)
        for head in range(PER_TILE):
            place = rows[:, 32 * head : 32 * head + 32]
            table_ref[PER_TILE * tile + head] = place[:SIDE, :SIDE]


def totals(terms, piece):
    terms = [terms[0]] + [move(terms[s], along_y(s)) for s in range(1, 4)]
    found = along_z_exchange(sum_for_z(terms, piece))
    whole = pl.BlockSpec(memory_space=pltpu.VMEM)
    weight, table = pl.pallas_call(
        totals_kernel,
        in_specs=[whole],
        out_specs=[whole] * 2,
        out_shape=[
            jax.ShapeDtypeStruct((4, D), F32),
            jax.ShapeDtypeStruct((HEADS, SIDE, SIDE), F32),
        ],
        compiler_params=params(),
        name="totals",
    )(found)
    log_sum = found[:, 3, D + 7 * TILE :: 32].astype(F32)
    return weight, table, log_sum.reshape(HEADS)


def per_device(
    query_map, key_map, value_map, out_grad, keep_mask, log_scale, bias_table, proj_weight
):
    logit_scale = jnp.exp(log_scale)
    tl, tr, bl, br = split_maps(query_map, key_map, value_map)
    quads = (br, move_map(tr, -1, 0), move_map(bl, 0, -1), move_map(tl, -1, -1))
    bias = bias_blocks(bias_table)
    tl, tr, bl, br = split_dropped(out_grad, keep_mask)
    bias, tr, bl = lax.optimization_barrier((bias, tr, bl))
    up, left = move_map(tr, -1, 0), move_map(bl, 0, -1)
    quads, tl = lax.optimization_barrier((quads, tl))
    attn_t, probs = forward(logit_scale * LOG2E, quads, bias)
    pieces = (br, up, left, move_map(tl, -1, -1))
    attn_t, pieces = lax.optimization_barrier((attn_t, pieces))
    dropped = jnp.concatenate(pieces, axis=0)
    other, dropped_other = move(attn_t, other_core), move(dropped, other_core)
    grad_attn = lax.dot_general(
        dropped, proj_weight, (((1,), (1,)), ((), ())), preferred_element_type=F32
    ).astype(BF16)
    found = backward(logit_scale, quads, grad_attn, probs, 0, EARLY)
    found, other, dropped_other = lax.optimization_barrier((found, other, dropped_other))
    place = place_scalars()
    terms = outer_terms(place, attn_t, other, dropped, dropped_other)
    terms, found = lax.optimization_barrier((terms, found))
    g_tl, g_bl, g_tr, g_br, table_part = backward(
        logit_scale, quads, grad_attn, probs, EARLY, INNER // TILE // GROUP - EARLY, found
    )
    down, right = move_map(g_bl, 1, 0), move_map(g_tr, 0, 1)
    sent = [move(terms[s], along_x(s)) for s in range(1, NX)]
    sent[0], sent[2], g_br, table_part = lax.optimization_barrier(
        (sent[0], sent[2], g_br, table_part)
    )
    arrived = (move_map(g_br, 1, 1), down, right)
    piece = table_pieces(table_part)
    sent, arrived = lax.optimization_barrier((sent, arrived))
    terms = sum_for_y(place, (terms[0], *sent))
    terms, piece = lax.optimization_barrier((terms, piece))
    piece = table_plane(piece)
    grads = join_maps(*arrived, g_tl)
    weight_grad, table_grad, log_grad = totals(terms, piece)
    return (*grads, weight_grad, table_grad, log_grad)


def solution(mesh):
    return jax.shard_map(
        per_device,
        mesh=mesh,
        in_specs=(
            P("row", "col", None),
            P("row", "col", None),
            P("row", "col", None),
            P("row", "col", None),
            P("row", "col", None),
            P(),
            P(),
            P(),
        ),
        out_specs=(
            P("row", "col", None),
            P("row", "col", None),
            P("row", "col", None),
            P(("row", "col"), None),
            P(),
            P(),
        ),
        check_vma=False,
    )
```

```python
import functools

import jax
import jax.numpy as jnp
import numpy as np
from jax import lax
from jax.experimental import pallas as pl
from jax.experimental.pallas import tpu as pltpu
from jax.sharding import PartitionSpec as P

D = 2048
HEADS = 32
HEAD_DIM = 32
INNER = 1024
WINDOWS = 256
KEEP_RATE = 0.9
SIDE = 31
LOG2E = 1.4426950408889634

NX, NYL, NZ, NYH, NCORE = 4, 2, 8, 2, 2

F32 = jnp.float32
BF16 = jnp.bfloat16
TILE = 128
PER_TILE = TILE // HEAD_DIM
GROUP = 2
BIAS_HEADS = 8
EARLY = 2
QUAD = 64
TOKENS = 256

VMEM_BYTES = 48 * 1024 * 1024


def params(vmem=VMEM_BYTES):
    return pltpu.CompilerParams(vmem_limit_bytes=vmem)


def cost(flops, nbytes):
    return pl.CostEstimate(flops=int(flops), bytes_accessed=int(nbytes), transcendentals=0)


def move(value, target):
    sizes = (NX, NYL, NZ, NYH, NCORE)
    pairs = []
    for src in range(NX * NYL * NZ * NYH * NCORE):
        place = np.unravel_index(src, sizes)
        goal = [int(g) % s for g, s in zip(target(*[int(p) for p in place]), sizes)]
        pairs.append((src, int(np.ravel_multi_index(goal, sizes))))
    return lax.ppermute(value, ("row", "col"), pairs)


def move_map(value, d_row, d_col):
    rows, cols = NX * NYL, NZ * NYH * NCORE
    pairs = [
        (r * cols + c, ((r + d_row) % rows) * cols + (c + d_col) % cols)
        for r in range(rows)
        for c in range(cols)
    ]
    return lax.ppermute(value, ("row", "col"), pairs)


def along_x(step):
    return lambda x, yl, z, yh, c: (x + step, yl, z, yh, c)


def along_y(step):
    def goal(x, yl, z, yh, c):
        y = (2 * yh + yl + step) % 4
        return (x, y % 2, z, y // 2, c)

    return goal


def along_z(step):
    return lambda x, yl, z, yh, c: (x, yl, z + step, yh, c)


def other_core(x, yl, z, yh, c):
    return (x, yl, z, yh, 1 - c)


def coordinates():
    row = lax.axis_index("row")
    col = lax.axis_index("col")
    x, y_lo = row // 2, row % 2
    z, y_hi, core = col // 4, (col // 2) % 2, col % 2
    return x, 2 * y_hi + y_lo, z, core


def quarters_of(block):
    n = block.shape[-1]
    cut = lambda a, b: block[a : a + 8, b : b + 8, :].reshape(QUAD, n).astype(BF16)
    return cut(0, 0), cut(0, 8), cut(8, 0), cut(8, 8)


def split_kernel(q_ref, k_ref, v_ref, tl_ref, tr_ref, bl_ref, br_ref):
    for which, ref in enumerate((q_ref, k_ref, v_ref)):
        for out, part in zip((tl_ref, tr_ref, bl_ref, br_ref), quarters_of(ref[...].astype(F32))):
            out[which] = part


def split_maps(query_map, key_map, value_map):
    spec = pl.BlockSpec((16, 16, 256), lambda t: (0, 0, t))
    out = pl.BlockSpec((3, QUAD, 256), lambda t: (0, 0, t))
    return pl.pallas_call(
        split_kernel,
        grid=(INNER // 256,),
        in_specs=[spec] * 3,
        out_specs=[out] * 4,
        out_shape=[jax.ShapeDtypeStruct((3, QUAD, INNER), BF16)] * 4,
        compiler_params=params(60 * 1024 * 1024),
        name="split_maps",
    )(query_map, key_map, value_map)


def drop_kernel(grad_ref, keep_ref, tl_ref, tr_ref, bl_ref, br_ref):
    dropped = grad_ref[...].astype(F32) * keep_ref[...].astype(F32) * (1.0 / KEEP_RATE)
    for out, part in zip((tl_ref, tr_ref, bl_ref, br_ref), quarters_of(dropped)):
        out[...] = part


def split_dropped(out_grad, keep_mask):
    spec = pl.BlockSpec((16, 16, 512), lambda t: (0, 0, t))
    out = pl.BlockSpec((QUAD, 512), lambda t: (0, t))
    return pl.pallas_call(
        drop_kernel,
        grid=(D // 512,),
        in_specs=[spec] * 2,
        out_specs=[out] * 4,
        out_shape=[jax.ShapeDtypeStruct((QUAD, D), BF16)] * 4,
        compiler_params=params(60 * 1024 * 1024),
        name="split_dropped",
    )(out_grad, keep_mask)


def join_kernel(tl_ref, tr_ref, bl_ref, br_ref, *outs):
    for which, out in enumerate(outs):
        part = lambda ref: ref[which].astype(F32).reshape(8, 8, ref.shape[-1])
        out[:8] = jnp.concatenate([part(tl_ref), part(tr_ref)], axis=1).astype(BF16)
        out[8:] = jnp.concatenate([part(bl_ref), part(br_ref)], axis=1).astype(BF16)


def join_maps(tl, tr, bl, br):
    spec = pl.BlockSpec((3, QUAD, 256), lambda t: (0, 0, t))
    out = pl.BlockSpec((16, 16, 256), lambda t: (0, 0, t))
    return pl.pallas_call(
        join_kernel,
        grid=(INNER // 256,),
        in_specs=[spec] * 4,
        out_specs=[out] * 3,
        out_shape=[jax.ShapeDtypeStruct((16, 16, INNER), BF16)] * 3,
        compiler_params=params(),
        name="join_maps",
    )(tl, tr, bl, br)


def bias_kernel(table_ref, out_ref):
    lane = iota((BIAS_HEADS, 8, 256), 2)
    turn = jnp.where(iota((SIDE, 32), 0) + iota((SIDE, 32), 1) == 30, LOG2E, 0.0)
    spread = jnp.where(iota((SIDE, 256), 1) // 8 == iota((SIDE, 256), 0), 1.0, 0.0)
    exact = dict(precision=lax.Precision.HIGHEST, preferred_element_type=F32)
    turned = [jnp.dot(table_ref[head], turn, **exact) for head in range(BIAS_HEADS)]
    wide = jnp.stack(
        [lax.dot_general(rows, spread, (((0,), (0,)), ((), ())), **exact) for rows in turned]
    )
    for d in range(3):
        strip = jnp.zeros((BIAS_HEADS, 8, 256), F32)
        for xi in range(8):
            first = 23 - 8 * d - xi
            strip = jnp.where(lane % 8 == xi, wide[:, first : first + 8, :], strip)
        strip = strip.reshape(BIAS_HEADS * 8, 256)
        for yj in range(16):
            start = 8 * (15 - yj)
            moved = strip if start == 0 else pltpu.roll(strip, 256 - start, 1)
            out_ref[:, d, 8 * yj : 8 * yj + 8, :] = moved[:, :128].reshape(BIAS_HEADS, 8, 128)


def bias_blocks(bias_table):
    return pl.pallas_call(
        bias_kernel,
        grid=(HEADS // BIAS_HEADS,),
        in_specs=[pl.BlockSpec((BIAS_HEADS, SIDE, SIDE), lambda t: (t, 0, 0))],
        out_specs=pl.BlockSpec((BIAS_HEADS, 3, 128, 128), lambda t: (t, 0, 0, 0)),
        out_shape=jax.ShapeDtypeStruct((HEADS, 3, 128, 128), F32),
        compiler_params=params(),
        cost_estimate=cost(1e7, 8e6),
        name="bias_blocks",
    )(bias_table)


def iota(shape, dim):
    return lax.broadcasted_iota(jnp.int32, shape, dim)


def per_head_sum(value):
    high = value.astype(BF16)
    low = (value - high.astype(F32)).astype(BF16)
    shape = (2 * TILE, TILE)
    same = (iota(shape, 0) % TILE) // HEAD_DIM == iota(shape, 1) // HEAD_DIM
    ones = jnp.where(same, 1.0, 0.0).astype(BF16)
    both = jnp.concatenate([high, low], axis=1)
    return jnp.dot(both, ones, preferred_element_type=F32)


def normalize(rows):
    value = rows.astype(F32)
    length = jnp.sqrt(per_head_sum(value * value))
    inverse = 1.0 / jnp.maximum(length, 1.0)
    return value * inverse, length, inverse


def normalize_back(unit, length, inverse, grad):
    projection = per_head_sum(unit * grad)
    return jnp.where(length > 1.0, (grad - unit * projection) * inverse, grad)


def of_head(rows, head):
    keep = iota(rows.shape, 1) // HEAD_DIM == head
    return jnp.where(keep, rows, jnp.zeros_like(rows))


def rows_of(refs, which, tile):
    lanes = slice(TILE * tile, TILE * tile + TILE)
    return jnp.concatenate([ref[which, :, lanes] for ref in refs], axis=0)


def mul(left, right):
    return jnp.dot(left, right, preferred_element_type=F32)


def head_rows(head):
    return slice(HEAD_DIM * head, HEAD_DIM * head + HEAD_DIM)


def cosines_of(k_round, q_round):
    q_t = q_round.T
    return [mul(of_head(k_round, head), q_t) for head in range(PER_TILE)]


def forward_kernel(scale_ref, tl_ref, bl_ref, tr_ref, br_ref, bias_ref, attn_ref, probs_ref):
    step = pl.program_id(0)
    quads = (tl_ref, bl_ref, tr_ref, br_ref)
    cosines, values_t = [], []
    for tile in range(GROUP):
        q_round = normalize(rows_of(quads, 0, tile))[0].astype(BF16)
        k_round = normalize(rows_of(quads, 1, tile))[0].astype(BF16)
        values_t.append(rows_of(quads, 2, tile).T)
        cosines += cosines_of(k_round, q_round)
    rounded = []
    for head in range(GROUP * PER_TILE):
        scale = scale_ref[step * GROUP * PER_TILE + head]
        halves = []
        for half in range(2):
            lanes = slice(128 * half, 128 * half + 128)
            bias = jnp.concatenate([bias_ref[head, 1 + half], bias_ref[head, half]], axis=0)
            scores = cosines[head][:, lanes] * scale + bias
            weights = jnp.exp2(scores - jnp.max(scores, axis=0, keepdims=True))
            probs = weights * (1.0 / jnp.sum(weights, axis=0, keepdims=True))
            probs_ref[head, :, lanes] = probs
            halves.append(probs.astype(BF16))
        rounded.append(jnp.concatenate(halves, axis=1))
    for head in range(GROUP * PER_TILE):
        value_t = values_t[head // PER_TILE][head_rows(head % PER_TILE)]
        attn_ref[head_rows(head), :] = mul(value_t, rounded[head]).astype(BF16)


def quad_spec():
    return pl.BlockSpec((3, QUAD, GROUP * TILE), lambda t: (0, 0, t))


def probs_spec():
    return pl.BlockSpec((GROUP * PER_TILE, TOKENS, TOKENS), lambda t: (t, 0, 0))


def forward(scales, quads, bias):
    return pl.pallas_call(
        forward_kernel,
        grid=(INNER // TILE // GROUP,),
        in_specs=[pl.BlockSpec(memory_space=pltpu.SMEM)]
        + [quad_spec()] * 4
        + [pl.BlockSpec((GROUP * PER_TILE, 3, 128, 128), lambda t: (t, 0, 0, 0))],
        out_specs=[pl.BlockSpec((GROUP * TILE, TOKENS), lambda t: (t, 0)), probs_spec()],
        out_shape=[
            jax.ShapeDtypeStruct((INNER, TOKENS), BF16),
            jax.ShapeDtypeStruct((HEADS, TOKENS, TOKENS), F32),
        ],
        compiler_params=params(),
        cost_estimate=cost(8e9, 16e6),
        name="forward",
    )(scales, *quads, bias)


def diagonal_sums(blocks):
    lane = iota((8, 128), 1)
    strips = []
    for block in blocks:
        total = jnp.zeros((8, 128), F32)
        first = jnp.zeros((8, 128), F32)
        for yj in range(16):
            start = 8 * (15 - yj)
            piece = block[8 * yj : 8 * yj + 8]
            if start:
                piece = pltpu.roll(piece, start, 1)
                first = first + jnp.where(lane >= start, piece, 0.0)
            else:
                first = first + piece
            total = total + piece
        strips.append(jnp.concatenate([first, total - first], axis=1))
    return strips


def offset_sums(strips):
    shape = strips[0].shape
    xj, lane = iota(shape, 0) % 8, iota(shape, 1)
    even = ((lane + xj) // 8) % 2 == 0
    sums = []
    for strip in strips:
        for bit in range(3):
            moved = pltpu.roll(strip, 256 - (1 << bit), 1)
            strip = jnp.where((xj // (1 << bit)) % 2 == 1, moved, strip)
        part = jnp.where(even, strip, 0.0)
        total = lambda v: jnp.sum(v.reshape(PER_TILE, 8, 256), axis=1)
        sums.append((pltpu.roll(total(part), 7, 1), pltpu.roll(total(strip - part), 255, 1)))
    inner = iota((PER_TILE, 256), 1) % 16
    result = []
    for parity in range(2):
        left, middle, right = (pair[parity] for pair in sums)
        result.append(left + jnp.where(inner >= 8, pltpu.roll(middle, 8, 1), 0.0))
        result.append(right + jnp.where(inner < 8, pltpu.roll(middle, 248, 1), 0.0))
    return result


def table_of(strips, log_sums):
    rows = offset_sums(strips)
    spot = iota((PER_TILE, 256), 1) == 240
    rows[2] = jnp.where(spot, jnp.concatenate(log_sums, axis=0), rows[2])
    shape = (32, 256)
    k, lane = iota(shape, 0), iota(shape, 1)
    mine, odd = lane // 16 == k // 2, k % 2 == 1
    total = jnp.zeros((PER_TILE * 32, TILE), F32)
    for half in range(2):
        picked = []
        for head in range(PER_TILE):
            both = jnp.where(odd, rows[2 + half][head : head + 1], rows[half][head : head + 1])
            picked.append(jnp.where(mine, both, 0.0).astype(BF16))
        source, goal = iota((256, TILE), 0), iota((256, TILE), 1)
        place = jnp.where(goal == 16 * half + source % 16, 1.0, 0.0).astype(BF16)
        total = total + mul(jnp.concatenate(picked, axis=0), place)
    table = total[:32]
    for head in range(1, PER_TILE):
        table = table + pltpu.roll(total[32 * head : 32 * head + 32], 32 * head, 1)
    return table


def backward_kernel(
    first_step,
    scale_ref,
    tl_ref,
    bl_ref,
    tr_ref,
    br_ref,
    grad_ref,
    probs_ref,
    *refs,
):
    gtl_ref, gbl_ref, gtr_ref, gbr_ref, table_ref = refs[-5:]
    step = pl.program_id(0) + first_step
    quads = (tl_ref, bl_ref, tr_ref, br_ref)
    heads = range(GROUP * PER_TILE)
    queries, keys, grads, grad_probs, cosines = [], [], [], [], []
    for tile in range(GROUP):
        queries.append(normalize(rows_of(quads, 0, tile)))
        keys.append(normalize(rows_of(quads, 1, tile)))
        grads.append(grad_ref[:, TILE * tile : TILE * tile + TILE])
        value, grad_t = rows_of(quads, 2, tile), grads[-1].T
        grad_probs += [mul(of_head(value, head), grad_t) for head in range(PER_TILE)]
        cosines += cosines_of(keys[-1][0].astype(BF16), queries[-1][0].astype(BF16))
    prob_rounds, grad_coss, blocks, log_sums = [], [], [], []
    for head in heads:
        scale = scale_ref[step * GROUP * PER_TILE + head]
        log_sum = jnp.zeros((1, 128), F32)
        halves, rounded, cos_grads = [], [], []
        for half in range(2):
            lanes = slice(128 * half, 128 * half + 128)
            probs = probs_ref[head, :, lanes]
            part = grad_probs[head][:, lanes]
            inner = jnp.sum(probs * part, axis=0, keepdims=True)
            score_grad = probs * (part - inner)
            halves.append(score_grad)
            log_sum = log_sum + jnp.sum(
                score_grad * cosines[head][:, lanes], axis=0, keepdims=True
            )
            rounded.append(probs.astype(BF16))
            cos_grads.append((score_grad * scale).astype(BF16))
        blocks.append((halves[0][128:], halves[0][:128] + halves[1][128:], halves[1][:128]))
        prob_rounds.append(jnp.concatenate(rounded, axis=1))
        grad_coss.append(jnp.concatenate(cos_grads, axis=1))
        log_sums.append(scale * jnp.sum(log_sum, axis=1, keepdims=True))
    for tile in range(GROUP):
        grad_v = jnp.zeros((TOKENS, TILE), F32)
        grad_k = jnp.zeros((TOKENS, TILE), F32)
        grad_q = []
        q_round, key_t = queries[tile][0].astype(BF16), keys[tile][0].astype(BF16).T
        for head in range(PER_TILE):
            grad_cos = grad_coss[PER_TILE * tile + head]
            grad_q.append(mul(key_t[head_rows(head)], grad_cos))
            grad_v = grad_v + mul(prob_rounds[PER_TILE * tile + head], of_head(grads[tile], head))
            grad_k = grad_k + mul(grad_cos, of_head(q_round, head))
        results = (
            normalize_back(*queries[tile], jnp.concatenate(grad_q, axis=0).T).astype(BF16),
            normalize_back(*keys[tile], grad_k).astype(BF16),
            grad_v.astype(BF16),
        )
        lanes = slice(TILE * tile, TILE * tile + TILE)
        for part, ref in enumerate((gtl_ref, gbl_ref, gtr_ref, gbr_ref)):
            for which, result in enumerate(results):
                ref[which, :, lanes] = result[QUAD * part : QUAD * part + QUAD]
    for tile in range(GROUP):
        mine = range(PER_TILE * tile, PER_TILE * tile + PER_TILE)
        found = [diagonal_sums(blocks[head]) for head in mine]
        strips = [jnp.concatenate([strip[d] for strip in found], axis=0) for d in range(3)]
        table_ref[tile] = table_of(strips, [log_sums[head] for head in mine]).astype(BF16)


def backward(scales, quads, grad_attn, probs, first, steps, earlier=()):
    quad = pl.BlockSpec((3, QUAD, GROUP * TILE), lambda t: (0, 0, t + first))
    return pl.pallas_call(
        functools.partial(backward_kernel, first),
        grid=(steps,),
        in_specs=[pl.BlockSpec(memory_space=pltpu.SMEM)]
        + [quad] * 4
        + [
            pl.BlockSpec((TOKENS, GROUP * TILE), lambda t: (0, t + first)),
            pl.BlockSpec((GROUP * PER_TILE, TOKENS, TOKENS), lambda t: (t + first, 0, 0)),
        ]
        + [pl.BlockSpec(memory_space=pl.ANY)] * len(earlier),
        out_specs=[quad] * 4 + [pl.BlockSpec((GROUP, 32, TILE), lambda t: (t + first, 0, 0))],
        out_shape=[jax.ShapeDtypeStruct((3, QUAD, INNER), BF16)] * 4
        + [jax.ShapeDtypeStruct((INNER // TILE, 32, TILE), BF16)],
        input_output_aliases={7 + i: i for i in range(len(earlier))},
        compiler_params=params(),
        cost_estimate=cost(8e9, 10e6),
        name="backward",
    )(scales, *quads, grad_attn, probs, *earlier)


def outer_kernel(place_ref, own_ref, other_ref, drop_ref, drop_other_ref, *refs):
    outs, left_ref = refs[:NX], refs[NX]
    goal, source = iota((64, TILE), 0), iota((64, TILE), 1)
    wanted = ((goal // 4) % NZ) * 16 + (goal // 32) * 8 + place_ref[3] * 4 + goal % 4
    pick = jnp.where(source == wanted, 1.0, 0.0).astype(BF16)
    for tile in range(INNER // TILE):
        rows, goals = slice(TILE * tile, TILE * tile + TILE), slice(64 * tile, 64 * tile + 64)
        left_ref[goals, :TOKENS] = mul(pick, own_ref[rows, :]).astype(BF16)
        left_ref[goals, TOKENS:] = mul(pick, other_ref[rows, :]).astype(BF16)
    for step, out in enumerate(outs):
        start = pl.multiple_of(((place_ref[0] + step) % NX) * 128, 128)
        left = left_ref[pl.ds(start, 128), :]
        for col in range(0, D, 512):
            part = mul(left[:, :TOKENS], drop_ref[:, col : col + 512])
            part = part + mul(left[:, TOKENS:], drop_other_ref[:, col : col + 512])
            out[:, col : col + 512] = part.astype(out.dtype)


def outer_terms(place, own, other, dropped, dropped_other):
    whole = pl.BlockSpec(memory_space=pltpu.VMEM)
    return pl.pallas_call(
        outer_kernel,
        in_specs=[pl.BlockSpec(memory_space=pltpu.SMEM)] + [whole] * 4,
        out_specs=[whole] * NX,
        out_shape=[jax.ShapeDtypeStruct((128, D), F32 if s == 0 else BF16) for s in range(NX)],
        scratch_shapes=[pltpu.VMEM((512, 2 * TOKENS), BF16)],
        compiler_params=params(),
        cost_estimate=cost(1.1e9, 6e6),
        name="outer_terms",
    )(place, own, other, dropped, dropped_other)


def sum_y_kernel(place_ref, *refs):
    terms, outs = refs[:4], refs[4:8]
    for step, out in enumerate(outs):
        y = (place_ref[1] + step) % 4
        start = pl.multiple_of(((y % 2) * 2 + y // 2) * 32, 32)
        rows = pl.ds(start, 32)
        total = terms[0][rows, :]
        for term in terms[1:]:
            total = total + term[rows, :].astype(F32)
        out[...] = total.astype(out.dtype)


def sum_for_y(place, terms):
    whole = pl.BlockSpec(memory_space=pltpu.VMEM)
    return pl.pallas_call(
        sum_y_kernel,
        in_specs=[pl.BlockSpec(memory_space=pltpu.SMEM)] + [whole] * 4,
        out_specs=[whole] * 4,
        out_shape=[jax.ShapeDtypeStruct((32, D), F32 if s == 0 else BF16) for s in range(4)],
        compiler_params=params(),
        name="sum_for_y",
    )(place, *terms)


def sum_z_kernel(*refs):
    terms, piece, out = refs[:4], refs[4], refs[5]
    total = terms[0][...]
    for term in terms[1:]:
        total = total + term[...].astype(F32)
    for z in range(NZ):
        out[z, :, :D] = total[4 * z : 4 * z + 4].astype(BF16)
        for part in range(8):
            lanes = slice(D + TILE * part, D + TILE * part + TILE)
            out[z, :, lanes] = piece[4 * part : 4 * part + 4].astype(BF16)


def sum_for_z(terms, piece):
    whole = pl.BlockSpec(memory_space=pltpu.VMEM)
    return pl.pallas_call(
        sum_z_kernel,
        in_specs=[whole] * 5,
        out_specs=whole,
        out_shape=jax.ShapeDtypeStruct((NZ, 4, D + 8 * TILE), BF16),
        compiler_params=params(),
        name="sum_for_z",
    )(*terms, piece)


def place_scalars():
    x, y, z, core = coordinates()
    return jnp.stack([x, y, z, core]).astype(jnp.int32)


def along_z_exchange(value):
    rest = NYH * NCORE
    groups = [[rest * z + one for z in range(NZ)] for one in range(rest)]
    return lax.all_to_all(value, "col", 0, 0, axis_index_groups=groups, tiled=True)


def table_pieces(part):
    return jnp.sum(along_z_exchange(part).astype(F32), axis=0)


def table_plane(piece):
    cols, rest = NZ * NYH * NCORE, NYH * NCORE
    groups = [
        [cols * row + rest * z + one for row in range(NX * NYL) for one in range(rest)]
        for z in range(NZ)
    ]
    same = jnp.broadcast_to(piece.astype(BF16), (len(groups[0]), 32, TILE))
    found = lax.all_to_all(
        same, ("row", "col"), 0, 0, axis_index_groups=groups, tiled=True
    )
    return jnp.sum(found.astype(F32), axis=0) / WINDOWS


def totals_kernel(found_ref, weight_ref, table_ref):
    total = found_ref[0, :, :D].astype(F32)
    for z in range(1, NZ):
        total = total + found_ref[z, :, :D].astype(F32)
    weight_ref[...] = total * (1.0 / WINDOWS)
    for tile in range(INNER // TILE):
        parts = [found_ref[tile, :, D + TILE * p : D + TILE * p + TILE] for p in range(8)]
        rows = jnp.concatenate([part.astype(F32) for part in parts], axis=0)
        for head in range(PER_TILE):
            place = rows[:, 32 * head : 32 * head + 32]
            table_ref[PER_TILE * tile + head] = place[:SIDE, :SIDE]


def totals(terms, piece):
    terms = [terms[0]] + [move(terms[s], along_y(s)) for s in range(1, 4)]
    found = along_z_exchange(sum_for_z(terms, piece))
    whole = pl.BlockSpec(memory_space=pltpu.VMEM)
    weight, table = pl.pallas_call(
        totals_kernel,
        in_specs=[whole],
        out_specs=[whole] * 2,
        out_shape=[
            jax.ShapeDtypeStruct((4, D), F32),
            jax.ShapeDtypeStruct((HEADS, SIDE, SIDE), F32),
        ],
        compiler_params=params(),
        name="totals",
    )(found)
    log_sum = found[:, 3, D + 7 * TILE :: 32].astype(F32)
    return weight, table, log_sum.reshape(HEADS)


def per_device(
    query_map, key_map, value_map, out_grad, keep_mask, log_scale, bias_table, proj_weight
):
    logit_scale = jnp.exp(log_scale)
    tl, tr, bl, br = split_maps(query_map, key_map, value_map)
    quads = (br, move_map(tr, -1, 0), move_map(bl, 0, -1), move_map(tl, -1, -1))
    bias = bias_blocks(bias_table)
    tl, tr, bl, br = split_dropped(out_grad, keep_mask)
    quads, tl, tr, bl = lax.optimization_barrier((quads, tl, tr, bl))
    up, left = move_map(tr, -1, 0), move_map(bl, 0, -1)
    attn_t, probs = forward(logit_scale * LOG2E, quads, bias)
    pieces = (br, up, left, move_map(tl, -1, -1))
    attn_t, pieces = lax.optimization_barrier((attn_t, pieces))
    dropped = jnp.concatenate(pieces, axis=0)
    other, dropped_other = move(attn_t, other_core), move(dropped, other_core)
    grad_attn = lax.dot_general(
        dropped, proj_weight, (((1,), (1,)), ((), ())), preferred_element_type=F32
    ).astype(BF16)
    found = backward(logit_scale, quads, grad_attn, probs, 0, EARLY)
    found, other, dropped_other = lax.optimization_barrier((found, other, dropped_other))
    place = place_scalars()
    terms = outer_terms(place, attn_t, other, dropped, dropped_other)
    terms, found = lax.optimization_barrier((terms, found))
    g_tl, g_bl, g_tr, g_br, table_part = backward(
        logit_scale, quads, grad_attn, probs, EARLY, INNER // TILE // GROUP - EARLY, found
    )
    arrived = (move_map(g_br, 1, 1), move_map(g_bl, 1, 0), move_map(g_tr, 0, 1))
    near = [move(terms[s], along_x(s)) for s in (1, 3)]
    near, across, table_part = lax.optimization_barrier((near, terms[2], table_part))
    across = move(across, along_x(2))
    piece = table_plane(table_pieces(table_part))
    across, arrived, piece = lax.optimization_barrier((across, arrived, piece))
    terms = sum_for_y(place, (terms[0], near[0], across, near[1]))
    grads = join_maps(*arrived, g_tl)
    weight_grad, table_grad, log_grad = totals(terms, piece)
    return (*grads, weight_grad, table_grad, log_grad)


def solution(mesh):
    return jax.shard_map(
        per_device,
        mesh=mesh,
        in_specs=(
            P("row", "col", None),
            P("row", "col", None),
            P("row", "col", None),
            P("row", "col", None),
            P("row", "col", None),
            P(),
            P(),
            P(),
        ),
        out_specs=(
            P("row", "col", None),
            P("row", "col", None),
            P("row", "col", None),
            P(("row", "col"), None),
            P(),
            P(),
        ),
        check_vma=False,
    )
```

```python
import functools

import jax
import jax.numpy as jnp
import numpy as np
from jax import lax
from jax.experimental import pallas as pl
from jax.experimental.pallas import tpu as pltpu
from jax.sharding import PartitionSpec as P

D = 2048
HEADS = 32
HEAD_DIM = 32
INNER = 1024
WINDOWS = 256
KEEP_RATE = 0.9
SIDE = 31
LOG2E = 1.4426950408889634

NX, NYL, NZ, NYH, NCORE = 4, 2, 8, 2, 2

F32 = jnp.float32
BF16 = jnp.bfloat16
TILE = 128
PER_TILE = TILE // HEAD_DIM
GROUP = 2
BIAS_HEADS = 8
EARLY = 2
QUAD = 64
TOKENS = 256

VMEM_BYTES = 48 * 1024 * 1024


def params(vmem=VMEM_BYTES):
    return pltpu.CompilerParams(vmem_limit_bytes=vmem)


def cost(flops, nbytes):
    return pl.CostEstimate(flops=int(flops), bytes_accessed=int(nbytes), transcendentals=0)


def move(value, target):
    sizes = (NX, NYL, NZ, NYH, NCORE)
    pairs = []
    for src in range(NX * NYL * NZ * NYH * NCORE):
        place = np.unravel_index(src, sizes)
        goal = [int(g) % s for g, s in zip(target(*[int(p) for p in place]), sizes)]
        pairs.append((src, int(np.ravel_multi_index(goal, sizes))))
    return lax.ppermute(value, ("row", "col"), pairs)


def move_map(value, d_row, d_col):
    rows, cols = NX * NYL, NZ * NYH * NCORE
    pairs = [
        (r * cols + c, ((r + d_row) % rows) * cols + (c + d_col) % cols)
        for r in range(rows)
        for c in range(cols)
    ]
    return lax.ppermute(value, ("row", "col"), pairs)


def along_x(step):
    return lambda x, yl, z, yh, c: (x + step, yl, z, yh, c)


def along_y(step):
    def goal(x, yl, z, yh, c):
        y = (2 * yh + yl + step) % 4
        return (x, y % 2, z, y // 2, c)

    return goal


def along_z(step):
    return lambda x, yl, z, yh, c: (x, yl, z + step, yh, c)


def other_core(x, yl, z, yh, c):
    return (x, yl, z, yh, 1 - c)


def coordinates():
    row = lax.axis_index("row")
    col = lax.axis_index("col")
    x, y_lo = row // 2, row % 2
    z, y_hi, core = col // 4, (col // 2) % 2, col % 2
    return x, 2 * y_hi + y_lo, z, core


def quarters_of(block):
    n = block.shape[-1]
    cut = lambda a, b: block[a : a + 8, b : b + 8, :].reshape(QUAD, n).astype(BF16)
    return cut(0, 0), cut(0, 8), cut(8, 0), cut(8, 8)


def split_kernel(q_ref, k_ref, v_ref, tl_ref, tr_ref, bl_ref, br_ref):
    for which, ref in enumerate((q_ref, k_ref, v_ref)):
        for out, part in zip((tl_ref, tr_ref, bl_ref, br_ref), quarters_of(ref[...].astype(F32))):
            out[which] = part


def split_maps(query_map, key_map, value_map):
    spec = pl.BlockSpec((16, 16, 256), lambda t: (0, 0, t))
    out = pl.BlockSpec((3, QUAD, 256), lambda t: (0, 0, t))
    return pl.pallas_call(
        split_kernel,
        grid=(INNER // 256,),
        in_specs=[spec] * 3,
        out_specs=[out] * 4,
        out_shape=[jax.ShapeDtypeStruct((3, QUAD, INNER), BF16)] * 4,
        compiler_params=params(60 * 1024 * 1024),
        name="split_maps",
    )(query_map, key_map, value_map)


def drop_kernel(grad_ref, keep_ref, tl_ref, tr_ref, bl_ref, br_ref):
    dropped = grad_ref[...].astype(F32) * keep_ref[...].astype(F32) * (1.0 / KEEP_RATE)
    for out, part in zip((tl_ref, tr_ref, bl_ref, br_ref), quarters_of(dropped)):
        out[...] = part


def split_dropped(out_grad, keep_mask):
    spec = pl.BlockSpec((16, 16, 512), lambda t: (0, 0, t))
    out = pl.BlockSpec((QUAD, 512), lambda t: (0, t))
    return pl.pallas_call(
        drop_kernel,
        grid=(D // 512,),
        in_specs=[spec] * 2,
        out_specs=[out] * 4,
        out_shape=[jax.ShapeDtypeStruct((QUAD, D), BF16)] * 4,
        compiler_params=params(60 * 1024 * 1024),
        name="split_dropped",
    )(out_grad, keep_mask)


def join_kernel(tl_ref, tr_ref, bl_ref, br_ref, *outs):
    for which, out in enumerate(outs):
        part = lambda ref: ref[which].astype(F32).reshape(8, 8, ref.shape[-1])
        out[:8] = jnp.concatenate([part(tl_ref), part(tr_ref)], axis=1).astype(BF16)
        out[8:] = jnp.concatenate([part(bl_ref), part(br_ref)], axis=1).astype(BF16)


def join_maps(tl, tr, bl, br):
    spec = pl.BlockSpec((3, QUAD, 256), lambda t: (0, 0, t))
    out = pl.BlockSpec((16, 16, 256), lambda t: (0, 0, t))
    return pl.pallas_call(
        join_kernel,
        grid=(INNER // 256,),
        in_specs=[spec] * 4,
        out_specs=[out] * 3,
        out_shape=[jax.ShapeDtypeStruct((16, 16, INNER), BF16)] * 3,
        compiler_params=params(),
        name="join_maps",
    )(tl, tr, bl, br)


def bias_kernel(table_ref, out_ref):
    lane = iota((BIAS_HEADS, 8, 256), 2)
    turn = jnp.where(iota((SIDE, 32), 0) + iota((SIDE, 32), 1) == 30, LOG2E, 0.0)
    spread = jnp.where(iota((SIDE, 256), 1) // 8 == iota((SIDE, 256), 0), 1.0, 0.0)
    exact = dict(precision=lax.Precision.HIGHEST, preferred_element_type=F32)
    turned = [jnp.dot(table_ref[head], turn, **exact) for head in range(BIAS_HEADS)]
    wide = jnp.stack(
        [lax.dot_general(rows, spread, (((0,), (0,)), ((), ())), **exact) for rows in turned]
    )
    for d in range(3):
        strip = jnp.zeros((BIAS_HEADS, 8, 256), F32)
        for xi in range(8):
            first = 23 - 8 * d - xi
            strip = jnp.where(lane % 8 == xi, wide[:, first : first + 8, :], strip)
        strip = strip.reshape(BIAS_HEADS * 8, 256)
        for yj in range(16):
            start = 8 * (15 - yj)
            moved = strip if start == 0 else pltpu.roll(strip, 256 - start, 1)
            out_ref[:, d, 8 * yj : 8 * yj + 8, :] = moved[:, :128].reshape(BIAS_HEADS, 8, 128)


def bias_blocks(bias_table):
    return pl.pallas_call(
        bias_kernel,
        grid=(HEADS // BIAS_HEADS,),
        in_specs=[pl.BlockSpec((BIAS_HEADS, SIDE, SIDE), lambda t: (t, 0, 0))],
        out_specs=pl.BlockSpec((BIAS_HEADS, 3, 128, 128), lambda t: (t, 0, 0, 0)),
        out_shape=jax.ShapeDtypeStruct((HEADS, 3, 128, 128), F32),
        compiler_params=params(),
        cost_estimate=cost(1e7, 8e6),
        name="bias_blocks",
    )(bias_table)


def iota(shape, dim):
    return lax.broadcasted_iota(jnp.int32, shape, dim)


def per_head_sum(value):
    high = value.astype(BF16)
    low = (value - high.astype(F32)).astype(BF16)
    shape = (2 * TILE, TILE)
    same = (iota(shape, 0) % TILE) // HEAD_DIM == iota(shape, 1) // HEAD_DIM
    ones = jnp.where(same, 1.0, 0.0).astype(BF16)
    both = jnp.concatenate([high, low], axis=1)
    return jnp.dot(both, ones, preferred_element_type=F32)


def normalize(rows):
    value = rows.astype(F32)
    length = jnp.sqrt(per_head_sum(value * value))
    inverse = 1.0 / jnp.maximum(length, 1.0)
    return value * inverse, length, inverse


def normalize_back(unit, length, inverse, grad):
    projection = per_head_sum(unit * grad)
    return jnp.where(length > 1.0, (grad - unit * projection) * inverse, grad)


def of_head(rows, head):
    keep = iota(rows.shape, 1) // HEAD_DIM == head
    return jnp.where(keep, rows, jnp.zeros_like(rows))


def rows_of(refs, which, tile):
    lanes = slice(TILE * tile, TILE * tile + TILE)
    return jnp.concatenate([ref[which, :, lanes] for ref in refs], axis=0)


def mul(left, right):
    return jnp.dot(left, right, preferred_element_type=F32)


def head_rows(head):
    return slice(HEAD_DIM * head, HEAD_DIM * head + HEAD_DIM)


def cosines_of(k_round, q_round):
    q_t = q_round.T
    return [mul(of_head(k_round, head), q_t) for head in range(PER_TILE)]


def forward_kernel(scale_ref, tl_ref, bl_ref, tr_ref, br_ref, bias_ref, attn_ref, probs_ref):
    step = pl.program_id(0)
    quads = (tl_ref, bl_ref, tr_ref, br_ref)
    cosines, values_t = [], []
    for tile in range(GROUP):
        q_round = normalize(rows_of(quads, 0, tile))[0].astype(BF16)
        k_round = normalize(rows_of(quads, 1, tile))[0].astype(BF16)
        values_t.append(rows_of(quads, 2, tile).T)
        cosines += cosines_of(k_round, q_round)
    rounded = []
    for head in range(GROUP * PER_TILE):
        scale = scale_ref[step * GROUP * PER_TILE + head]
        halves = []
        for half in range(2):
            lanes = slice(128 * half, 128 * half + 128)
            bias = jnp.concatenate([bias_ref[head, 1 + half], bias_ref[head, half]], axis=0)
            scores = cosines[head][:, lanes] * scale + bias
            weights = jnp.exp2(scores - jnp.max(scores, axis=0, keepdims=True))
            probs = weights * (1.0 / jnp.sum(weights, axis=0, keepdims=True))
            probs_ref[head, :, lanes] = probs
            halves.append(probs.astype(BF16))
        rounded.append(jnp.concatenate(halves, axis=1))
    for head in range(GROUP * PER_TILE):
        value_t = values_t[head // PER_TILE][head_rows(head % PER_TILE)]
        attn_ref[head_rows(head), :] = mul(value_t, rounded[head]).astype(BF16)


def quad_spec():
    return pl.BlockSpec((3, QUAD, GROUP * TILE), lambda t: (0, 0, t))


def probs_spec():
    return pl.BlockSpec((GROUP * PER_TILE, TOKENS, TOKENS), lambda t: (t, 0, 0))


def forward(scales, quads, bias):
    return pl.pallas_call(
        forward_kernel,
        grid=(INNER // TILE // GROUP,),
        in_specs=[pl.BlockSpec(memory_space=pltpu.SMEM)]
        + [quad_spec()] * 4
        + [pl.BlockSpec((GROUP * PER_TILE, 3, 128, 128), lambda t: (t, 0, 0, 0))],
        out_specs=[pl.BlockSpec((GROUP * TILE, TOKENS), lambda t: (t, 0)), probs_spec()],
        out_shape=[
            jax.ShapeDtypeStruct((INNER, TOKENS), BF16),
            jax.ShapeDtypeStruct((HEADS, TOKENS, TOKENS), F32),
        ],
        compiler_params=params(),
        cost_estimate=cost(8e9, 16e6),
        name="forward",
    )(scales, *quads, bias)


def diagonal_sums(blocks):
    lane = iota((8, 128), 1)
    strips = []
    for block in blocks:
        total = jnp.zeros((8, 128), F32)
        first = jnp.zeros((8, 128), F32)
        for yj in range(16):
            start = 8 * (15 - yj)
            piece = block[8 * yj : 8 * yj + 8]
            if start:
                piece = pltpu.roll(piece, start, 1)
                first = first + jnp.where(lane >= start, piece, 0.0)
            else:
                first = first + piece
            total = total + piece
        strips.append(jnp.concatenate([first, total - first], axis=1))
    return strips


def offset_sums(strips):
    shape = strips[0].shape
    xj, lane = iota(shape, 0) % 8, iota(shape, 1)
    even = ((lane + xj) // 8) % 2 == 0
    sums = []
    for strip in strips:
        for bit in range(3):
            moved = pltpu.roll(strip, 256 - (1 << bit), 1)
            strip = jnp.where((xj // (1 << bit)) % 2 == 1, moved, strip)
        part = jnp.where(even, strip, 0.0)
        total = lambda v: jnp.sum(v.reshape(PER_TILE, 8, 256), axis=1)
        sums.append((pltpu.roll(total(part), 7, 1), pltpu.roll(total(strip - part), 255, 1)))
    inner = iota((PER_TILE, 256), 1) % 16
    result = []
    for parity in range(2):
        left, middle, right = (pair[parity] for pair in sums)
        result.append(left + jnp.where(inner >= 8, pltpu.roll(middle, 8, 1), 0.0))
        result.append(right + jnp.where(inner < 8, pltpu.roll(middle, 248, 1), 0.0))
    return result


def table_of(strips, log_sums):
    rows = offset_sums(strips)
    spot = iota((PER_TILE, 256), 1) == 240
    rows[2] = jnp.where(spot, jnp.concatenate(log_sums, axis=0), rows[2])
    shape = (32, 256)
    k, lane = iota(shape, 0), iota(shape, 1)
    mine, odd = lane // 16 == k // 2, k % 2 == 1
    total = jnp.zeros((PER_TILE * 32, TILE), F32)
    for half in range(2):
        picked = []
        for head in range(PER_TILE):
            both = jnp.where(odd, rows[2 + half][head : head + 1], rows[half][head : head + 1])
            picked.append(jnp.where(mine, both, 0.0).astype(BF16))
        source, goal = iota((256, TILE), 0), iota((256, TILE), 1)
        place = jnp.where(goal == 16 * half + source % 16, 1.0, 0.0).astype(BF16)
        total = total + mul(jnp.concatenate(picked, axis=0), place)
    table = total[:32]
    for head in range(1, PER_TILE):
        table = table + pltpu.roll(total[32 * head : 32 * head + 32], 32 * head, 1)
    return table


def backward_kernel(
    first_step,
    scale_ref,
    tl_ref,
    bl_ref,
    tr_ref,
    br_ref,
    grad_ref,
    probs_ref,
    *refs,
):
    gtl_ref, gbl_ref, gtr_ref, gbr_ref, table_ref = refs[-5:]
    step = pl.program_id(0) + first_step
    quads = (tl_ref, bl_ref, tr_ref, br_ref)
    heads = range(GROUP * PER_TILE)
    queries, keys, grads, grad_probs, cosines = [], [], [], [], []
    for tile in range(GROUP):
        queries.append(normalize(rows_of(quads, 0, tile)))
        keys.append(normalize(rows_of(quads, 1, tile)))
        grads.append(grad_ref[:, TILE * tile : TILE * tile + TILE])
        value, grad_t = rows_of(quads, 2, tile), grads[-1].T
        grad_probs += [mul(of_head(value, head), grad_t) for head in range(PER_TILE)]
        cosines += cosines_of(keys[-1][0].astype(BF16), queries[-1][0].astype(BF16))
    prob_rounds, grad_coss, blocks, log_sums = [], [], [], []
    for head in heads:
        scale = scale_ref[step * GROUP * PER_TILE + head]
        log_sum = jnp.zeros((1, 128), F32)
        halves, rounded, cos_grads = [], [], []
        for half in range(2):
            lanes = slice(128 * half, 128 * half + 128)
            probs = probs_ref[head, :, lanes]
            part = grad_probs[head][:, lanes]
            inner = jnp.sum(probs * part, axis=0, keepdims=True)
            score_grad = probs * (part - inner)
            halves.append(score_grad)
            log_sum = log_sum + jnp.sum(
                score_grad * cosines[head][:, lanes], axis=0, keepdims=True
            )
            rounded.append(probs.astype(BF16))
            cos_grads.append((score_grad * scale).astype(BF16))
        blocks.append((halves[0][128:], halves[0][:128] + halves[1][128:], halves[1][:128]))
        prob_rounds.append(jnp.concatenate(rounded, axis=1))
        grad_coss.append(jnp.concatenate(cos_grads, axis=1))
        log_sums.append(scale * jnp.sum(log_sum, axis=1, keepdims=True))
    for tile in range(GROUP):
        grad_v = jnp.zeros((TOKENS, TILE), F32)
        grad_k = jnp.zeros((TOKENS, TILE), F32)
        grad_q = []
        q_round, key_t = queries[tile][0].astype(BF16), keys[tile][0].astype(BF16).T
        for head in range(PER_TILE):
            grad_cos = grad_coss[PER_TILE * tile + head]
            grad_q.append(mul(key_t[head_rows(head)], grad_cos))
            grad_v = grad_v + mul(prob_rounds[PER_TILE * tile + head], of_head(grads[tile], head))
            grad_k = grad_k + mul(grad_cos, of_head(q_round, head))
        results = (
            normalize_back(*queries[tile], jnp.concatenate(grad_q, axis=0).T).astype(BF16),
            normalize_back(*keys[tile], grad_k).astype(BF16),
            grad_v.astype(BF16),
        )
        lanes = slice(TILE * tile, TILE * tile + TILE)
        for part, ref in enumerate((gtl_ref, gbl_ref, gtr_ref, gbr_ref)):
            for which, result in enumerate(results):
                ref[which, :, lanes] = result[QUAD * part : QUAD * part + QUAD]
    for tile in range(GROUP):
        mine = range(PER_TILE * tile, PER_TILE * tile + PER_TILE)
        found = [diagonal_sums(blocks[head]) for head in mine]
        strips = [jnp.concatenate([strip[d] for strip in found], axis=0) for d in range(3)]
        table_ref[tile] = table_of(strips, [log_sums[head] for head in mine]).astype(BF16)


def backward(scales, quads, grad_attn, probs, first, steps, earlier=()):
    quad = pl.BlockSpec((3, QUAD, GROUP * TILE), lambda t: (0, 0, t + first))
    return pl.pallas_call(
        functools.partial(backward_kernel, first),
        grid=(steps,),
        in_specs=[pl.BlockSpec(memory_space=pltpu.SMEM)]
        + [quad] * 4
        + [
            pl.BlockSpec((TOKENS, GROUP * TILE), lambda t: (0, t + first)),
            pl.BlockSpec((GROUP * PER_TILE, TOKENS, TOKENS), lambda t: (t + first, 0, 0)),
        ]
        + [pl.BlockSpec(memory_space=pl.ANY)] * len(earlier),
        out_specs=[quad] * 4 + [pl.BlockSpec((GROUP, 32, TILE), lambda t: (t + first, 0, 0))],
        out_shape=[jax.ShapeDtypeStruct((3, QUAD, INNER), BF16)] * 4
        + [jax.ShapeDtypeStruct((INNER // TILE, 32, TILE), BF16)],
        input_output_aliases={7 + i: i for i in range(len(earlier))},
        compiler_params=params(),
        cost_estimate=cost(8e9, 10e6),
        name="backward",
    )(scales, *quads, grad_attn, probs, *earlier)


def outer_kernel(place_ref, own_ref, other_ref, drop_ref, drop_other_ref, *refs):
    outs, left_ref = refs[:NX], refs[NX]
    goal, source = iota((64, TILE), 0), iota((64, TILE), 1)
    wanted = ((goal // 4) % NZ) * 16 + (goal // 32) * 8 + place_ref[3] * 4 + goal % 4
    pick = jnp.where(source == wanted, 1.0, 0.0).astype(BF16)
    for tile in range(INNER // TILE):
        rows, goals = slice(TILE * tile, TILE * tile + TILE), slice(64 * tile, 64 * tile + 64)
        left_ref[goals, :TOKENS] = mul(pick, own_ref[rows, :]).astype(BF16)
        left_ref[goals, TOKENS:] = mul(pick, other_ref[rows, :]).astype(BF16)
    for step, out in enumerate(outs):
        start = pl.multiple_of(((place_ref[0] + step) % NX) * 128, 128)
        left = left_ref[pl.ds(start, 128), :]
        for col in range(0, D, 512):
            part = mul(left[:, :TOKENS], drop_ref[:, col : col + 512])
            part = part + mul(left[:, TOKENS:], drop_other_ref[:, col : col + 512])
            out[:, col : col + 512] = part.astype(out.dtype)


def outer_terms(place, own, other, dropped, dropped_other):
    whole = pl.BlockSpec(memory_space=pltpu.VMEM)
    return pl.pallas_call(
        outer_kernel,
        in_specs=[pl.BlockSpec(memory_space=pltpu.SMEM)] + [whole] * 4,
        out_specs=[whole] * NX,
        out_shape=[jax.ShapeDtypeStruct((128, D), F32 if s == 0 else BF16) for s in range(NX)],
        scratch_shapes=[pltpu.VMEM((512, 2 * TOKENS), BF16)],
        compiler_params=params(),
        cost_estimate=cost(1.1e9, 6e6),
        name="outer_terms",
    )(place, own, other, dropped, dropped_other)


def sum_y_kernel(place_ref, *refs):
    terms, outs = refs[:4], refs[4:8]
    for step, out in enumerate(outs):
        y = (place_ref[1] + step) % 4
        start = pl.multiple_of(((y % 2) * 2 + y // 2) * 32, 32)
        rows = pl.ds(start, 32)
        total = terms[0][rows, :]
        for term in terms[1:]:
            total = total + term[rows, :].astype(F32)
        out[...] = total.astype(out.dtype)


def sum_for_y(place, terms):
    whole = pl.BlockSpec(memory_space=pltpu.VMEM)
    return pl.pallas_call(
        sum_y_kernel,
        in_specs=[pl.BlockSpec(memory_space=pltpu.SMEM)] + [whole] * 4,
        out_specs=[whole] * 4,
        out_shape=[jax.ShapeDtypeStruct((32, D), F32 if s == 0 else BF16) for s in range(4)],
        compiler_params=params(),
        name="sum_for_y",
    )(place, *terms)


def sum_z_kernel(*refs):
    terms, piece, out = refs[:4], refs[4], refs[5]
    total = terms[0][...]
    for term in terms[1:]:
        total = total + term[...].astype(F32)
    for z in range(NZ):
        out[z, :, :D] = total[4 * z : 4 * z + 4].astype(BF16)
        for part in range(8):
            lanes = slice(D + TILE * part, D + TILE * part + TILE)
            out[z, :, lanes] = piece[4 * part : 4 * part + 4].astype(BF16)


def sum_for_z(terms, piece):
    whole = pl.BlockSpec(memory_space=pltpu.VMEM)
    return pl.pallas_call(
        sum_z_kernel,
        in_specs=[whole] * 5,
        out_specs=whole,
        out_shape=jax.ShapeDtypeStruct((NZ, 4, D + 8 * TILE), BF16),
        compiler_params=params(),
        name="sum_for_z",
    )(*terms, piece)


def place_scalars():
    x, y, z, core = coordinates()
    return jnp.stack([x, y, z, core]).astype(jnp.int32)


def along_z_exchange(value):
    rest = NYH * NCORE
    groups = [[rest * z + one for z in range(NZ)] for one in range(rest)]
    return lax.all_to_all(value, "col", 0, 0, axis_index_groups=groups, tiled=True)


def table_pieces(part):
    return jnp.sum(along_z_exchange(part).astype(F32), axis=0)


def table_plane(piece):
    cols, rest = NZ * NYH * NCORE, NYH * NCORE
    groups = [
        [cols * row + rest * z + one for row in range(NX * NYL) for one in range(rest)]
        for z in range(NZ)
    ]
    same = jnp.broadcast_to(piece.astype(BF16), (len(groups[0]), 32, TILE))
    found = lax.all_to_all(
        same, ("row", "col"), 0, 0, axis_index_groups=groups, tiled=True
    )
    return jnp.sum(found.astype(F32), axis=0) / WINDOWS


def totals_kernel(found_ref, weight_ref, table_ref):
    total = found_ref[0, :, :D].astype(F32)
    for z in range(1, NZ):
        total = total + found_ref[z, :, :D].astype(F32)
    weight_ref[...] = total * (1.0 / WINDOWS)
    for tile in range(INNER // TILE):
        parts = [found_ref[tile, :, D + TILE * p : D + TILE * p + TILE] for p in range(8)]
        rows = jnp.concatenate([part.astype(F32) for part in parts], axis=0)
        for head in range(PER_TILE):
            place = rows[:, 32 * head : 32 * head + 32]
            table_ref[PER_TILE * tile + head] = place[:SIDE, :SIDE]


def totals(terms, piece):
    terms = [terms[0]] + [move(terms[s], along_y(s)) for s in range(1, 4)]
    found = along_z_exchange(sum_for_z(terms, piece))
    whole = pl.BlockSpec(memory_space=pltpu.VMEM)
    weight, table = pl.pallas_call(
        totals_kernel,
        in_specs=[whole],
        out_specs=[whole] * 2,
        out_shape=[
            jax.ShapeDtypeStruct((4, D), F32),
            jax.ShapeDtypeStruct((HEADS, SIDE, SIDE), F32),
        ],
        compiler_params=params(),
        name="totals",
    )(found)
    log_sum = found[:, 3, D + 7 * TILE :: 32].astype(F32)
    return weight, table, log_sum.reshape(HEADS)


def per_device(
    query_map, key_map, value_map, out_grad, keep_mask, log_scale, bias_table, proj_weight
):
    logit_scale = jnp.exp(log_scale)
    tl, tr, bl, br = split_maps(query_map, key_map, value_map)
    quads = (br, move_map(tr, -1, 0), move_map(bl, 0, -1), move_map(tl, -1, -1))
    bias = bias_blocks(bias_table)
    tl, tr, bl, br = split_dropped(out_grad, keep_mask)
    quads, tl, tr, bl = lax.optimization_barrier((quads, tl, tr, bl))
    up, left = move_map(tr, -1, 0), move_map(bl, 0, -1)
    attn_t, probs = forward(logit_scale * LOG2E, quads, bias)
    pieces = (br, up, left, move_map(tl, -1, -1))
    attn_t, pieces = lax.optimization_barrier((attn_t, pieces))
    dropped = jnp.concatenate(pieces, axis=0)
    other, dropped_other = move(attn_t, other_core), move(dropped, other_core)
    grad_attn = lax.dot_general(
        dropped, proj_weight, (((1,), (1,)), ((), ())), preferred_element_type=F32
    ).astype(BF16)
    found = backward(logit_scale, quads, grad_attn, probs, 0, EARLY)
    found, other, dropped_other = lax.optimization_barrier((found, other, dropped_other))
    place = place_scalars()
    terms = outer_terms(place, attn_t, other, dropped, dropped_other)
    terms, found = lax.optimization_barrier((terms, found))
    g_tl, g_bl, g_tr, g_br, table_part = backward(
        logit_scale, quads, grad_attn, probs, EARLY, INNER // TILE // GROUP - EARLY, found
    )
    arrived = (move_map(g_br, 1, 1), move_map(g_bl, 1, 0), move_map(g_tr, 0, 1))
    near = [move(terms[s], along_x(s)) for s in (1, 3)]
    near, across, table_part = lax.optimization_barrier((near, terms[2], table_part))
    across = move(across, along_x(2))
    piece = table_pieces(table_part)
    across, arrived = lax.optimization_barrier((across, arrived))
    terms = sum_for_y(place, (terms[0], near[0], across, near[1]))
    terms, piece = lax.optimization_barrier((terms, piece))
    piece = table_plane(piece)
    grads = join_maps(*arrived, g_tl)
    weight_grad, table_grad, log_grad = totals(terms, piece)
    return (*grads, weight_grad, table_grad, log_grad)


def solution(mesh):
    return jax.shard_map(
        per_device,
        mesh=mesh,
        in_specs=(
            P("row", "col", None),
            P("row", "col", None),
            P("row", "col", None),
            P("row", "col", None),
            P("row", "col", None),
            P(),
            P(),
            P(),
        ),
        out_specs=(
            P("row", "col", None),
            P("row", "col", None),
            P("row", "col", None),
            P(("row", "col"), None),
            P(),
            P(),
        ),
        check_vma=False,
    )
```

```python
import functools

import jax
import jax.numpy as jnp
import numpy as np
from jax import lax
from jax.experimental import pallas as pl
from jax.experimental.pallas import tpu as pltpu
from jax.sharding import PartitionSpec as P

D = 2048
HEADS = 32
HEAD_DIM = 32
INNER = 1024
WINDOWS = 256
KEEP_RATE = 0.9
SIDE = 31
LOG2E = 1.4426950408889634

NX, NYL, NZ, NYH, NCORE = 4, 2, 8, 2, 2

F32 = jnp.float32
BF16 = jnp.bfloat16
TILE = 128
PER_TILE = TILE // HEAD_DIM
GROUP = 2
BIAS_HEADS = 8
EARLY = 2
QUAD = 64
TOKENS = 256

VMEM_BYTES = 48 * 1024 * 1024


def params(vmem=VMEM_BYTES):
    return pltpu.CompilerParams(vmem_limit_bytes=vmem)


def cost(flops, nbytes):
    return pl.CostEstimate(flops=int(flops), bytes_accessed=int(nbytes), transcendentals=0)


def move(value, target):
    sizes = (NX, NYL, NZ, NYH, NCORE)
    pairs = []
    for src in range(NX * NYL * NZ * NYH * NCORE):
        place = np.unravel_index(src, sizes)
        goal = [int(g) % s for g, s in zip(target(*[int(p) for p in place]), sizes)]
        pairs.append((src, int(np.ravel_multi_index(goal, sizes))))
    return lax.ppermute(value, ("row", "col"), pairs)


def move_map(value, d_row, d_col):
    rows, cols = NX * NYL, NZ * NYH * NCORE
    pairs = [
        (r * cols + c, ((r + d_row) % rows) * cols + (c + d_col) % cols)
        for r in range(rows)
        for c in range(cols)
    ]
    return lax.ppermute(value, ("row", "col"), pairs)


def along_x(step):
    return lambda x, yl, z, yh, c: (x + step, yl, z, yh, c)


def along_y(step):
    def goal(x, yl, z, yh, c):
        y = (2 * yh + yl + step) % 4
        return (x, y % 2, z, y // 2, c)

    return goal


def along_z(step):
    return lambda x, yl, z, yh, c: (x, yl, z + step, yh, c)


def other_core(x, yl, z, yh, c):
    return (x, yl, z, yh, 1 - c)


def coordinates():
    row = lax.axis_index("row")
    col = lax.axis_index("col")
    x, y_lo = row // 2, row % 2
    z, y_hi, core = col // 4, (col // 2) % 2, col % 2
    return x, 2 * y_hi + y_lo, z, core


def quarters_of(block):
    n = block.shape[-1]
    cut = lambda a, b: block[a : a + 8, b : b + 8, :].reshape(QUAD, n).astype(BF16)
    return cut(0, 0), cut(0, 8), cut(8, 0), cut(8, 8)


def split_kernel(q_ref, k_ref, v_ref, tl_ref, tr_ref, bl_ref, br_ref):
    for which, ref in enumerate((q_ref, k_ref, v_ref)):
        for out, part in zip((tl_ref, tr_ref, bl_ref, br_ref), quarters_of(ref[...].astype(F32))):
            out[which] = part


def split_maps(query_map, key_map, value_map):
    spec = pl.BlockSpec((16, 16, 256), lambda t: (0, 0, t))
    out = pl.BlockSpec((3, QUAD, 256), lambda t: (0, 0, t))
    return pl.pallas_call(
        split_kernel,
        grid=(INNER // 256,),
        in_specs=[spec] * 3,
        out_specs=[out] * 4,
        out_shape=[jax.ShapeDtypeStruct((3, QUAD, INNER), BF16)] * 4,
        compiler_params=params(60 * 1024 * 1024),
        name="split_maps",
    )(query_map, key_map, value_map)


def drop_kernel(grad_ref, keep_ref, tl_ref, tr_ref, bl_ref, br_ref):
    dropped = grad_ref[...].astype(F32) * keep_ref[...].astype(F32) * (1.0 / KEEP_RATE)
    for out, part in zip((tl_ref, tr_ref, bl_ref, br_ref), quarters_of(dropped)):
        out[...] = part


def split_dropped(out_grad, keep_mask):
    spec = pl.BlockSpec((16, 16, 512), lambda t: (0, 0, t))
    out = pl.BlockSpec((QUAD, 512), lambda t: (0, t))
    return pl.pallas_call(
        drop_kernel,
        grid=(D // 512,),
        in_specs=[spec] * 2,
        out_specs=[out] * 4,
        out_shape=[jax.ShapeDtypeStruct((QUAD, D), BF16)] * 4,
        compiler_params=params(60 * 1024 * 1024),
        name="split_dropped",
    )(out_grad, keep_mask)


def join_kernel(tl_ref, tr_ref, bl_ref, br_ref, *outs):
    for which, out in enumerate(outs):
        part = lambda ref: ref[which].astype(F32).reshape(8, 8, ref.shape[-1])
        out[:8] = jnp.concatenate([part(tl_ref), part(tr_ref)], axis=1).astype(BF16)
        out[8:] = jnp.concatenate([part(bl_ref), part(br_ref)], axis=1).astype(BF16)


def join_maps(tl, tr, bl, br):
    spec = pl.BlockSpec((3, QUAD, 256), lambda t: (0, 0, t))
    out = pl.BlockSpec((16, 16, 256), lambda t: (0, 0, t))
    return pl.pallas_call(
        join_kernel,
        grid=(INNER // 256,),
        in_specs=[spec] * 4,
        out_specs=[out] * 3,
        out_shape=[jax.ShapeDtypeStruct((16, 16, INNER), BF16)] * 3,
        compiler_params=params(),
        name="join_maps",
    )(tl, tr, bl, br)


def bias_kernel(table_ref, out_ref):
    lane = iota((BIAS_HEADS, 8, 256), 2)
    turn = jnp.where(iota((SIDE, 32), 0) + iota((SIDE, 32), 1) == 30, LOG2E, 0.0)
    spread = jnp.where(iota((SIDE, 256), 1) // 8 == iota((SIDE, 256), 0), 1.0, 0.0)
    exact = dict(precision=lax.Precision.HIGHEST, preferred_element_type=F32)
    turned = [jnp.dot(table_ref[head], turn, **exact) for head in range(BIAS_HEADS)]
    wide = jnp.stack(
        [lax.dot_general(rows, spread, (((0,), (0,)), ((), ())), **exact) for rows in turned]
    )
    for d in range(3):
        strip = jnp.zeros((BIAS_HEADS, 8, 256), F32)
        for xi in range(8):
            first = 23 - 8 * d - xi
            strip = jnp.where(lane % 8 == xi, wide[:, first : first + 8, :], strip)
        strip = strip.reshape(BIAS_HEADS * 8, 256)
        for yj in range(16):
            start = 8 * (15 - yj)
            moved = strip if start == 0 else pltpu.roll(strip, 256 - start, 1)
            out_ref[:, d, 8 * yj : 8 * yj + 8, :] = moved[:, :128].reshape(BIAS_HEADS, 8, 128)


def bias_blocks(bias_table):
    return pl.pallas_call(
        bias_kernel,
        grid=(HEADS // BIAS_HEADS,),
        in_specs=[pl.BlockSpec((BIAS_HEADS, SIDE, SIDE), lambda t: (t, 0, 0))],
        out_specs=pl.BlockSpec((BIAS_HEADS, 3, 128, 128), lambda t: (t, 0, 0, 0)),
        out_shape=jax.ShapeDtypeStruct((HEADS, 3, 128, 128), F32),
        compiler_params=params(),
        cost_estimate=cost(1e7, 8e6),
        name="bias_blocks",
    )(bias_table)


def iota(shape, dim):
    return lax.broadcasted_iota(jnp.int32, shape, dim)


def per_head_sum(value):
    high = value.astype(BF16)
    low = (value - high.astype(F32)).astype(BF16)
    shape = (2 * TILE, TILE)
    same = (iota(shape, 0) % TILE) // HEAD_DIM == iota(shape, 1) // HEAD_DIM
    ones = jnp.where(same, 1.0, 0.0).astype(BF16)
    both = jnp.concatenate([high, low], axis=1)
    return jnp.dot(both, ones, preferred_element_type=F32)


def normalize(rows):
    value = rows.astype(F32)
    length = jnp.sqrt(per_head_sum(value * value))
    inverse = 1.0 / jnp.maximum(length, 1.0)
    return value * inverse, length, inverse


def normalize_back(unit, length, inverse, grad):
    projection = per_head_sum(unit * grad)
    return jnp.where(length > 1.0, (grad - unit * projection) * inverse, grad)


def of_head(rows, head):
    keep = iota(rows.shape, 1) // HEAD_DIM == head
    return jnp.where(keep, rows, jnp.zeros_like(rows))


def rows_of(refs, which, tile):
    lanes = slice(TILE * tile, TILE * tile + TILE)
    return jnp.concatenate([ref[which, :, lanes] for ref in refs], axis=0)


def mul(left, right):
    return jnp.dot(left, right, preferred_element_type=F32)


def head_rows(head):
    return slice(HEAD_DIM * head, HEAD_DIM * head + HEAD_DIM)


def cosines_of(k_round, q_round):
    q_t = q_round.T
    return [mul(of_head(k_round, head), q_t) for head in range(PER_TILE)]


def forward_kernel(scale_ref, tl_ref, bl_ref, tr_ref, br_ref, bias_ref, attn_ref, probs_ref):
    step = pl.program_id(0)
    quads = (tl_ref, bl_ref, tr_ref, br_ref)
    cosines, values_t = [], []
    for tile in range(GROUP):
        q_round = normalize(rows_of(quads, 0, tile))[0].astype(BF16)
        k_round = normalize(rows_of(quads, 1, tile))[0].astype(BF16)
        values_t.append(rows_of(quads, 2, tile).T)
        cosines += cosines_of(k_round, q_round)
    rounded = []
    for head in range(GROUP * PER_TILE):
        scale = scale_ref[step * GROUP * PER_TILE + head]
        halves = []
        for half in range(2):
            lanes = slice(128 * half, 128 * half + 128)
            bias = jnp.concatenate([bias_ref[head, 1 + half], bias_ref[head, half]], axis=0)
            scores = cosines[head][:, lanes] * scale + bias
            weights = jnp.exp2(scores - jnp.max(scores, axis=0, keepdims=True))
            probs = weights * (1.0 / jnp.sum(weights, axis=0, keepdims=True))
            probs_ref[head, :, lanes] = probs
            halves.append(probs.astype(BF16))
        rounded.append(jnp.concatenate(halves, axis=1))
    for head in range(GROUP * PER_TILE):
        value_t = values_t[head // PER_TILE][head_rows(head % PER_TILE)]
        attn_ref[head_rows(head), :] = mul(value_t, rounded[head]).astype(BF16)


def quad_spec():
    return pl.BlockSpec((3, QUAD, GROUP * TILE), lambda t: (0, 0, t))


def probs_spec():
    return pl.BlockSpec((GROUP * PER_TILE, TOKENS, TOKENS), lambda t: (t, 0, 0))


def forward(scales, quads, bias):
    return pl.pallas_call(
        forward_kernel,
        grid=(INNER // TILE // GROUP,),
        in_specs=[pl.BlockSpec(memory_space=pltpu.SMEM)]
        + [quad_spec()] * 4
        + [pl.BlockSpec((GROUP * PER_TILE, 3, 128, 128), lambda t: (t, 0, 0, 0))],
        out_specs=[pl.BlockSpec((GROUP * TILE, TOKENS), lambda t: (t, 0)), probs_spec()],
        out_shape=[
            jax.ShapeDtypeStruct((INNER, TOKENS), BF16),
            jax.ShapeDtypeStruct((HEADS, TOKENS, TOKENS), F32),
        ],
        compiler_params=params(),
        cost_estimate=cost(8e9, 16e6),
        name="forward",
    )(scales, *quads, bias)


def diagonal_sums(blocks):
    lane = iota((8, 128), 1)
    strips = []
    for block in blocks:
        total = jnp.zeros((8, 128), F32)
        first = jnp.zeros((8, 128), F32)
        for yj in range(16):
            start = 8 * (15 - yj)
            piece = block[8 * yj : 8 * yj + 8]
            if start:
                piece = pltpu.roll(piece, start, 1)
                first = first + jnp.where(lane >= start, piece, 0.0)
            else:
                first = first + piece
            total = total + piece
        strips.append(jnp.concatenate([first, total - first], axis=1))
    return strips


def offset_sums(strips):
    shape = strips[0].shape
    xj, lane = iota(shape, 0) % 8, iota(shape, 1)
    even = ((lane + xj) // 8) % 2 == 0
    sums = []
    for strip in strips:
        for bit in range(3):
            moved = pltpu.roll(strip, 256 - (1 << bit), 1)
            strip = jnp.where((xj // (1 << bit)) % 2 == 1, moved, strip)
        part = jnp.where(even, strip, 0.0)
        total = lambda v: jnp.sum(v.reshape(PER_TILE, 8, 256), axis=1)
        sums.append((pltpu.roll(total(part), 7, 1), pltpu.roll(total(strip - part), 255, 1)))
    inner = iota((PER_TILE, 256), 1) % 16
    result = []
    for parity in range(2):
        left, middle, right = (pair[parity] for pair in sums)
        result.append(left + jnp.where(inner >= 8, pltpu.roll(middle, 8, 1), 0.0))
        result.append(right + jnp.where(inner < 8, pltpu.roll(middle, 248, 1), 0.0))
    return result


def table_of(strips, log_sums):
    rows = offset_sums(strips)
    spot = iota((PER_TILE, 256), 1) == 240
    rows[2] = jnp.where(spot, jnp.concatenate(log_sums, axis=0), rows[2])
    shape = (32, 256)
    k, lane = iota(shape, 0), iota(shape, 1)
    mine, odd = lane // 16 == k // 2, k % 2 == 1
    total = jnp.zeros((PER_TILE * 32, TILE), F32)
    for half in range(2):
        picked = []
        for head in range(PER_TILE):
            both = jnp.where(odd, rows[2 + half][head : head + 1], rows[half][head : head + 1])
            picked.append(jnp.where(mine, both, 0.0).astype(BF16))
        source, goal = iota((256, TILE), 0), iota((256, TILE), 1)
        place = jnp.where(goal == 16 * half + source % 16, 1.0, 0.0).astype(BF16)
        total = total + mul(jnp.concatenate(picked, axis=0), place)
    table = total[:32]
    for head in range(1, PER_TILE):
        table = table + pltpu.roll(total[32 * head : 32 * head + 32], 32 * head, 1)
    return table


def backward_kernel(
    first_step,
    scale_ref,
    tl_ref,
    bl_ref,
    tr_ref,
    br_ref,
    grad_ref,
    probs_ref,
    *refs,
):
    gtl_ref, gbl_ref, gtr_ref, gbr_ref, table_ref = refs[-5:]
    step = pl.program_id(0) + first_step
    quads = (tl_ref, bl_ref, tr_ref, br_ref)
    heads = range(GROUP * PER_TILE)
    queries, keys, grads, grad_probs, cosines = [], [], [], [], []
    for tile in range(GROUP):
        queries.append(normalize(rows_of(quads, 0, tile)))
        keys.append(normalize(rows_of(quads, 1, tile)))
        grads.append(grad_ref[:, TILE * tile : TILE * tile + TILE])
        value, grad_t = rows_of(quads, 2, tile), grads[-1].T
        grad_probs += [mul(of_head(value, head), grad_t) for head in range(PER_TILE)]
        cosines += cosines_of(keys[-1][0].astype(BF16), queries[-1][0].astype(BF16))
    prob_rounds, grad_coss, blocks, log_sums = [], [], [], []
    for head in heads:
        scale = scale_ref[step * GROUP * PER_TILE + head]
        log_sum = jnp.zeros((1, 128), F32)
        halves, rounded, cos_grads = [], [], []
        for half in range(2):
            lanes = slice(128 * half, 128 * half + 128)
            probs = probs_ref[head, :, lanes]
            part = grad_probs[head][:, lanes]
            inner = jnp.sum(probs * part, axis=0, keepdims=True)
            score_grad = probs * (part - inner)
            halves.append(score_grad)
            log_sum = log_sum + jnp.sum(
                score_grad * cosines[head][:, lanes], axis=0, keepdims=True
            )
            rounded.append(probs.astype(BF16))
            cos_grads.append((score_grad * scale).astype(BF16))
        blocks.append((halves[0][128:], halves[0][:128] + halves[1][128:], halves[1][:128]))
        prob_rounds.append(jnp.concatenate(rounded, axis=1))
        grad_coss.append(jnp.concatenate(cos_grads, axis=1))
        log_sums.append(scale * jnp.sum(log_sum, axis=1, keepdims=True))
    for tile in range(GROUP):
        grad_v = jnp.zeros((TOKENS, TILE), F32)
        grad_k = jnp.zeros((TOKENS, TILE), F32)
        grad_q = []
        q_round, key_t = queries[tile][0].astype(BF16), keys[tile][0].astype(BF16).T
        for head in range(PER_TILE):
            grad_cos = grad_coss[PER_TILE * tile + head]
            grad_q.append(mul(key_t[head_rows(head)], grad_cos))
            grad_v = grad_v + mul(prob_rounds[PER_TILE * tile + head], of_head(grads[tile], head))
            grad_k = grad_k + mul(grad_cos, of_head(q_round, head))
        results = (
            normalize_back(*queries[tile], jnp.concatenate(grad_q, axis=0).T).astype(BF16),
            normalize_back(*keys[tile], grad_k).astype(BF16),
            grad_v.astype(BF16),
        )
        lanes = slice(TILE * tile, TILE * tile + TILE)
        for part, ref in enumerate((gtl_ref, gbl_ref, gtr_ref, gbr_ref)):
            for which, result in enumerate(results):
                ref[which, :, lanes] = result[QUAD * part : QUAD * part + QUAD]
    for tile in range(GROUP):
        mine = range(PER_TILE * tile, PER_TILE * tile + PER_TILE)
        found = [diagonal_sums(blocks[head]) for head in mine]
        strips = [jnp.concatenate([strip[d] for strip in found], axis=0) for d in range(3)]
        table_ref[tile] = table_of(strips, [log_sums[head] for head in mine]).astype(BF16)


def backward(scales, quads, grad_attn, probs, first, steps, earlier=()):
    quad = pl.BlockSpec((3, QUAD, GROUP * TILE), lambda t: (0, 0, t + first))
    return pl.pallas_call(
        functools.partial(backward_kernel, first),
        grid=(steps,),
        in_specs=[pl.BlockSpec(memory_space=pltpu.SMEM)]
        + [quad] * 4
        + [
            pl.BlockSpec((TOKENS, GROUP * TILE), lambda t: (0, t + first)),
            pl.BlockSpec((GROUP * PER_TILE, TOKENS, TOKENS), lambda t: (t + first, 0, 0)),
        ]
        + [pl.BlockSpec(memory_space=pl.ANY)] * len(earlier),
        out_specs=[quad] * 4 + [pl.BlockSpec((GROUP, 32, TILE), lambda t: (t + first, 0, 0))],
        out_shape=[jax.ShapeDtypeStruct((3, QUAD, INNER), BF16)] * 4
        + [jax.ShapeDtypeStruct((INNER // TILE, 32, TILE), BF16)],
        input_output_aliases={7 + i: i for i in range(len(earlier))},
        compiler_params=params(),
        cost_estimate=cost(8e9, 10e6),
        name="backward",
    )(scales, *quads, grad_attn, probs, *earlier)


def outer_kernel(place_ref, own_ref, other_ref, drop_ref, drop_other_ref, *refs):
    outs, left_ref = refs[:NX], refs[NX]
    goal, source = iota((64, TILE), 0), iota((64, TILE), 1)
    wanted = ((goal // 4) % NZ) * 16 + (goal // 32) * 8 + place_ref[3] * 4 + goal % 4
    pick = jnp.where(source == wanted, 1.0, 0.0).astype(BF16)
    for tile in range(INNER // TILE):
        rows, goals = slice(TILE * tile, TILE * tile + TILE), slice(64 * tile, 64 * tile + 64)
        left_ref[goals, :TOKENS] = mul(pick, own_ref[rows, :]).astype(BF16)
        left_ref[goals, TOKENS:] = mul(pick, other_ref[rows, :]).astype(BF16)
    for step, out in enumerate(outs):
        start = pl.multiple_of(((place_ref[0] + step) % NX) * 128, 128)
        left = left_ref[pl.ds(start, 128), :]
        for col in range(0, D, 512):
            part = mul(left[:, :TOKENS], drop_ref[:, col : col + 512])
            part = part + mul(left[:, TOKENS:], drop_other_ref[:, col : col + 512])
            out[:, col : col + 512] = part.astype(out.dtype)


def outer_terms(place, own, other, dropped, dropped_other):
    whole = pl.BlockSpec(memory_space=pltpu.VMEM)
    return pl.pallas_call(
        outer_kernel,
        in_specs=[pl.BlockSpec(memory_space=pltpu.SMEM)] + [whole] * 4,
        out_specs=[whole] * NX,
        out_shape=[jax.ShapeDtypeStruct((128, D), F32 if s == 0 else BF16) for s in range(NX)],
        scratch_shapes=[pltpu.VMEM((512, 2 * TOKENS), BF16)],
        compiler_params=params(),
        cost_estimate=cost(1.1e9, 6e6),
        name="outer_terms",
    )(place, own, other, dropped, dropped_other)


def sum_y_kernel(place_ref, *refs):
    terms, outs = refs[:4], refs[4:8]
    for step, out in enumerate(outs):
        y = (place_ref[1] + step) % 4
        start = pl.multiple_of(((y % 2) * 2 + y // 2) * 32, 32)
        rows = pl.ds(start, 32)
        total = terms[0][rows, :]
        for term in terms[1:]:
            total = total + term[rows, :].astype(F32)
        out[...] = total.astype(out.dtype)


def sum_for_y(place, terms):
    whole = pl.BlockSpec(memory_space=pltpu.VMEM)
    return pl.pallas_call(
        sum_y_kernel,
        in_specs=[pl.BlockSpec(memory_space=pltpu.SMEM)] + [whole] * 4,
        out_specs=[whole] * 4,
        out_shape=[jax.ShapeDtypeStruct((32, D), F32 if s == 0 else BF16) for s in range(4)],
        compiler_params=params(),
        name="sum_for_y",
    )(place, *terms)


def sum_z_kernel(*refs):
    terms, piece, out = refs[:4], refs[4], refs[5]
    total = terms[0][...]
    for term in terms[1:]:
        total = total + term[...].astype(F32)
    for z in range(NZ):
        out[z, :, :D] = total[4 * z : 4 * z + 4].astype(BF16)
        for part in range(8):
            lanes = slice(D + TILE * part, D + TILE * part + TILE)
            out[z, :, lanes] = piece[4 * part : 4 * part + 4].astype(BF16)


def sum_for_z(terms, piece):
    whole = pl.BlockSpec(memory_space=pltpu.VMEM)
    return pl.pallas_call(
        sum_z_kernel,
        in_specs=[whole] * 5,
        out_specs=whole,
        out_shape=jax.ShapeDtypeStruct((NZ, 4, D + 8 * TILE), BF16),
        compiler_params=params(),
        name="sum_for_z",
    )(*terms, piece)


def place_scalars():
    x, y, z, core = coordinates()
    return jnp.stack([x, y, z, core]).astype(jnp.int32)


def along_z_exchange(value):
    rest = NYH * NCORE
    groups = [[rest * z + one for z in range(NZ)] for one in range(rest)]
    return lax.all_to_all(value, "col", 0, 0, axis_index_groups=groups, tiled=True)


def table_pieces(part):
    return jnp.sum(along_z_exchange(part).astype(F32), axis=0)


def table_plane(piece):
    cols, rest = NZ * NYH * NCORE, NYH * NCORE
    groups = [
        [cols * row + rest * z + one for row in range(NX * NYL) for one in range(rest)]
        for z in range(NZ)
    ]
    same = jnp.broadcast_to(piece.astype(BF16), (len(groups[0]), 32, TILE))
    found = lax.all_to_all(
        same, ("row", "col"), 0, 0, axis_index_groups=groups, tiled=True
    )
    return jnp.sum(found.astype(F32), axis=0) / WINDOWS


def totals_kernel(found_ref, weight_ref, table_ref):
    total = found_ref[0, :, :D].astype(F32)
    for z in range(1, NZ):
        total = total + found_ref[z, :, :D].astype(F32)
    weight_ref[...] = total * (1.0 / WINDOWS)
    for tile in range(INNER // TILE):
        parts = [found_ref[tile, :, D + TILE * p : D + TILE * p + TILE] for p in range(8)]
        rows = jnp.concatenate([part.astype(F32) for part in parts], axis=0)
        for head in range(PER_TILE):
            place = rows[:, 32 * head : 32 * head + 32]
            table_ref[PER_TILE * tile + head] = place[:SIDE, :SIDE]


def totals(terms, piece):
    terms = [terms[0]] + [move(terms[s], along_y(s)) for s in range(1, 4)]
    found = along_z_exchange(sum_for_z(terms, piece))
    whole = pl.BlockSpec(memory_space=pltpu.VMEM)
    weight, table = pl.pallas_call(
        totals_kernel,
        in_specs=[whole],
        out_specs=[whole] * 2,
        out_shape=[
            jax.ShapeDtypeStruct((4, D), F32),
            jax.ShapeDtypeStruct((HEADS, SIDE, SIDE), F32),
        ],
        compiler_params=params(),
        name="totals",
    )(found)
    log_sum = found[:, 3, D + 7 * TILE :: 32].astype(F32)
    return weight, table, log_sum.reshape(HEADS)


def per_device(
    query_map, key_map, value_map, out_grad, keep_mask, log_scale, bias_table, proj_weight
):
    logit_scale = jnp.exp(log_scale)
    tl, tr, bl, br = split_maps(query_map, key_map, value_map)
    quads = (br, move_map(tr, -1, 0), move_map(bl, 0, -1), move_map(tl, -1, -1))
    bias = bias_blocks(bias_table)
    tl, tr, bl, br = split_dropped(out_grad, keep_mask)
    quads, tl, tr, bl = lax.optimization_barrier((quads, tl, tr, bl))
    up, left = move_map(tr, -1, 0), move_map(bl, 0, -1)
    attn_t, probs = forward(logit_scale * LOG2E, quads, bias)
    pieces = (br, up, left, move_map(tl, -1, -1))
    attn_t, pieces = lax.optimization_barrier((attn_t, pieces))
    dropped = jnp.concatenate(pieces, axis=0)
    other, dropped_other = move(attn_t, other_core), move(dropped, other_core)
    grad_attn = lax.dot_general(
        dropped, proj_weight, (((1,), (1,)), ((), ())), preferred_element_type=F32
    ).astype(BF16)
    found = backward(logit_scale, quads, grad_attn, probs, 0, EARLY)
    found, other, dropped_other = lax.optimization_barrier((found, other, dropped_other))
    place = place_scalars()
    terms = outer_terms(place, attn_t, other, dropped, dropped_other)
    terms, found = lax.optimization_barrier((terms, found))
    g_tl, g_bl, g_tr, g_br, table_part = backward(
        logit_scale, quads, grad_attn, probs, EARLY, INNER // TILE // GROUP - EARLY, found
    )
    down, right = move_map(g_bl, 1, 0), move_map(g_tr, 0, 1)
    sent = [move(terms[s], along_x(s)) for s in range(1, NX)]
    sent[0], sent[2], g_br, table_part = lax.optimization_barrier(
        (sent[0], sent[2], g_br, table_part)
    )
    arrived = (move_map(g_br, 1, 1), down, right)
    piece = table_pieces(table_part)
    sent, arrived = lax.optimization_barrier((sent, arrived))
    terms = sum_for_y(place, (terms[0], *sent))
    terms, piece = lax.optimization_barrier((terms, piece))
    piece = table_plane(piece)
    grads = join_maps(*arrived, g_tl)
    weight_grad, table_grad, log_grad = totals(terms, piece)
    return (*grads, weight_grad, table_grad, log_grad)


def solution(mesh):
    return jax.shard_map(
        per_device,
        mesh=mesh,
        in_specs=(
            P("row", "col", None),
            P("row", "col", None),
            P("row", "col", None),
            P("row", "col", None),
            P("row", "col", None),
            P(),
            P(),
            P(),
        ),
        out_specs=(
            P("row", "col", None),
            P("row", "col", None),
            P("row", "col", None),
            P(("row", "col"), None),
            P(),
            P(),
        ),
        check_vma=False,
    )
```
